32 devices in a mesh: node: 4 (over y, x), grid: 8 (over z, core).
Axes of the slice: x: 2, y: 2, z: 4, core: 2. Of those that a mesh axis runs over, the one named last changes fastest.
Arguments:
- probes: float32 [1, 48, 192, 256], P(None, 'grid'), may hold values from -6 to 6
- potential: float32 [48, 192, 256], P('grid'), may hold values from -2 to 1
- warm_start: bfloat16 [4, 1, 2, 48, 192, 256], P('node', None, None, 'grid'), may hold values from -0.29882812 to 0.29882812
- shift_points: float32 [4, 2], P('node'), may hold values from -4 to 9, as said below
- quad_weights: float32 [4, 2], P('node'), may hold values from -0.3 to 0.3
Outputs:
- moments: float32 [2, 1, 2, 48, 192, 256], P(None, None, None, 'grid', 'node')
- trace_estimate: float32 [2], replicated
The draws below stay inside these ranges and needn't reach their ends.
Inputs may be any that keep to these rules, and one draw needn't show every extreme that they name: `shift_points`: column 0 holds real parts in -1 to 9; column 1 holds imaginary parts whose magnitude lies in 1 to 4.
All inputs are finite; a program needn't handle non-finite values.
Results may differ from the reference program's by a relative error of at most 0.0003.
Values may be sent and summed in bfloat16 or wider, within the bound.
A program may use at most 192 MiB of HBM per device.

```python
import math
import jax
import jax.numpy as jnp
from jax import lax

NX = 192
NY = 256
PROBES = 1
ITERS = 2
MOMENTS = 2
NZ = 48
SHIFTS = 4


def draw_shift_points(key, part):
    key_real, key_size, key_sign = jax.random.split(key, 3)
    real_part = jax.random.uniform(key_real, (SHIFTS,), jnp.float32, -1.0, 9.0)
    magnitude = jnp.exp(jax.random.uniform(key_size, (SHIFTS,), jnp.float32, 0.0, math.log(4.0)))
    signs = jnp.where(jax.random.bernoulli(key_sign, 0.5, (SHIFTS,)), 1.0, -1.0).astype(jnp.float32)
    return jnp.stack([real_part, signs * magnitude], axis=1)


def levels(stream_key, dims, pieces, low, largest):
    level, own = 1.0, jax.random.fold_in(stream_key, 6)
    for axis_at, blocks in pieces:
        heights = jnp.exp(jax.random.uniform(jax.random.fold_in(own, axis_at), (blocks,), jnp.float32, low / len(pieces), largest / len(pieces)))
        level = level * jnp.repeat(heights, dims[axis_at] // blocks).reshape([-1 if axis == axis_at else 1 for axis in range(len(dims))])
    return level


def bell_draw(key, shape, deviation, most, pieces=(), held_as=jnp.bfloat16):
    result = deviation * jax.random.normal(key, shape, jnp.float32)
    if pieces:
        result = result * levels(key, shape, pieces, -0.22, 0.18)
    return jnp.clip(result, -most, most).astype(held_as)


def setup_inputs(seed: int = 0) -> dict:
    key_of = jax.random.split(jax.random.key(seed), 6)
    return {
        "probes": bell_draw(key_of[0], (PROBES, NZ, NX, NY), 1.0, 6.0, ((1, 8),), jnp.float32),
        "potential": jnp.clip(-2.0 + 3.0 * jax.random.uniform(key_of[1], (NZ, NX, NY), jnp.float32) ** levels(key_of[1], (NZ, NX, NY), ((0, 8),), -0.2, 0.2), -2.0, 1.0),
        "warm_start": bell_draw(key_of[2], (SHIFTS, PROBES, 2, NZ, NX, NY), 0.05, 0.29882812, ((0, 4), (3, 8))),
        "shift_points": draw_shift_points(jax.random.fold_in(key_of[5], 71), 0),
        "quad_weights": jnp.clip(jax.random.uniform(key_of[4], (SHIFTS, 2), jnp.float32, -0.3, 0.3) * levels(key_of[4], (SHIFTS, 2), ((0, 4),), -0.4, 0.0), -0.3, 0.3),
    }


near_weight = 4.0 / 3.0
far_weight = -1.0 / 12.0
self_weight = -7.5


def hamiltonian_apply(padded, potential, shift_real, shift_imag):
    middle = padded[:, :, :, 2:-2]
    near_sum = (padded[:, :, :, 1:-3] + padded[:, :, :, 3:-1]) + (jnp.roll(middle, 1, 4) + jnp.roll(middle, -1, 4)) + (jnp.roll(middle, 1, 5) + jnp.roll(middle, -1, 5))
    far_sum = (padded[:, :, :, :-4] + padded[:, :, :, 4:]) + (jnp.roll(middle, 2, 4) + jnp.roll(middle, -2, 4)) + (jnp.roll(middle, 2, 5) + jnp.roll(middle, -2, 5))
    laplacian = near_weight * near_sum + far_weight * far_sum + self_weight * middle
    real_shift = shift_real[:, None, None, None, None]
    imag_shift = shift_imag[:, None, None, None, None]
    real_part = middle[:, :, 0]
    imag_part = middle[:, :, 1]
    result_real = real_shift * real_part - imag_shift * imag_part + 0.5 * laplacian[:, :, 0] - potential * real_part
    result_imag = real_shift * imag_part + imag_shift * real_part + 0.5 * laplacian[:, :, 1] - potential * imag_part
    return jnp.stack([result_real, result_imag], axis=2)


def wrap_pad(vector):
    return jnp.concatenate([vector[:, :, :, -2:], vector, vector[:, :, :, :2]], axis=3)


def bilinear(first_vec, second_vec):
    real_sum = jnp.sum(first_vec[:, :, 0] * second_vec[:, :, 0] - first_vec[:, :, 1] * second_vec[:, :, 1], axis=(2, 3, 4))
    imag_sum = jnp.sum(first_vec[:, :, 0] * second_vec[:, :, 1] + first_vec[:, :, 1] * second_vec[:, :, 0], axis=(2, 3, 4))
    return jnp.stack([real_sum, imag_sum], axis=-1)


def complex_times(factor_one, factor_two):
    return jnp.stack([factor_one[..., 0] * factor_two[..., 0] - factor_one[..., 1] * factor_two[..., 1], factor_one[..., 0] * factor_two[..., 1] + factor_one[..., 1] * factor_two[..., 0]], axis=-1)


def complex_divide(factor_one, factor_two):
    magnitude = factor_two[..., 0] * factor_two[..., 0] + factor_two[..., 1] * factor_two[..., 1]
    return jnp.stack([(factor_one[..., 0] * factor_two[..., 0] + factor_one[..., 1] * factor_two[..., 1]) / magnitude, (factor_one[..., 1] * factor_two[..., 0] - factor_one[..., 0] * factor_two[..., 1]) / magnitude], axis=-1)


def scale_field(scalars, vector):
    real_scalar = scalars[..., 0][:, :, None, None, None]
    imag_scalar = scalars[..., 1][:, :, None, None, None]
    return jnp.stack([real_scalar * vector[:, :, 0] - imag_scalar * vector[:, :, 1], real_scalar * vector[:, :, 1] + imag_scalar * vector[:, :, 0]], axis=2)


def cocg_shift(start_guess, source, potential, shift_real, shift_imag):
    solution = start_guess
    residual = source - hamiltonian_apply(wrap_pad(start_guess), potential, shift_real, shift_imag)
    direction = residual
    norm_now = bilinear(residual, residual)
    for iteration in range(ITERS):
        applied = hamiltonian_apply(wrap_pad(direction), potential, shift_real, shift_imag)
        step_length = complex_divide(norm_now, bilinear(direction, applied))
        solution = solution + scale_field(step_length, direction)
        residual = residual - scale_field(step_length, applied)
        if iteration + 1 < ITERS:
            norm_next = bilinear(residual, residual)
            direction = residual + scale_field(complex_divide(norm_next, norm_now), direction)
            norm_now = norm_next
    return solution


def reference(probes, potential, warm_start, shift_points, quad_weights):
    source = jnp.stack([probes, jnp.zeros_like(probes)], axis=1)[None]

    def shift_step(running, inputs):
        moments, trace_value = running
        start_guess, shift_point, weight = inputs
        solution = cocg_shift(start_guess.astype(jnp.float32)[None], source, potential, shift_point[0:1], shift_point[1:2])[0]
        scaled_shift = jnp.stack([(shift_point[0] - 4.0) / 5.0, shift_point[1] / 5.0])
        weight_power = weight
        moment_terms = []
        for degree in range(MOMENTS):
            moment_terms.append(jnp.stack([weight_power[0] * solution[:, 0] - weight_power[1] * solution[:, 1], weight_power[0] * solution[:, 1] + weight_power[1] * solution[:, 0]], axis=1))
            weight_power = complex_times(weight_power, scaled_shift)
        moments = moments + jnp.stack(moment_terms)
        inner_sum = jnp.stack([jnp.sum(probes * solution[:, 0]), jnp.sum(probes * solution[:, 1])]) / PROBES
        trace_value = trace_value + complex_times(weight, inner_sum)
        return (moments, trace_value), None

    initial = (jnp.zeros((MOMENTS, PROBES, 2, NZ, NX, NY), jnp.float32), jnp.zeros((2,), jnp.float32))
    (moments, trace_value), unused_out = lax.scan(shift_step, initial, (warm_start, shift_points, quad_weights))
    return moments, trace_value
```

```python
import functools

import jax
import jax.numpy as jnp
import ml_dtypes
import numpy as np
from jax import lax
from jax.experimental import pallas as pl
from jax.experimental.pallas import tpu as pltpu
from jax.sharding import PartitionSpec as P

MESH = pl.DeviceIdType.MESH
SUMS = 16
NEAR, FAR = 16.0, -1.0


def up_to(size, step):
    return -(-size // step) * step


def weight_of(distance):
    return {1: NEAR, 2: FAR}.get(abs(distance), 0.0)


def ring_matrix(size, diagonal):
    matrix = np.zeros((size, size), np.float32)
    at = np.arange(size)
    for step, weight in ((1, NEAR), (2, FAR)):
        matrix[at, (at + step) % size] += weight
        matrix[at, (at - step) % size] += weight
    matrix[at, at] += diagonal
    return matrix.astype(ml_dtypes.bfloat16)


def table(block):
    tall = up_to(block, 16)
    sizes = {
        "own": (tall, tall),
        "halo0": (tall, 16),
        "halo1": (tall, 16),
        "split0": (tall, 2 * block + 16),
        "split1": (tall, 2 * block + 16),
        "ahead": (tall, 2 * block),
        "edge_own": (16, 2 * tall),
        "edge_halo": (16, 48),
        "cross": (16, 16),
    }
    at, places = 0, {}
    for name, (rows, cols) in sizes.items():
        places[name] = (at, rows, cols)
        at += rows
    return places, at, up_to(max(cols for rows, cols in sizes.values()), 128)


def small_matrices(block, depth):
    tall = up_to(block, 16)
    places, rows, cols = table(block)
    whole = np.zeros((rows, cols), np.float32)
    view = {name: whole[at : at + n, :m] for name, (at, n, m) in places.items()}
    wide = [-4, -3, -2, -1, block, block + 1, block + 2, block + 3]
    slim = [-2, -1, block, block + 1]
    for i in range(block):
        for j in range(block):
            w = weight_of(i - j)
            view["own"][i, j] = w
            for s in range(2):
                view[f"split{s}"][i, j] = w
                view[f"split{s}"][i, block + j] = w
            if j > i:
                view["ahead"][i, j] = 2 * w
                view["ahead"][i, block + j] = 2 * w
        for s in range(2):
            for c, x in enumerate(wide):
                view[f"halo{s}"][i, 8 * s + c] = weight_of(i - x)
            for c, x in enumerate(slim):
                view[f"split{s}"][i, 2 * block + 4 * s + c] = weight_of(i - x)
                view[f"split{s}"][i, 2 * block + 8 + 4 * s + c] = weight_of(i - x)
    for s in range(2):
        for t, x in enumerate(slim):
            row, here = 4 * s + t, wide.index(x)
            for j in range(block):
                view["edge_own"][row, tall * s + j] = weight_of(x - j)
            for c, other in enumerate(wide):
                view["edge_halo"][row, 16 + 8 * s + c] += weight_of(x - other)
            for q in range(6):
                view["edge_halo"][row, 8 * q + here] += weight_of(q - 2 - s)
            view["edge_halo"][8 + row, 16 + 8 * s + here] = 1.0
    for p in range(depth):
        for e in range(2):
            for f in range(2):
                view["cross"][2 * p + e, 2 * p + f] = 2 * weight_of(2 - e + f)
    return whole.astype(ml_dtypes.bfloat16)


def halo_picks(width, nodes):
    block = width // nodes
    picks = np.zeros((nodes * 16, 2 * width), np.float32)
    for m in range(nodes):
        for s in range(2):
            for c, x in enumerate([-4, -3, -2, -1, block, block + 1, block + 2, block + 3]):
                picks[16 * m + 8 * s + c, width * s + (block * m + x) % width] = 1.0
    return picks.astype(ml_dtypes.bfloat16)


def core_picks(width, nodes):
    block = width // nodes
    tall = up_to(block, 16)
    picks = np.zeros((nodes * tall, width), np.float32)
    for m in range(nodes):
        for i in range(block):
            picks[tall * m + i, block * m + i] = 1.0
    return picks.astype(ml_dtypes.bfloat16)


def cmul(a, b):
    return a[0] * b[0] - a[1] * b[1], a[0] * b[1] + a[1] * b[0]


def cdiv(a, b):
    size = b[0] * b[0] + b[1] * b[1]
    return (a[0] * b[0] + a[1] * b[1]) / size, (a[1] * b[0] - a[0] * b[1]) / size


def fold(values):
    rows, cols = values.shape
    return jnp.sum(values.reshape(rows // 8, 8, cols), axis=0)


def dot(a, b):
    return jnp.dot(a, b, preferred_element_type=jnp.float32)


def kernel(
    nodes,
    slabs,
    warm,
    probes,
    potential,
    shift_hbm,
    weight_hbm,
    along_y_hbm,
    small_hbm,
    picks_hbm,
    core_hbm,
    moments,
    trace,
    own,
    hsend,
    csend,
    wbuf,
    halo,
    bbuf,
    vbuf,
    bside,
    vside,
    bedge,
    vedge,
    rbuf,
    redge,
    qbuf,
    qfirst,
    qlast,
    qhead,
    qahead,
    edge_out,
    edge_in,
    acc,
    sums,
    totals,
    notes,
    shift_ref,
    weight_ref,
    along_y,
    small,
    picks,
    cpicks,
    local_sem,
    b_send,
    b_recv,
    a_send,
    a_recv,
    z_send,
    z_recv,
    q_send,
    q_recv,
    x_send,
    x_recv,
    s_send,
    s_recv,
    t_send,
    t_recv,
):
    f32, bf16 = jnp.float32, jnp.bfloat16
    node, slab = lax.axis_index("node"), lax.axis_index("grid")
    depth, width, length = own.shape[1:]
    pairs = depth // 2
    block = width // nodes
    tall = up_to(block, 16)
    narrow = block % 16 == 0
    lower = nodes // 2
    places = table(block)[0]
    above = (node, lax.rem(slab + 1, slabs))
    below = (node, lax.rem(slab + slabs - 1, slabs))
    step = 16 if narrow else 8
    mine = pl.ds(pl.multiple_of(node * block, step), block)
    left = pl.ds(pl.multiple_of(lax.rem(node * block + width - 8, width), 8), 8)
    right = pl.ds(pl.multiple_of(lax.rem(node * block + block, width), 8), 8)

    def matrix(name):
        at, rows, cols = places[name]
        return small[at : at + rows, 0:cols]

    loads = []

    def load(source, target):
        copy = pltpu.make_async_copy(source, target, local_sem.at[len(loads)])
        copy.start()
        loads.append(copy)

    load(shift_hbm, shift_ref)
    load(weight_hbm, weight_ref)
    load(warm.at[0, 0], own)
    load(picks_hbm, picks)
    if not narrow:
        load(core_hbm, cpicks)
    first_loads = len(loads)
    load(along_y_hbm, along_y)
    load(small_hbm, small)
    load(probes.at[0, :, mine], bbuf.at[2 : depth + 2])
    load(potential.at[:, mine], vbuf.at[2 : depth + 2])
    load(probes.at[0, :, left], bside.at[0])
    load(probes.at[0, :, right], bside.at[1])
    load(potential.at[:, left], vside.at[0])
    load(potential.at[:, right], vside.at[1])
    if narrow:
        load(warm.at[0, 0, :, :, mine], wbuf.at[0, :, 4 : depth + 4])

    barrier = pltpu.get_barrier_semaphore()
    for k in range(1, slabs):
        pl.semaphore_signal(
            barrier, inc=1, device_id=(node, lax.rem(slab + k, slabs)), device_id_type=MESH
        )
    for k in range(1, nodes):
        pl.semaphore_signal(
            barrier, inc=1, device_id=(lax.rem(node + k, nodes), slab), device_id_type=MESH
        )
    pl.semaphore_wait(barrier, slabs + nodes - 2)

    def remote(source, target, send_sem, recv_sem, device):
        return pltpu.make_async_remote_copy(
            src_ref=source,
            dst_ref=target,
            send_sem=send_sem,
            recv_sem=recv_sem,
            device_id=device,
            device_id_type=MESH,
        )

    def peer(k):
        return lax.rem(node + k, nodes)

    def core(m, first, last):
        if narrow:
            rows = pl.ds(pl.multiple_of(m * block, step), block)
            return warm.at[0, 0, :, first:last, rows]
        return csend.at[m, :, first:last]

    chunks = ((0, 2), (depth - 2, depth), (2, depth - 2))

    def gather_copy(k, c):
        first, last = chunks[c]
        return remote(
            core(peer(k), first, last),
            wbuf.at[k, :, 4 + first : 4 + last],
            a_send.at[k, c],
            a_recv.at[k, c],
            (peer(k), slab),
        )

    def halo_copy(k):
        return remote(
            hsend.at[peer(k)],
            halo.at[k, :, 1 : pairs + 1],
            a_send.at[k, 3],
            a_recv.at[k, 3],
            (peer(k), slab),
        )

    def note_copy(k):
        return remote(notes.at[0], notes.at[k], a_send.at[k, 4], a_recv.at[k, 4], (peer(k), slab))

    top = depth + 4
    routes = (
        ((4, 6), (top, top + 2), below),
        ((top - 2, top), (2, 4), above),
        ((6, 8), (top + 2, top + 4), below),
        ((top - 4, top - 2), (0, 2), above),
    )

    def forward(k, c):
        source, target, device = routes[c]
        if isinstance(k, int) and k == 0:
            part = core(node, source[0] - 4, source[1] - 4)
        else:
            part = wbuf.at[k, :, source[0] : source[1]]
        return remote(
            part, wbuf.at[k, :, target[0] : target[1]], z_send.at[k, c], z_recv.at[k, c], device
        )

    def forward_halo(k, c):
        source, target, device = ((1, pairs + 1, below), (pairs, 0, above))[c]
        return remote(
            halo.at[k, :, source],
            halo.at[k, :, target],
            z_send.at[k, 4 + c],
            z_recv.at[k, 4 + c],
            device,
        )

    sides = []
    for at, (source, target) in enumerate(((probes.at[0], bbuf), (potential, vbuf))):
        for c, (first, there, device) in enumerate(
            ((0, depth + 2, below), (depth - 2, 0, above))
        ):
            sides.append(
                remote(
                    source.at[first : first + 2, mine],
                    target.at[there : there + 2],
                    b_send.at[2 * at + c],
                    b_recv.at[2 * at + c],
                    device,
                )
            )

    def pick():
        for copy in loads[2:first_loads]:
            copy.wait()
        for i in range(pairs):
            for part in range(2):
                rows = own[part, 2 * i : 2 * i + 2].reshape(2 * width, length)
                picked = dot(picks[...], rows).astype(bf16)
                for m in range(nodes):
                    hsend[m, part, i] = picked[16 * m : 16 * m + 16]
        if not narrow:
            for part in range(2):
                for p in range(depth):
                    picked = dot(cpicks[...], own[part, p]).astype(bf16)
                    for m in range(nodes):
                        csend[m, part, p] = picked[tall * m : tall * m + tall]

    def send_cores():
        for c in range(3):
            for k in range(1, nodes):
                gather_copy(k, c).start()
        for c in range(4):
            forward(0, c).start()
            if c == 1:
                for copy in sides:
                    copy.start()

    if narrow:
        send_cores()
    for copy in loads[0:2]:
        copy.wait()
    row = lax.broadcasted_iota(jnp.int32, (8, length), 0)
    note = jnp.zeros((8, length), f32)
    entries = (shift_ref[0, 0], shift_ref[0, 1], weight_ref[0, 0], weight_ref[0, 1])
    for i, entry in enumerate(entries):
        note = jnp.where(row == i, entry, note)
    notes[0] = note
    for k in range(1, nodes):
        note_copy(k).start()
    pick()
    if not narrow:
        send_cores()
    for k in range(1, nodes):
        halo_copy(k).start()
    for part in range(2):
        for i in range(pairs):
            halo[0, part, 1 + i] = hsend[node, part, i]
    for c in range(2):
        forward_halo(0, c).start()
    if not narrow:
        for part in range(2):
            for p in range(depth):
                wbuf[0, part, 4 + p] = csend[node, part, p]

    acc[...] = jnp.zeros_like(acc)
    qfirst[...] = jnp.zeros_like(qfirst)
    qlast[...] = jnp.zeros_like(qlast)
    qbuf[lower:nodes, :, depth : depth + 2] = jnp.zeros((nodes - lower, 2, 2, block, length), f32)
    for copy in loads[first_loads:]:
        copy.wait()
    for i in range(pairs):
        for s in range(2):
            for side in range(2):
                there = 4 * s + 2 * side
                here = 6 if side == 0 else 0
                bedge[i, there : there + 2] = bside[side, 2 * i + s, here : here + 2]
                vedge[i, there : there + 2] = vside[side, 2 * i + s, here : here + 2]

    def shift_of(k):
        return notes[k, 0:1, :], notes[k, 1:2, :]

    def apply(shift, field, stencil, local):
        diagonal = shift[0] - local
        return (
            diagonal * field[0] - shift[1] * field[1] + stencil[0] * (1.0 / 24.0),
            diagonal * field[1] + shift[1] * field[0] + stencil[1] * (1.0 / 24.0),
        )

    def added(k, first, count, low, high, terms):
        def body(i, carry):
            for s in range(2):
                carry = tuple(c + fold(v) for c, v in zip(carry, terms(i, s)))
            return carry

        zero = jnp.zeros((8, length), f32)
        for i, total in enumerate(lax.fori_loop(low, high, body, (zero,) * count)):
            acc[k * SUMS + first + i] += total

    def wide(values):
        return values.astype(f32)[0:block]

    def residual(k, i, s):
        pp = 2 * i + s
        stencil, field = [], []
        for part in range(2):
            centre = wbuf[k, part, pp + 2]
            plane = (
                dot(centre, along_y[...])
                + dot(matrix("own"), centre)
                + dot(matrix(f"halo{s}"), halo[k, part, i])
            )[0:block]
            at = [wide(wbuf[k, part, pp + j]) for j in (0, 1, 3, 4)]
            stencil.append(plane + 16.0 * (at[1] + at[2]) - (at[0] + at[3]))
            field.append(wide(centre))
        source = bbuf[pp]
        image = apply(shift_of(k), field, stencil, vbuf[pp])
        r = source - image[0], -image[1]
        rbuf[k, 0, pp] = r[0]
        rbuf[k, 1, pp] = r[1]
        return source, field, r

    def residual_terms(k, i, s):
        source, field, r = residual(k, i, s)
        return (
            r[0] * r[0] - r[1] * r[1],
            2.0 * r[0] * r[1],
            source * field[0],
            source * field[1],
            source * r[0],
            source * r[1],
        )

    def edge_pair(k, i):
        stencil, field = [], []
        for part in range(2):
            middle = wbuf[k, part, pl.ds(4 + 2 * i, 2)].reshape(2 * tall, length)
            around = halo[k, part, pl.ds(i, 3)].reshape(48, length)
            both = dot(matrix("edge_halo"), around)
            plane = dot(both.astype(bf16), along_y[...])
            beside = dot(matrix("edge_own"), middle)
            stencil.append(beside[0:8] + both[0:8] + plane[8:16])
            field.append(both[8:16])
        image = apply(shift_of(k), field, stencil, vedge[i])
        redge[k, 0, i] = bedge[i] - image[0]
        redge[k, 1, i] = -image[1]

    def split(values):
        high = values.astype(bf16)
        return high, (values - high.astype(f32)).astype(bf16)

    def pack(values):
        high, low = split(values)
        if narrow:
            return jnp.concatenate([high, low], axis=0)
        return jnp.concatenate([high.astype(f32), low.astype(f32)], axis=0).astype(bf16)

    def slim(values):
        high, low = split(values)
        return jnp.concatenate([high.astype(f32), low.astype(f32)], axis=0).astype(bf16)

    def along(packed):
        both = dot(packed, along_y[...])
        return both[0:block] + both[block : 2 * block]

    def image_terms(k, i, s):
        p = 2 * i + s
        stencil, field = [], []
        for part in range(2):
            at = [rbuf[k, part, p + j] for j in range(5)]
            packed = pack(at[2])
            side = jnp.concatenate([packed, slim(redge[k, part, i])], axis=0)
            plane = along(packed) + dot(matrix(f"split{s}"), side)[0:block]
            stencil.append(plane + 16.0 * (at[1] + at[3]) - (at[0] + at[4]))
            field.append(at[2])
        source = bbuf[p + 2]
        q = apply(shift_of(k), field, stencil, vbuf[p + 2])
        qbuf[k, 0, p] = q[0]
        qbuf[k, 1, p] = q[1]
        return (
            *cmul(field, q),
            q[0] * q[0] - q[1] * q[1],
            2.0 * q[0] * q[1],
            source * q[0],
            source * q[1],
        )

    def energy_terms(k, i, s):
        p = 2 * i + s
        stencil, field = [], []
        for part in range(2):
            at = [qbuf[k, part, p + j] for j in range(3)]
            packed = pack(at[0])
            plane = along(packed) + dot(matrix("ahead"), packed)[0:block]
            stencil.append(plane + 32.0 * at[1] - 2.0 * at[2])
            field.append(at[0])
        return cmul(field, apply(shift_of(k), field, stencil, vbuf[p + 2]))

    def own_step(k, carry):
        @pl.when(k == 1)
        def _():
            for c in range(2):
                for j in range(1, nodes):
                    gather_copy(j, c).wait_recv()
                    forward(j, c).start()
            for j in range(1, nodes):
                note_copy(j).wait_recv()
                halo_copy(j).wait_recv()
                for c in range(2):
                    forward_halo(j, c).start()
            for j in range(1, nodes):
                gather_copy(j, 2).wait_recv()
                for c in range(2, 4):
                    forward(j, c).start()

        for c in range(2):
            forward(k, c).wait_recv()
            forward_halo(k, c).wait_recv()
        added(k, 0, 6, 1, pairs + 1, functools.partial(residual_terms, k))

        def edges(i, inner):
            edge_pair(k, i)
            return inner

        lax.fori_loop(0, pairs, edges, 0)
        added(k, 6, 6, 1, pairs - 1, functools.partial(image_terms, k))
        return carry

    with jax.named_scope("residual"):
        lax.fori_loop(0, nodes, own_step, 0)

    for copy in sides:
        copy.wait_recv()

    def q_copy(k, down):
        if down:
            return remote(
                edge_out.at[k], edge_in.at[k], q_send.at[k], q_recv.at[k], below
            )
        return remote(edge_out.at[k], edge_in.at[k], q_send.at[k], q_recv.at[k], above)

    def x_copy(k):
        there = lax.rem(k + nodes - 1, nodes)
        return remote(
            qhead.at[k], qahead.at[there], x_send.at[k], x_recv.at[there], (peer(nodes - 1), slab)
        )

    def x_arrival(k):
        return remote(
            qhead.at[k], qahead.at[k], x_send.at[k], x_recv.at[k], (peer(nodes - 1), slab)
        )

    def outer_step(k, carry):
        for c in range(2, 4):
            forward(k, c).wait_recv()

        def outer(j, inner):
            for s in range(2):
                residual(k, j * (pairs + 1), s)
            return inner

        lax.fori_loop(0, 2, outer, 0)

        def ends(j, s):
            return image_terms(k, j * (pairs - 1), s)

        added(k, 6, 6, 0, 2, ends)

        def narrowed(first):
            for part in range(2):
                for p in range(2):
                    values = qbuf[k, part, first + p]
                    if narrow:
                        edge_out[k, part, p] = values.astype(bf16)
                    else:
                        filler = jnp.zeros((tall - block, length), f32)
                        edge_out[k, part, p] = jnp.concatenate([values, filler], axis=0).astype(bf16)

        @pl.when(k < lower)
        def _():
            narrowed(0)
            q_copy(k, True).start()

        @pl.when(k >= lower)
        def _():
            narrowed(depth - 2)
            q_copy(k, False).start()

        for part in range(2):
            for p in range(depth):
                qfirst[k, part, 2 * p : 2 * p + 2] = qbuf[k, part, p, 0:2]
                qlast[k, part, 2 * p : 2 * p + 2] = qbuf[k, part, p, block - 2 : block]
            qhead[k, part] = qfirst[k, part].astype(bf16)
        x_copy(k).start()
        return carry

    with jax.named_scope("image"):
        lax.fori_loop(0, nodes, outer_step, 0)

    def energy_step(k, carry):
        @pl.when(k < lower)
        def _():
            q_copy(k, True).wait_recv()
            for part in range(2):
                for p in range(2):
                    qbuf[k, part, depth + p] = wide(edge_in[k, part, p])

        added(k, 12, 2, 0, pairs, functools.partial(energy_terms, k))
        x_arrival(k).wait_recv()
        last = [qlast[k, part] for part in range(2)]
        ahead = [dot(matrix("cross"), qahead[k, part]) for part in range(2)]
        crossing = cmul(last, ahead)
        for part in range(2):
            acc[k * SUMS + 12 + part] += fold(crossing[part] * (1.0 / 24.0))

        @pl.when(k >= lower)
        def _():
            q_copy(k, False).wait_recv()
            near = [wide(edge_in[k, part, 1]) for part in range(2)]
            far = [wide(edge_in[k, part, 0]) for part in range(2)]
            zeroth = [qbuf[k, part, 0] for part in range(2)]
            first = [qbuf[k, part, 1] for part in range(2)]
            one = cmul(zeroth, [32.0 * near[part] - 2.0 * far[part] for part in range(2)])
            two = cmul(first, near)
            for part in range(2):
                acc[k * SUMS + 12 + part] += fold((one[part] - 2.0 * two[part]) * (1.0 / 24.0))

        return carry

    with jax.named_scope("energy"):
        lax.fori_loop(0, nodes, energy_step, 0)

    with jax.named_scope("scalars"):
        lane = lax.broadcasted_iota(jnp.int32, (SUMS, 128), 1)
        shift_at = [lax.rem(node - k + nodes, nodes) for k in range(nodes)]
        mine_sum = jnp.zeros((SUMS, 128), f32)
        for k in range(nodes):
            partial = jnp.sum(acc[k * SUMS : (k + 1) * SUMS], axis=1)
            lanes = partial[:, 0:128]
            for at in range(128, length, 128):
                lanes = lanes + partial[:, at : at + 128]
            whole = jnp.sum(lanes, axis=1, keepdims=True)
            mine_sum = mine_sum + jnp.where(lane == shift_at[k], whole, 0.0)
        sums[0] = mine_sum
        slab_copies = [
            remote(
                sums.at[0],
                sums.at[k],
                s_send.at[k],
                s_recv.at[k],
                (node, lax.rem(slab + k, slabs)),
            )
            for k in range(1, slabs)
        ]
        for copy in slab_copies:
            copy.start()
        for copy in slab_copies:
            copy.wait_recv()
        total = jnp.zeros((SUMS, 128), f32)
        for owner in range(slabs):
            total = total + sums[lax.rem(slab - owner + slabs, slabs)]
        totals[0] = total
        node_copies = [
            remote(totals.at[0], totals.at[k], t_send.at[k], t_recv.at[k], (peer(k), slab))
            for k in range(1, nodes)
        ]
        for copy in node_copies:
            copy.start()
        for copy in node_copies:
            copy.wait_recv()
        total = jnp.zeros((SUMS, 128), f32)
        for owner in range(nodes):
            total = total + totals[lax.rem(node - owner + nodes, nodes)]
        pair = lambda i: (total[i : i + 1], total[i + 1 : i + 2])
        s0, t0, t1, s1, s2, t2, s3 = (pair(i) for i in range(0, 14, 2))
        row_lane = lax.broadcasted_iota(jnp.int32, (8, 128), 1)
        known = jnp.zeros((8, 128), f32)
        for k in range(nodes):
            known = known + jnp.where(row_lane == shift_at[k], notes[k][:, 0:128], 0.0)
        shift = known[0:1], known[1:2]
        weight = known[2:3], known[3:4]
        step0 = cdiv(s0, s1)
        square = cmul(step0, step0)
        norm1 = cmul(square, s2)
        norm1 = norm1[0] - s0[0], norm1[1] - s0[1]
        ratio = cdiv(norm1, s0)
        grow = ratio[0] + 1.0, ratio[1]
        one = cmul(cmul(grow, grow), s1)
        two = cmul(cmul(grow, step0), s2)
        three = cmul(square, s3)
        step1 = cdiv(
            norm1, (one[0] - 2.0 * two[0] + three[0], one[1] - 2.0 * two[1] + three[1])
        )
        coef_r = cmul(step1, grow)
        coef_r = coef_r[0] + step0[0], coef_r[1] + step0[1]
        coef_q = cmul(step1, step0)
        coef_q = -coef_q[0], -coef_q[1]
        inner_r, inner_q = cmul(coef_r, t1), cmul(coef_q, t2)
        inner = t0[0] + inner_r[0] + inner_q[0], t0[1] + inner_r[1] + inner_q[1]
        share = cmul(weight, inner)
        following = cmul(weight, ((shift[0] - 4.0) * 0.2, shift[1] * 0.2))
        sub = lax.broadcasted_iota(jnp.int32, (SUMS, 128), 0)
        factors = jnp.zeros((SUMS, 128), f32)
        for i, entry in enumerate((*weight, *following, *share, *coef_r, *coef_q)):
            factors = jnp.where(sub == i, entry, factors)
        for part in range(2):
            trace[part] = jnp.sum(jnp.where((sub == 4 + part) & (lane < nodes), factors, 0.0))

    with jax.named_scope("moments"):
        scale = []
        for k in range(nodes):
            one_lane = jnp.where(lane == shift_at[k], factors, 0.0)
            values = jnp.broadcast_to(jnp.sum(one_lane, axis=1, keepdims=True), (SUMS, length))
            scale.append([(values[i : i + 1], values[i + 1 : i + 2]) for i in (0, 2, 6, 8)])
        piece = 16 if narrow else block

        def moment_plane(p, carry):
            def step(i, inner_carry):
                rows = pl.ds(pl.multiple_of(i * piece, piece), piece)
                values = [None] * 4
                for k in range(nodes):
                    if narrow:
                        x = [wbuf[k, part, p + 4, rows].astype(f32) for part in range(2)]
                    else:
                        x = [wide(wbuf[k, part, p + 4]) for part in range(2)]
                    r = [rbuf[k, part, p + 2, rows] for part in range(2)]
                    q = [qbuf[k, part, p, rows] for part in range(2)]
                    along_r, along_q = cmul(scale[k][2], r), cmul(scale[k][3], q)
                    field = [x[part] + along_r[part] + along_q[part] for part in range(2)]
                    for degree in range(2):
                        term = cmul(scale[k][degree], field)
                        for part in range(2):
                            at = 2 * degree + part
                            values[at] = term[part] if k == 0 else values[at] + term[part]
                for degree in range(2):
                    for part in range(2):
                        moments[degree, 0, part, p, rows] = values[2 * degree + part]
                return inner_carry

            lax.fori_loop(0, block // piece, step, 0)
            return carry

        lax.fori_loop(0, depth, moment_plane, 0)

    for copy in [*sides, *slab_copies, *node_copies]:
        copy.wait_send()
    for k in range(nodes):
        if k:
            for c in range(3):
                gather_copy(k, c).wait_send()
            halo_copy(k).wait_send()
            note_copy(k).wait_send()
        for c in range(4):
            forward(k, c).wait_send()
        for c in range(2):
            forward_halo(k, c).wait_send()
        q_copy(k, k < lower).wait_send()
        x_copy(k).wait_send()


def per_device(nodes, slabs, probes, potential, warm_start, shift_points, quad_weights):
    depth, width, length = potential.shape
    block = width // nodes
    tall = up_to(block, 16)
    narrow = block % 16 == 0
    pairs = depth // 2
    f32, bf16 = jnp.float32, jnp.bfloat16
    anywhere = pl.BlockSpec(memory_space=pltpu.HBM)
    vector = pl.BlockSpec(memory_space=pltpu.VMEM)
    scalars = pl.BlockSpec(memory_space=pltpu.SMEM)
    dma = pltpu.SemaphoreType.DMA
    small = small_matrices(block, depth)
    picks = halo_picks(width, nodes)
    cpicks = np.zeros((16, 128), ml_dtypes.bfloat16) if narrow else core_picks(width, nodes)
    return pl.pallas_call(
        functools.partial(kernel, nodes, slabs),
        out_shape=(
            jax.ShapeDtypeStruct((2, 1, 2, depth, block, length), f32),
            jax.ShapeDtypeStruct((2,), f32),
        ),
        in_specs=[anywhere] * 9,
        out_specs=(vector, scalars),
        scratch_shapes=[
            pltpu.VMEM((2, depth, width, length), bf16),
            pltpu.VMEM((nodes, 2, pairs, 16, length), bf16),
            pltpu.VMEM((16, 128) if narrow else (nodes, 2, depth, tall, length), bf16),
            pltpu.VMEM((nodes, 2, depth + 8, tall, length), bf16),
            pltpu.VMEM((nodes, 2, pairs + 2, 16, length), bf16),
            pltpu.VMEM((depth + 4, block, length), f32),
            pltpu.VMEM((depth + 4, block, length), f32),
            pltpu.VMEM((2, depth, 8, length), f32),
            pltpu.VMEM((2, depth, 8, length), f32),
            pltpu.VMEM((pairs, 8, length), f32),
            pltpu.VMEM((pairs, 8, length), f32),
            pltpu.VMEM((nodes, 2, depth + 4, block, length), f32),
            pltpu.VMEM((nodes, 2, pairs, 8, length), f32),
            pltpu.VMEM((nodes, 2, depth + 2, block, length), f32),
            pltpu.VMEM((nodes, 2, 16, length), f32),
            pltpu.VMEM((nodes, 2, 16, length), f32),
            pltpu.VMEM((nodes, 2, 16, length), bf16),
            pltpu.VMEM((nodes, 2, 16, length), bf16),
            pltpu.VMEM((nodes, 2, 2, tall, length), bf16),
            pltpu.VMEM((nodes, 2, 2, tall, length), bf16),
            pltpu.VMEM((nodes * SUMS, 8, length), f32),
            pltpu.VMEM((slabs, SUMS, 128), f32),
            pltpu.VMEM((nodes, SUMS, 128), f32),
            pltpu.VMEM((nodes, 8, length), f32),
            pltpu.SMEM((1, 2), f32),
            pltpu.SMEM((1, 2), f32),
            pltpu.VMEM((length, length), bf16),
            pltpu.VMEM(small.shape, bf16),
            pltpu.VMEM(picks.shape, bf16),
            pltpu.VMEM(cpicks.shape, bf16),
            dma((14,)),
            dma((4,)),
            dma((4,)),
            dma((nodes, 5)),
            dma((nodes, 5)),
            dma((nodes, 6)),
            dma((nodes, 6)),
            dma((nodes,)),
            dma((nodes,)),
            dma((nodes,)),
            dma((nodes,)),
            dma((slabs,)),
            dma((slabs,)),
            dma((nodes,)),
            dma((nodes,)),
        ],
        compiler_params=pltpu.CompilerParams(
            collective_id=0, has_side_effects=True, vmem_limit_bytes=60 * 1024 * 1024
        ),
    )(
        warm_start,
        probes,
        potential,
        shift_points,
        quad_weights,
        jnp.asarray(ring_matrix(length, -90.0)),
        jnp.asarray(small),
        jnp.asarray(picks),
        jnp.asarray(cpicks),
    )


def solution(mesh):
    return jax.shard_map(
        functools.partial(per_device, mesh.shape["node"], mesh.shape["grid"]),
        mesh=mesh,
        in_specs=(
            P(None, "grid", None, None),
            P("grid", None, None),
            P("node", None, None, "grid", None, None),
            P("node", None),
            P("node", None),
        ),
        out_specs=(P(None, None, None, "grid", "node", None), P()),
        check_vma=False,
    )
```

```python
import functools

import jax
import jax.numpy as jnp
import ml_dtypes
import numpy as np
from jax import lax
from jax.experimental import pallas as pl
from jax.experimental.pallas import tpu as pltpu
from jax.sharding import PartitionSpec as P

MESH = pl.DeviceIdType.MESH
SUMS = 16
NEAR, FAR = 16.0, -1.0


def up_to(size, step):
    return -(-size // step) * step


def weight_of(distance):
    return {1: NEAR, 2: FAR}.get(abs(distance), 0.0)


def ring_matrix(size, diagonal):
    matrix = np.zeros((size, size), np.float32)
    at = np.arange(size)
    for step, weight in ((1, NEAR), (2, FAR)):
        matrix[at, (at + step) % size] += weight
        matrix[at, (at - step) % size] += weight
    matrix[at, at] += diagonal
    return matrix.astype(ml_dtypes.bfloat16)


def table(block, depth):
    tall = up_to(block, 16)
    pairs = depth // 2
    sizes = {
        "own": (tall, tall),
        "halo0": (tall, 16),
        "halo1": (tall, 16),
        "split0": (tall, 2 * block + 16),
        "split1": (tall, 2 * block + 16),
        "ahead": (tall, 2 * block),
        "edge_own": (16, 2 * tall),
        "edge_halo": (16 * pairs, 16 * (pairs + 2)),
        "cross": (16, 16),
    }
    at, places = 0, {}
    for name, (rows, cols) in sizes.items():
        places[name] = (at, rows, cols)
        at += rows
    return places, at, up_to(max(cols for rows, cols in sizes.values()), 128)


def small_matrices(block, depth):
    tall = up_to(block, 16)
    places, rows, cols = table(block, depth)
    whole = np.zeros((rows, cols), np.float32)
    view = {name: whole[at : at + n, :m] for name, (at, n, m) in places.items()}
    wide = [-4, -3, -2, -1, block, block + 1, block + 2, block + 3]
    slim = [-2, -1, block, block + 1]
    for i in range(block):
        for j in range(block):
            w = weight_of(i - j)
            view["own"][i, j] = w
            for s in range(2):
                view[f"split{s}"][i, j] = w
                view[f"split{s}"][i, block + j] = w
            if j > i:
                view["ahead"][i, j] = 2 * w
                view["ahead"][i, block + j] = 2 * w
        for s in range(2):
            for c, x in enumerate(wide):
                view[f"halo{s}"][i, 8 * s + c] = weight_of(i - x)
            for c, x in enumerate(slim):
                view[f"split{s}"][i, 2 * block + 4 * s + c] = weight_of(i - x)
                view[f"split{s}"][i, 2 * block + 8 + 4 * s + c] = weight_of(i - x)
    for s in range(2):
        for t, x in enumerate(slim):
            row, here = 4 * s + t, wide.index(x)
            for j in range(block):
                view["edge_own"][row, tall * s + j] = weight_of(x - j)
            for i in range(depth // 2):
                to, at = 8 * i + row, 16 * i
                for c, other in enumerate(wide):
                    view["edge_halo"][to, at + 16 + 8 * s + c] += weight_of(x - other)
                for q in range(6):
                    view["edge_halo"][to, at + 8 * q + here] += weight_of(q - 2 - s)
                view["edge_halo"][4 * depth + to, at + 16 + 8 * s + here] = 1.0
    for p in range(depth):
        for e in range(2):
            for f in range(2):
                view["cross"][2 * p + e, 2 * p + f] = 2 * weight_of(2 - e + f)
    return whole.astype(ml_dtypes.bfloat16)


def halo_picks(width, nodes):
    block = width // nodes
    picks = np.zeros((nodes * 16, 2 * width), np.float32)
    for m in range(nodes):
        for s in range(2):
            for c, x in enumerate([-4, -3, -2, -1, block, block + 1, block + 2, block + 3]):
                picks[16 * m + 8 * s + c, width * s + (block * m + x) % width] = 1.0
    return picks.astype(ml_dtypes.bfloat16)


def core_picks(width, nodes):
    block = width // nodes
    tall = up_to(block, 16)
    picks = np.zeros((nodes * tall, width), np.float32)
    for m in range(nodes):
        for i in range(block):
            picks[tall * m + i, block * m + i] = 1.0
    return picks.astype(ml_dtypes.bfloat16)


def cmul(a, b):
    return a[0] * b[0] - a[1] * b[1], a[0] * b[1] + a[1] * b[0]


def cdiv(a, b):
    size = b[0] * b[0] + b[1] * b[1]
    return (a[0] * b[0] + a[1] * b[1]) / size, (a[1] * b[0] - a[0] * b[1]) / size


def fold(values):
    rows, cols = values.shape
    return jnp.sum(values.reshape(rows // 8, 8, cols), axis=0)


def dot(a, b):
    return jnp.dot(a, b, preferred_element_type=jnp.float32)


def kernel(
    nodes,
    slabs,
    warm,
    probes,
    potential,
    shift_hbm,
    weight_hbm,
    along_y_hbm,
    small_hbm,
    picks_hbm,
    core_hbm,
    moments,
    trace,
    own,
    hsend,
    csend,
    wbuf,
    halo,
    bbuf,
    vbuf,
    bside,
    vside,
    bedge,
    vedge,
    rbuf,
    redge,
    far_out,
    far_in,
    qbuf,
    qfirst,
    qlast,
    qhead,
    qahead,
    edge_out,
    edge_in,
    acc,
    sums,
    totals,
    notes,
    shift_ref,
    weight_ref,
    along_y,
    small,
    picks,
    cpicks,
    local_sem,
    b_send,
    b_recv,
    a_send,
    a_recv,
    z_send,
    z_recv,
    q_send,
    q_recv,
    x_send,
    x_recv,
    s_send,
    s_recv,
    t_send,
    t_recv,
):
    f32, bf16 = jnp.float32, jnp.bfloat16
    node, slab = lax.axis_index("node"), lax.axis_index("grid")
    depth, width, length = own.shape[1:]
    pairs = depth // 2
    block = width // nodes
    tall = up_to(block, 16)
    narrow = block % 16 == 0
    lower = nodes // 2
    places = table(block, depth)[0]
    above = (node, lax.rem(slab + 1, slabs))
    below = (node, lax.rem(slab + slabs - 1, slabs))
    step = 16 if narrow else 8
    mine = pl.ds(pl.multiple_of(node * block, step), block)
    left = pl.ds(pl.multiple_of(lax.rem(node * block + width - 8, width), 8), 8)
    right = pl.ds(pl.multiple_of(lax.rem(node * block + block, width), 8), 8)

    def matrix(name):
        at, rows, cols = places[name]
        return small[at : at + rows, 0:cols]

    loads = []

    def load(source, target):
        copy = pltpu.make_async_copy(source, target, local_sem.at[len(loads)])
        copy.start()
        loads.append(copy)

    load(shift_hbm, shift_ref)
    load(weight_hbm, weight_ref)
    load(warm.at[0, 0], own)
    load(picks_hbm, picks)
    if not narrow:
        load(core_hbm, cpicks)
    first_loads = len(loads)
    load(along_y_hbm, along_y)
    load(small_hbm, small)
    load(probes.at[0, :, mine], bbuf.at[2 : depth + 2])
    load(potential.at[:, mine], vbuf.at[2 : depth + 2])
    load(probes.at[0, :, left], bside.at[0])
    load(probes.at[0, :, right], bside.at[1])
    load(potential.at[:, left], vside.at[0])
    load(potential.at[:, right], vside.at[1])
    if narrow:
        load(warm.at[0, 0, :, :, mine], wbuf.at[0, :, 4 : depth + 4])

    barrier = pltpu.get_barrier_semaphore()
    for k in range(1, slabs):
        pl.semaphore_signal(
            barrier, inc=1, device_id=(node, lax.rem(slab + k, slabs)), device_id_type=MESH
        )
    for k in range(1, nodes):
        pl.semaphore_signal(
            barrier, inc=1, device_id=(lax.rem(node + k, nodes), slab), device_id_type=MESH
        )
    pl.semaphore_wait(barrier, slabs + nodes - 2)

    def remote(source, target, send_sem, recv_sem, device):
        return pltpu.make_async_remote_copy(
            src_ref=source,
            dst_ref=target,
            send_sem=send_sem,
            recv_sem=recv_sem,
            device_id=device,
            device_id_type=MESH,
        )

    def peer(k):
        return lax.rem(node + k, nodes)

    def core(m, first, last):
        if narrow:
            rows = pl.ds(pl.multiple_of(m * block, step), block)
            return warm.at[0, 0, :, first:last, rows]
        return csend.at[m, :, first:last]

    chunks = ((0, 2), (depth - 2, depth), (2, depth - 2))

    def gather_copy(k, c):
        first, last = chunks[c]
        return remote(
            core(peer(k), first, last),
            wbuf.at[k, :, 4 + first : 4 + last],
            a_send.at[k, c],
            a_recv.at[k, c],
            (peer(k), slab),
        )

    def halo_copy(k):
        return remote(
            hsend.at[peer(k)],
            halo.at[k, :, 1 : pairs + 1],
            a_send.at[k, 3],
            a_recv.at[k, 3],
            (peer(k), slab),
        )

    def note_copy(k):
        return remote(notes.at[0], notes.at[k], a_send.at[k, 4], a_recv.at[k, 4], (peer(k), slab))

    top = depth + 4
    routes = (
        ((4, 6), (top, top + 2), below),
        ((top - 2, top), (2, 4), above),
        ((6, 7), (top + 2, top + 3), below),
        ((top - 3, top - 2), (1, 2), above),
    )

    def forward(k, c):
        source, target, device = routes[c]
        if isinstance(k, int) and k == 0:
            part = core(node, source[0] - 4, source[1] - 4)
        else:
            part = wbuf.at[k, :, source[0] : source[1]]
        return remote(
            part, wbuf.at[k, :, target[0] : target[1]], z_send.at[k, c], z_recv.at[k, c], device
        )

    def forward_halo(k, c):
        source, target, device = ((1, pairs + 1, below), (pairs, 0, above))[c]
        return remote(
            halo.at[k, :, source],
            halo.at[k, :, target],
            z_send.at[k, 4 + c],
            z_recv.at[k, 4 + c],
            device,
        )

    sides = []
    for at, (source, target) in enumerate(((probes.at[0], bbuf), (potential, vbuf))):
        for c, (first, there, device) in enumerate(
            ((0, depth + 2, below), (depth - 1, 1, above))
        ):
            sides.append(
                remote(
                    source.at[first : first + 1, mine],
                    target.at[there : there + 1],
                    b_send.at[2 * at + c],
                    b_recv.at[2 * at + c],
                    device,
                )
            )

    def far_copy(k, c):
        return remote(
            far_out.at[k, c], far_in.at[k, c], z_send.at[k, 6 + c], z_recv.at[k, 6 + c], routes[c][2]
        )

    def pick():
        for copy in loads[2:first_loads]:
            copy.wait()
        for i in range(pairs):
            for part in range(2):
                rows = own[part, 2 * i : 2 * i + 2].reshape(2 * width, length)
                picked = dot(picks[...], rows).astype(bf16)
                for m in range(nodes):
                    hsend[m, part, i] = picked[16 * m : 16 * m + 16]
        if not narrow:
            for part in range(2):
                for p in range(depth):
                    picked = dot(cpicks[...], own[part, p]).astype(bf16)
                    for m in range(nodes):
                        csend[m, part, p] = picked[tall * m : tall * m + tall]

    def send_cores():
        for c in range(3):
            for k in range(1, nodes):
                gather_copy(k, c).start()
        for c in range(4):
            forward(0, c).start()
            if c == 1:
                for copy in sides:
                    copy.start()

    if narrow:
        send_cores()
    for copy in loads[0:2]:
        copy.wait()
    row = lax.broadcasted_iota(jnp.int32, (8, length), 0)
    note = jnp.zeros((8, length), f32)
    entries = (shift_ref[0, 0], shift_ref[0, 1], weight_ref[0, 0], weight_ref[0, 1])
    for i, entry in enumerate(entries):
        note = jnp.where(row == i, entry, note)
    notes[0] = note
    for k in range(1, nodes):
        note_copy(k).start()
    pick()
    if not narrow:
        send_cores()
    for k in range(1, nodes):
        halo_copy(k).start()
    for part in range(2):
        for i in range(pairs):
            halo[0, part, 1 + i] = hsend[node, part, i]
    for c in range(2):
        forward_halo(0, c).start()
    if not narrow:
        for part in range(2):
            for p in range(depth):
                wbuf[0, part, 4 + p] = csend[node, part, p]

    acc[...] = jnp.zeros_like(acc)
    qfirst[...] = jnp.zeros_like(qfirst)
    qlast[...] = jnp.zeros_like(qlast)
    qbuf[lower:nodes, :, depth : depth + 2] = jnp.zeros((nodes - lower, 2, 2, block, length), f32)
    for copy in loads[first_loads:]:
        copy.wait()
    for i in range(pairs):
        for s in range(2):
            for side in range(2):
                there = 8 * i + 4 * s + 2 * side
                here = 6 if side == 0 else 0
                bedge[there : there + 2] = bside[side, 2 * i + s, here : here + 2]
                vedge[there : there + 2] = vside[side, 2 * i + s, here : here + 2]

    def shift_of(k):
        return notes[k, 0:1, :], notes[k, 1:2, :]

    def apply(shift, field, stencil, local):
        diagonal = shift[0] - local
        return (
            diagonal * field[0] - shift[1] * field[1] + stencil[0] * (1.0 / 24.0),
            diagonal * field[1] + shift[1] * field[0] + stencil[1] * (1.0 / 24.0),
        )

    def added(k, first, count, low, high, terms):
        def body(i, carry):
            for s in range(2):
                carry = tuple(c + fold(v) for c, v in zip(carry, terms(i, s)))
            return carry

        zero = jnp.zeros((8, length), f32)
        for i, total in enumerate(lax.fori_loop(low, high, body, (zero,) * count)):
            acc[k * SUMS + first + i] += total

    def wide(values):
        return values.astype(f32)[0:block]

    def residual(k, i, s):
        pp = 2 * i + s
        stencil, field = [], []
        for part in range(2):
            centre = wbuf[k, part, pp + 2]
            plane = (
                dot(centre, along_y[...])
                + dot(matrix("own"), centre)
                + dot(matrix(f"halo{s}"), halo[k, part, i])
            )[0:block]
            at = [wide(wbuf[k, part, pp + j]) for j in (0, 1, 3, 4)]
            stencil.append(plane + 16.0 * (at[1] + at[2]) - (at[0] + at[3]))
            field.append(wide(centre))
        source = bbuf[pp]
        image = apply(shift_of(k), field, stencil, vbuf[pp])
        r = source - image[0], -image[1]
        rbuf[k, 0, pp] = r[0]
        rbuf[k, 1, pp] = r[1]
        return source, field, r

    def residual_terms(k, i, s):
        source, field, r = residual(k, i, s)
        return (
            r[0] * r[0] - r[1] * r[1],
            2.0 * r[0] * r[1],
            source * field[0],
            source * field[1],
            source * r[0],
            source * r[1],
        )

    def edge_rows(k):
        stencil, field = [], []
        for part in range(2):
            around = halo[k, part].reshape(16 * (pairs + 2), length)
            both = dot(matrix("edge_halo"), around)
            plane = dot(both.astype(bf16), along_y[...])
            beside = [
                dot(matrix("edge_own"), wbuf[k, part, 4 + 2 * i : 6 + 2 * i].reshape(2 * tall, length))
                for i in range(pairs)
            ]
            beside = jnp.concatenate([rows[0:8] for rows in beside], axis=0)
            stencil.append(beside + both[0 : 4 * depth] + plane[4 * depth :])
            field.append(both[4 * depth :])
        image = apply(shift_of(k), field, stencil, vedge[...])
        redge[k, 0] = bedge[...] - image[0]
        redge[k, 1] = -image[1]

    def split(values):
        high = values.astype(bf16)
        return high, (values - high.astype(f32)).astype(bf16)

    def pack(values):
        high, low = split(values)
        if narrow:
            return jnp.concatenate([high, low], axis=0)
        return jnp.concatenate([high.astype(f32), low.astype(f32)], axis=0).astype(bf16)

    def slim(values):
        high, low = split(values)
        return jnp.concatenate([high.astype(f32), low.astype(f32)], axis=0).astype(bf16)

    def along(packed):
        both = dot(packed, along_y[...])
        return both[0:block] + both[block : 2 * block]

    def image_terms(k, i, s):
        p = 2 * i + s
        stencil, field = [], []
        for part in range(2):
            at = [rbuf[k, part, p + j] for j in range(5)]
            packed = pack(at[2])
            side = jnp.concatenate([packed, slim(redge[k, part, pl.ds(pl.multiple_of(8 * i, 8), 8)])], axis=0)
            plane = along(packed) + dot(matrix(f"split{s}"), side)[0:block]
            stencil.append(plane + 16.0 * (at[1] + at[3]) - (at[0] + at[4]))
            field.append(at[2])
        source = bbuf[p + 2]
        q = apply(shift_of(k), field, stencil, vbuf[p + 2])
        qbuf[k, 0, p] = q[0]
        qbuf[k, 1, p] = q[1]
        return (
            *cmul(field, q),
            q[0] * q[0] - q[1] * q[1],
            2.0 * q[0] * q[1],
            source * q[0],
            source * q[1],
        )

    def energy_terms(k, i, s):
        p = 2 * i + s
        stencil, field = [], []
        for part in range(2):
            at = [qbuf[k, part, p + j] for j in range(3)]
            packed = pack(at[0])
            plane = along(packed) + dot(matrix("ahead"), packed)[0:block]
            stencil.append(plane + 32.0 * at[1] - 2.0 * at[2])
            field.append(at[0])
        return cmul(field, apply(shift_of(k), field, stencil, vbuf[p + 2]))

    def narrowed(values):
        if not narrow:
            filler = jnp.zeros((tall - block, length), f32)
            values = jnp.concatenate([values, filler], axis=0)
        return values.astype(bf16)

    def own_step(k, carry):
        @pl.when(k == 1)
        def _():
            for c in range(2):
                for j in range(1, nodes):
                    gather_copy(j, c).wait_recv()
                    forward(j, c).start()
            for j in range(1, nodes):
                note_copy(j).wait_recv()
                halo_copy(j).wait_recv()
                for c in range(2):
                    forward_halo(j, c).start()
            for j in range(1, nodes):
                gather_copy(j, 2).wait_recv()
                for c in range(2, 4):
                    forward(j, c).start()

        for c in range(2):
            forward(k, c).wait_recv()
            forward_halo(k, c).wait_recv()
        added(k, 0, 6, 1, pairs + 1, functools.partial(residual_terms, k))

        for c, at in enumerate((3, depth)):
            for part in range(2):
                far_out[k, c, part] = narrowed(rbuf[k, part, at])
            far_copy(k, c).start()
        edge_rows(k)
        added(k, 6, 6, 1, pairs - 1, functools.partial(image_terms, k))
        return carry

    with jax.named_scope("residual"):
        lax.fori_loop(0, nodes, own_step, 0)

    for copy in sides:
        copy.wait_recv()

    def q_copy(k, down):
        if down:
            return remote(
                edge_out.at[k], edge_in.at[k], q_send.at[k], q_recv.at[k], below
            )
        return remote(edge_out.at[k], edge_in.at[k], q_send.at[k], q_recv.at[k], above)

    def x_copy(k):
        there = lax.rem(k + nodes - 1, nodes)
        return remote(
            qhead.at[k], qahead.at[there], x_send.at[k], x_recv.at[there], (peer(nodes - 1), slab)
        )

    def x_arrival(k):
        return remote(
            qhead.at[k], qahead.at[k], x_send.at[k], x_recv.at[k], (peer(nodes - 1), slab)
        )

    def outer_step(k, carry):
        for c in range(2, 4):
            forward(k, c).wait_recv()

        residual(k, 0, 1)
        residual(k, pairs + 1, 0)
        for c, at in enumerate((depth + 3, 0)):
            far_copy(k, c).wait_recv()
            for part in range(2):
                rbuf[k, part, at] = wide(far_in[k, c, part])

        def ends(j, s):
            return image_terms(k, j * (pairs - 1), s)

        added(k, 6, 6, 0, 2, ends)

        def share_q(first):
            for part in range(2):
                for p in range(2):
                    edge_out[k, part, p] = narrowed(qbuf[k, part, first + p])

        @pl.when(k < lower)
        def _():
            share_q(0)
            q_copy(k, True).start()

        @pl.when(k >= lower)
        def _():
            share_q(depth - 2)
            q_copy(k, False).start()

        for part in range(2):
            for p in range(depth):
                qfirst[k, part, 2 * p : 2 * p + 2] = qbuf[k, part, p, 0:2]
                qlast[k, part, 2 * p : 2 * p + 2] = qbuf[k, part, p, block - 2 : block]
            qhead[k, part] = qfirst[k, part].astype(bf16)
        x_copy(k).start()
        return carry

    with jax.named_scope("image"):
        lax.fori_loop(0, nodes, outer_step, 0)

    def energy_step(k, carry):
        @pl.when(k < lower)
        def _():
            q_copy(k, True).wait_recv()
            for part in range(2):
                for p in range(2):
                    qbuf[k, part, depth + p] = wide(edge_in[k, part, p])

        added(k, 12, 2, 0, pairs, functools.partial(energy_terms, k))
        x_arrival(k).wait_recv()
        last = [qlast[k, part] for part in range(2)]
        ahead = [dot(matrix("cross"), qahead[k, part]) for part in range(2)]
        crossing = cmul(last, ahead)
        for part in range(2):
            acc[k * SUMS + 12 + part] += fold(crossing[part] * (1.0 / 24.0))

        @pl.when(k >= lower)
        def _():
            q_copy(k, False).wait_recv()
            near = [wide(edge_in[k, part, 1]) for part in range(2)]
            far = [wide(edge_in[k, part, 0]) for part in range(2)]
            zeroth = [qbuf[k, part, 0] for part in range(2)]
            first = [qbuf[k, part, 1] for part in range(2)]
            one = cmul(zeroth, [32.0 * near[part] - 2.0 * far[part] for part in range(2)])
            two = cmul(first, near)
            for part in range(2):
                acc[k * SUMS + 12 + part] += fold((one[part] - 2.0 * two[part]) * (1.0 / 24.0))

        return carry

    with jax.named_scope("energy"):
        lax.fori_loop(0, nodes, energy_step, 0)

    with jax.named_scope("scalars"):
        lane = lax.broadcasted_iota(jnp.int32, (SUMS, 128), 1)
        shift_at = [lax.rem(node - k + nodes, nodes) for k in range(nodes)]
        mine_sum = jnp.zeros((SUMS, 128), f32)
        for k in range(nodes):
            partial = jnp.sum(acc[k * SUMS : (k + 1) * SUMS], axis=1)
            lanes = partial[:, 0:128]
            for at in range(128, length, 128):
                lanes = lanes + partial[:, at : at + 128]
            whole = jnp.sum(lanes, axis=1, keepdims=True)
            mine_sum = mine_sum + jnp.where(lane == shift_at[k], whole, 0.0)
        sums[0] = mine_sum
        slab_copies = [
            remote(
                sums.at[0],
                sums.at[k],
                s_send.at[k],
                s_recv.at[k],
                (node, lax.rem(slab + k, slabs)),
            )
            for k in range(1, slabs)
        ]
        for copy in slab_copies:
            copy.start()
        for copy in slab_copies:
            copy.wait_recv()
        total = jnp.zeros((SUMS, 128), f32)
        for owner in range(slabs):
            total = total + sums[lax.rem(slab - owner + slabs, slabs)]
        totals[0] = total
        node_copies = [
            remote(totals.at[0], totals.at[k], t_send.at[k], t_recv.at[k], (peer(k), slab))
            for k in range(1, nodes)
        ]
        for copy in node_copies:
            copy.start()
        for copy in node_copies:
            copy.wait_recv()
        total = jnp.zeros((SUMS, 128), f32)
        for owner in range(nodes):
            total = total + totals[lax.rem(node - owner + nodes, nodes)]
        pair = lambda i: (total[i : i + 1], total[i + 1 : i + 2])
        s0, t0, t1, s1, s2, t2, s3 = (pair(i) for i in range(0, 14, 2))
        row_lane = lax.broadcasted_iota(jnp.int32, (8, 128), 1)
        known = jnp.zeros((8, 128), f32)
        for k in range(nodes):
            known = known + jnp.where(row_lane == shift_at[k], notes[k][:, 0:128], 0.0)
        shift = known[0:1], known[1:2]
        weight = known[2:3], known[3:4]
        step0 = cdiv(s0, s1)
        square = cmul(step0, step0)
        norm1 = cmul(square, s2)
        norm1 = norm1[0] - s0[0], norm1[1] - s0[1]
        ratio = cdiv(norm1, s0)
        grow = ratio[0] + 1.0, ratio[1]
        one = cmul(cmul(grow, grow), s1)
        two = cmul(cmul(grow, step0), s2)
        three = cmul(square, s3)
        step1 = cdiv(
            norm1, (one[0] - 2.0 * two[0] + three[0], one[1] - 2.0 * two[1] + three[1])
        )
        coef_r = cmul(step1, grow)
        coef_r = coef_r[0] + step0[0], coef_r[1] + step0[1]
        coef_q = cmul(step1, step0)
        coef_q = -coef_q[0], -coef_q[1]
        inner_r, inner_q = cmul(coef_r, t1), cmul(coef_q, t2)
        inner = t0[0] + inner_r[0] + inner_q[0], t0[1] + inner_r[1] + inner_q[1]
        share = cmul(weight, inner)
        following = cmul(weight, ((shift[0] - 4.0) * 0.2, shift[1] * 0.2))
        sub = lax.broadcasted_iota(jnp.int32, (SUMS, 128), 0)
        factors = jnp.zeros((SUMS, 128), f32)
        for i, entry in enumerate((*weight, *following, *share, *coef_r, *coef_q)):
            factors = jnp.where(sub == i, entry, factors)
        for part in range(2):
            trace[part] = jnp.sum(jnp.where((sub == 4 + part) & (lane < nodes), factors, 0.0))

    with jax.named_scope("moments"):
        scale = []
        for k in range(nodes):
            one_lane = jnp.where(lane == shift_at[k], factors, 0.0)
            values = jnp.broadcast_to(jnp.sum(one_lane, axis=1, keepdims=True), (SUMS, length))
            scale.append([(values[i : i + 1], values[i + 1 : i + 2]) for i in (0, 2, 6, 8)])
        piece = 16 if narrow else block

        def moment_plane(p, carry):
            def step(i, inner_carry):
                rows = pl.ds(pl.multiple_of(i * piece, piece), piece)
                values = [None] * 4
                for k in range(nodes):
                    if narrow:
                        x = [wbuf[k, part, p + 4, rows].astype(f32) for part in range(2)]
                    else:
                        x = [wide(wbuf[k, part, p + 4]) for part in range(2)]
                    r = [rbuf[k, part, p + 2, rows] for part in range(2)]
                    q = [qbuf[k, part, p, rows] for part in range(2)]
                    along_r, along_q = cmul(scale[k][2], r), cmul(scale[k][3], q)
                    field = [x[part] + along_r[part] + along_q[part] for part in range(2)]
                    for degree in range(2):
                        term = cmul(scale[k][degree], field)
                        for part in range(2):
                            at = 2 * degree + part
                            values[at] = term[part] if k == 0 else values[at] + term[part]
                for degree in range(2):
                    for part in range(2):
                        moments[degree, 0, part, p, rows] = values[2 * degree + part]
                return inner_carry

            lax.fori_loop(0, block // piece, step, 0)
            return carry

        lax.fori_loop(0, depth, moment_plane, 0)

    for copy in [*sides, *slab_copies, *node_copies]:
        copy.wait_send()
    for k in range(nodes):
        if k:
            for c in range(3):
                gather_copy(k, c).wait_send()
            halo_copy(k).wait_send()
            note_copy(k).wait_send()
        for c in range(4):
            forward(k, c).wait_send()
        for c in range(2):
            forward_halo(k, c).wait_send()
            far_copy(k, c).wait_send()
        q_copy(k, k < lower).wait_send()
        x_copy(k).wait_send()


def per_device(nodes, slabs, probes, potential, warm_start, shift_points, quad_weights):
    depth, width, length = potential.shape
    block = width // nodes
    tall = up_to(block, 16)
    narrow = block % 16 == 0
    pairs = depth // 2
    f32, bf16 = jnp.float32, jnp.bfloat16
    anywhere = pl.BlockSpec(memory_space=pltpu.HBM)
    vector = pl.BlockSpec(memory_space=pltpu.VMEM)
    scalars = pl.BlockSpec(memory_space=pltpu.SMEM)
    dma = pltpu.SemaphoreType.DMA
    small = small_matrices(block, depth)
    picks = halo_picks(width, nodes)
    cpicks = picks if narrow else core_picks(width, nodes)
    return pl.pallas_call(
        functools.partial(kernel, nodes, slabs),
        out_shape=(
            pltpu.VMEM((2, 1, 2, depth, block, length), f32),
            jax.ShapeDtypeStruct((2,), f32),
        ),
        in_specs=[anywhere] * 9,
        out_specs=(vector, scalars),
        scratch_shapes=[
            pltpu.VMEM((2, depth, width, length), bf16),
            pltpu.VMEM((nodes, 2, pairs, 16, length), bf16),
            pltpu.VMEM((16, 128) if narrow else (nodes, 2, depth, tall, length), bf16),
            pltpu.VMEM((nodes, 2, depth + 8, tall, length), bf16),
            pltpu.VMEM((nodes, 2, pairs + 2, 16, length), bf16),
            pltpu.VMEM((depth + 4, block, length), f32),
            pltpu.VMEM((depth + 4, block, length), f32),
            pltpu.VMEM((2, depth, 8, length), f32),
            pltpu.VMEM((2, depth, 8, length), f32),
            pltpu.VMEM((4 * depth, length), f32),
            pltpu.VMEM((4 * depth, length), f32),
            pltpu.VMEM((nodes, 2, depth + 4, block, length), f32),
            pltpu.VMEM((nodes, 2, 4 * depth, length), f32),
            pltpu.VMEM((nodes, 2, 2, tall, length), bf16),
            pltpu.VMEM((nodes, 2, 2, tall, length), bf16),
            pltpu.VMEM((nodes, 2, depth + 2, block, length), f32),
            pltpu.VMEM((nodes, 2, 16, length), f32),
            pltpu.VMEM((nodes, 2, 16, length), f32),
            pltpu.VMEM((nodes, 2, 16, length), bf16),
            pltpu.VMEM((nodes, 2, 16, length), bf16),
            pltpu.VMEM((nodes, 2, 2, tall, length), bf16),
            pltpu.VMEM((nodes, 2, 2, tall, length), bf16),
            pltpu.VMEM((nodes * SUMS, 8, length), f32),
            pltpu.VMEM((slabs, SUMS, 128), f32),
            pltpu.VMEM((nodes, SUMS, 128), f32),
            pltpu.VMEM((nodes, 8, length), f32),
            pltpu.SMEM((1, 2), f32),
            pltpu.SMEM((1, 2), f32),
            pltpu.VMEM((length, length), bf16),
            pltpu.VMEM(small.shape, bf16),
            pltpu.VMEM(picks.shape, bf16),
            pltpu.VMEM((16, 128) if narrow else cpicks.shape, bf16),
            dma((14,)),
            dma((4,)),
            dma((4,)),
            dma((nodes, 5)),
            dma((nodes, 5)),
            dma((nodes, 8)),
            dma((nodes, 8)),
            dma((nodes,)),
            dma((nodes,)),
            dma((nodes,)),
            dma((nodes,)),
            dma((slabs,)),
            dma((slabs,)),
            dma((nodes,)),
            dma((nodes,)),
        ],
        compiler_params=pltpu.CompilerParams(
            collective_id=0, has_side_effects=True, vmem_limit_bytes=58 * 1024 * 1024
        ),
    )(
        warm_start,
        probes,
        potential,
        shift_points,
        quad_weights,
        jnp.asarray(ring_matrix(length, -90.0)),
        jnp.asarray(small),
        jnp.asarray(picks),
        jnp.asarray(cpicks),
    )


def solution(mesh):
    return jax.shard_map(
        functools.partial(per_device, mesh.shape["node"], mesh.shape["grid"]),
        mesh=mesh,
        in_specs=(
            P(None, "grid", None, None),
            P("grid", None, None),
            P("node", None, None, "grid", None, None),
            P("node", None),
            P("node", None),
        ),
        out_specs=(P(None, None, None, "grid", "node", None), P()),
        check_vma=False,
    )
```

```python
import functools

import jax
import jax.numpy as jnp
import ml_dtypes
import numpy as np
from jax import lax
from jax.experimental import pallas as pl
from jax.experimental.pallas import tpu as pltpu
from jax.sharding import PartitionSpec as P

MESH = pl.DeviceIdType.MESH
SUMS = 16
NEAR, FAR = 16.0, -1.0


def up_to(size, step):
    return -(-size // step) * step


def weight_of(distance):
    return {1: NEAR, 2: FAR}.get(abs(distance), 0.0)


def ring_matrix(size, diagonal):
    matrix = np.zeros((size, size), np.float32)
    at = np.arange(size)
    for step, weight in ((1, NEAR), (2, FAR)):
        matrix[at, (at + step) % size] += weight
        matrix[at, (at - step) % size] += weight
    matrix[at, at] += diagonal
    return matrix.astype(ml_dtypes.bfloat16)


def table(block, depth):
    tall = up_to(block, 16)
    pairs = depth // 2
    sizes = {
        "own": (tall, tall),
        "halo0": (tall, 16),
        "halo1": (tall, 16),
        "split0": (tall, 2 * block + 16),
        "split1": (tall, 2 * block + 16),
        "ahead": (tall, 2 * block),
        "edge_own": (16, 2 * tall),
        "edge_halo": (16 * pairs, 16 * (pairs + 2)),
        "cross": (16, 16),
    }
    at, places = 0, {}
    for name, (rows, cols) in sizes.items():
        places[name] = (at, rows, cols)
        at += rows
    return places, at, up_to(max(cols for rows, cols in sizes.values()), 128)


def small_matrices(block, depth):
    tall = up_to(block, 16)
    places, rows, cols = table(block, depth)
    whole = np.zeros((rows, cols), np.float32)
    view = {name: whole[at : at + n, :m] for name, (at, n, m) in places.items()}
    wide = [-4, -3, -2, -1, block, block + 1, block + 2, block + 3]
    slim = [-2, -1, block, block + 1]
    for i in range(block):
        for j in range(block):
            w = weight_of(i - j)
            view["own"][i, j] = w
            for s in range(2):
                view[f"split{s}"][i, j] = w
                view[f"split{s}"][i, block + j] = w
            if j > i:
                view["ahead"][i, j] = 2 * w
                view["ahead"][i, block + j] = 2 * w
        for s in range(2):
            for c, x in enumerate(wide):
                view[f"halo{s}"][i, 8 * s + c] = weight_of(i - x)
            for c, x in enumerate(slim):
                view[f"split{s}"][i, 2 * block + 4 * s + c] = weight_of(i - x)
                view[f"split{s}"][i, 2 * block + 8 + 4 * s + c] = weight_of(i - x)
    for s in range(2):
        for t, x in enumerate(slim):
            row, here = 4 * s + t, wide.index(x)
            for j in range(block):
                view["edge_own"][row, tall * s + j] = weight_of(x - j)
            for i in range(depth // 2):
                to, at = 8 * i + row, 16 * i
                for c, other in enumerate(wide):
                    view["edge_halo"][to, at + 16 + 8 * s + c] += weight_of(x - other)
                for q in range(6):
                    view["edge_halo"][to, at + 8 * q + here] += weight_of(q - 2 - s)
                view["edge_halo"][4 * depth + to, at + 16 + 8 * s + here] = 1.0
    for p in range(depth):
        for e in range(2):
            for f in range(2):
                view["cross"][2 * p + e, 2 * p + f] = 2 * weight_of(2 - e + f)
    return whole.astype(ml_dtypes.bfloat16)


def halo_picks(width, nodes):
    block = width // nodes
    picks = np.zeros((nodes * 16, 2 * width), np.float32)
    for m in range(nodes):
        for s in range(2):
            for c, x in enumerate([-4, -3, -2, -1, block, block + 1, block + 2, block + 3]):
                picks[16 * m + 8 * s + c, width * s + (block * m + x) % width] = 1.0
    return picks.astype(ml_dtypes.bfloat16)


def core_picks(width, nodes):
    block = width // nodes
    tall = up_to(block, 16)
    picks = np.zeros((nodes * tall, width), np.float32)
    for m in range(nodes):
        for i in range(block):
            picks[tall * m + i, block * m + i] = 1.0
    return picks.astype(ml_dtypes.bfloat16)


def offsets(nodes):
    every = [(a, b) for a in range(nodes // 2) for b in range(2)]
    return [(0, 0)] + sorted(every[1:], key=lambda at: -(at[0] > 0) - (at[1] > 0))


def cmul(a, b):
    return a[0] * b[0] - a[1] * b[1], a[0] * b[1] + a[1] * b[0]


def cdiv(a, b):
    size = b[0] * b[0] + b[1] * b[1]
    return (a[0] * b[0] + a[1] * b[1]) / size, (a[1] * b[0] - a[0] * b[1]) / size


def fold(values):
    rows, cols = values.shape
    return jnp.sum(values.reshape(rows // 8, 8, cols), axis=0)


def dot(a, b):
    return jnp.dot(a, b, preferred_element_type=jnp.float32)


def kernel(
    nodes,
    slabs,
    warm,
    probes,
    potential,
    shift_hbm,
    weight_hbm,
    along_y_hbm,
    small_hbm,
    picks_hbm,
    core_hbm,
    moments,
    trace,
    own,
    hsend,
    csend,
    wbuf,
    halo,
    bbuf,
    vbuf,
    bside,
    vside,
    bedge,
    vedge,
    rbuf,
    redge,
    far_out,
    far_in,
    qbuf,
    qfirst,
    qlast,
    qhead,
    qahead,
    edge_out,
    edge_in,
    acc,
    sums,
    notes,
    shift_ref,
    weight_ref,
    along_y,
    small,
    picks,
    cpicks,
    local_sem,
    b_send,
    b_recv,
    a_send,
    a_recv,
    z_send,
    z_recv,
    q_send,
    q_recv,
    x_send,
    x_recv,
    s_send,
    s_recv,
):
    f32, bf16 = jnp.float32, jnp.bfloat16
    node, slab = lax.axis_index("node"), lax.axis_index("grid")
    depth, width, length = own.shape[1:]
    pairs = depth // 2
    block = width // nodes
    tall = up_to(block, 16)
    narrow = block % 16 == 0
    lower = nodes // 2
    places = table(block, depth)[0]
    above = (node, lax.rem(slab + 1, slabs))
    below = (node, lax.rem(slab + slabs - 1, slabs))
    step = 16 if narrow else 8
    mine = pl.ds(pl.multiple_of(node * block, step), block)
    left = pl.ds(pl.multiple_of(lax.rem(node * block + width - 8, width), 8), 8)
    right = pl.ds(pl.multiple_of(lax.rem(node * block + block, width), 8), 8)

    def matrix(name):
        at, rows, cols = places[name]
        return small[at : at + rows, 0:cols]

    loads = []

    def load(source, target):
        copy = pltpu.make_async_copy(source, target, local_sem.at[len(loads)])
        copy.start()
        loads.append(copy)

    load(shift_hbm, shift_ref)
    load(weight_hbm, weight_ref)
    load(warm.at[0, 0], own)
    load(picks_hbm, picks)
    if not narrow:
        load(core_hbm, cpicks)
    first_loads = len(loads)
    load(along_y_hbm, along_y)
    load(small_hbm, small)
    load(probes.at[0, :, mine], bbuf.at[2 : depth + 2])
    load(potential.at[:, mine], vbuf.at[2 : depth + 2])
    load(probes.at[0, :, left], bside.at[0])
    load(probes.at[0, :, right], bside.at[1])
    load(potential.at[:, left], vside.at[0])
    load(potential.at[:, right], vside.at[1])
    if narrow:
        load(warm.at[0, 0, :, :, mine], wbuf.at[0, :, 4 : depth + 4])

    barrier = pltpu.get_barrier_semaphore()
    for k in range(1, slabs):
        pl.semaphore_signal(
            barrier, inc=1, device_id=(node, lax.rem(slab + k, slabs)), device_id_type=MESH
        )
    for k in range(1, nodes):
        pl.semaphore_signal(
            barrier, inc=1, device_id=(lax.rem(node + k, nodes), slab), device_id_type=MESH
        )
    pl.semaphore_wait(barrier, slabs + nodes - 2)

    def remote(source, target, send_sem, recv_sem, device):
        return pltpu.make_async_remote_copy(
            src_ref=source,
            dst_ref=target,
            send_sem=send_sem,
            recv_sem=recv_sem,
            device_id=device,
            device_id_type=MESH,
        )

    steps = offsets(nodes)
    distant = sum(1 for a, b in steps if a and b)
    tall_y = nodes // 2
    at_y, at_x = node // 2, lax.rem(node, 2)

    def peer(k):
        a, b = steps[k]
        return lax.rem(at_y + a, tall_y) * 2 + lax.rem(at_x + b, 2)

    def owner_of(k):
        a, b = steps[k]
        return lax.rem(at_y + tall_y - a, tall_y) * 2 + lax.rem(at_x + b, 2)

    def core(m, first, last):
        if narrow:
            rows = pl.ds(pl.multiple_of(m * block, step), block)
            return warm.at[0, 0, :, first:last, rows]
        return csend.at[m, :, first:last]

    chunks = ((0, 2), (depth - 2, depth), (2, depth - 2))

    def gather_copy(k, c):
        first, last = chunks[c]
        return remote(
            core(peer(k), first, last),
            wbuf.at[k, :, 4 + first : 4 + last],
            a_send.at[k, c],
            a_recv.at[k, c],
            (peer(k), slab),
        )

    def halo_copy(k):
        return remote(
            hsend.at[peer(k)],
            halo.at[k, :, 1 : pairs + 1],
            a_send.at[k, 3],
            a_recv.at[k, 3],
            (peer(k), slab),
        )

    def note_copy(k):
        return remote(notes.at[0], notes.at[k], a_send.at[k, 4], a_recv.at[k, 4], (peer(k), slab))

    top = depth + 4
    routes = (
        ((4, 6), (top, top + 2), below),
        ((top - 2, top), (2, 4), above),
        ((6, 7), (top + 2, top + 3), below),
        ((top - 3, top - 2), (1, 2), above),
    )

    def forward(k, c):
        source, target, device = routes[c]
        if isinstance(k, int) and k == 0:
            part = core(node, source[0] - 4, source[1] - 4)
        else:
            part = wbuf.at[k, :, source[0] : source[1]]
        return remote(
            part, wbuf.at[k, :, target[0] : target[1]], z_send.at[k, c], z_recv.at[k, c], device
        )

    def forward_halo(k, c):
        source, target, device = ((1, pairs + 1, below), (pairs, 0, above))[c]
        return remote(
            halo.at[k, :, source],
            halo.at[k, :, target],
            z_send.at[k, 4 + c],
            z_recv.at[k, 4 + c],
            device,
        )

    sides = []
    for at, (source, target) in enumerate(((probes.at[0], bbuf), (potential, vbuf))):
        for c, (first, there, device) in enumerate(
            ((0, depth + 2, below), (depth - 1, 1, above))
        ):
            sides.append(
                remote(
                    source.at[first : first + 1, mine],
                    target.at[there : there + 1],
                    b_send.at[2 * at + c],
                    b_recv.at[2 * at + c],
                    device,
                )
            )

    def far_copy(k, c):
        return remote(
            far_out.at[k, c], far_in.at[k, c], z_send.at[k, 6 + c], z_recv.at[k, 6 + c], routes[c][2]
        )

    order = [(k, c) for c in range(3) for k in range(1, nodes)]

    def pick():
        for copy in loads[2:first_loads]:
            copy.wait()
        for i in range(pairs):
            for part in range(2):
                rows = own[part, 2 * i : 2 * i + 2].reshape(2 * width, length)
                picked = dot(picks[...], rows).astype(bf16)
                for m in range(nodes):
                    hsend[m, part, i] = picked[16 * m : 16 * m + 16]
        if not narrow:
            for part in range(2):
                for p in range(depth):
                    picked = dot(cpicks[...], own[part, p]).astype(bf16)
                    for m in range(nodes):
                        csend[m, part, p] = picked[tall * m : tall * m + tall]

    def send_cores():
        for k, c in order:
            gather_copy(k, c).start()
        for c in range(4):
            forward(0, c).start()
        for copy in sides:
            copy.start()

    if narrow:
        send_cores()
    for copy in loads[0:2]:
        copy.wait()
    row = lax.broadcasted_iota(jnp.int32, (8, length), 0)
    note = jnp.zeros((8, length), f32)
    entries = (shift_ref[0, 0], shift_ref[0, 1], weight_ref[0, 0], weight_ref[0, 1])
    for i, entry in enumerate(entries):
        note = jnp.where(row == i, entry, note)
    notes[0] = note
    for k in range(1, nodes):
        note_copy(k).start()
    pick()
    if not narrow:
        send_cores()
    for k in range(1, nodes):
        halo_copy(k).start()
    for part in range(2):
        for i in range(pairs):
            halo[0, part, 1 + i] = hsend[node, part, i]
    for c in range(2):
        forward_halo(0, c).start()
    if not narrow:
        for part in range(2):
            for p in range(depth):
                wbuf[0, part, 4 + p] = csend[node, part, p]

    acc[...] = jnp.zeros_like(acc)
    qfirst[...] = jnp.zeros_like(qfirst)
    qlast[...] = jnp.zeros_like(qlast)
    qbuf[lower:nodes, :, depth : depth + 2] = jnp.zeros((nodes - lower, 2, 2, block, length), f32)
    for copy in loads[first_loads:]:
        copy.wait()
    for i in range(pairs):
        for s in range(2):
            for side in range(2):
                there = 8 * i + 4 * s + 2 * side
                here = 6 if side == 0 else 0
                bedge[there : there + 2] = bside[side, 2 * i + s, here : here + 2]
                vedge[there : there + 2] = vside[side, 2 * i + s, here : here + 2]

    def shift_of(k):
        return notes[k, 0:1, :], notes[k, 1:2, :]

    def apply(shift, field, stencil, local):
        diagonal = shift[0] - local
        return (
            diagonal * field[0] - shift[1] * field[1] + stencil[0] * (1.0 / 24.0),
            diagonal * field[1] + shift[1] * field[0] + stencil[1] * (1.0 / 24.0),
        )

    def added(k, first, count, low, high, terms):
        def body(i, carry):
            for s in range(2):
                carry = tuple(c + fold(v) for c, v in zip(carry, terms(i, s)))
            return carry

        zero = jnp.zeros((8, length), f32)
        for i, total in enumerate(lax.fori_loop(low, high, body, (zero,) * count)):
            acc[k * SUMS + first + i] += total

    def wide(values):
        return values.astype(f32)[0:block]

    def residual(k, i, s):
        pp = 2 * i + s
        stencil, field = [], []
        for part in range(2):
            centre = wbuf[k, part, pp + 2]
            plane = (
                dot(centre, along_y[...])
                + dot(matrix("own"), centre)
                + dot(matrix(f"halo{s}"), halo[k, part, i])
            )[0:block]
            at = [wide(wbuf[k, part, pp + j]) for j in (0, 1, 3, 4)]
            stencil.append(plane + 16.0 * (at[1] + at[2]) - (at[0] + at[3]))
            field.append(wide(centre))
        source = bbuf[pp]
        image = apply(shift_of(k), field, stencil, vbuf[pp])
        r = source - image[0], -image[1]
        rbuf[k, 0, pp] = r[0]
        rbuf[k, 1, pp] = r[1]
        return source, field, r

    def residual_terms(k, i, s):
        source, field, r = residual(k, i, s)
        return (
            r[0] * r[0] - r[1] * r[1],
            2.0 * r[0] * r[1],
            source * field[0],
            source * field[1],
            source * r[0],
            source * r[1],
        )

    def edge_rows(k):
        stencil, field = [], []
        for part in range(2):
            around = halo[k, part].reshape(16 * (pairs + 2), length)
            both = dot(matrix("edge_halo"), around)
            plane = dot(both.astype(bf16), along_y[...])
            beside = [
                dot(matrix("edge_own"), wbuf[k, part, 4 + 2 * i : 6 + 2 * i].reshape(2 * tall, length))
                for i in range(pairs)
            ]
            beside = jnp.concatenate([rows[0:8] for rows in beside], axis=0)
            stencil.append(beside + both[0 : 4 * depth] + plane[4 * depth :])
            field.append(both[4 * depth :])
        image = apply(shift_of(k), field, stencil, vedge[...])
        redge[k, 0] = bedge[...] - image[0]
        redge[k, 1] = -image[1]

    def split(values):
        high = values.astype(bf16)
        return high, (values - high.astype(f32)).astype(bf16)

    def pack(values):
        high, low = split(values)
        if narrow:
            return jnp.concatenate([high, low], axis=0)
        return jnp.concatenate([high.astype(f32), low.astype(f32)], axis=0).astype(bf16)

    def slim(values):
        high, low = split(values)
        return jnp.concatenate([high.astype(f32), low.astype(f32)], axis=0).astype(bf16)

    def along(packed):
        both = dot(packed, along_y[...])
        return both[0:block] + both[block : 2 * block]

    def image_terms(k, i, s):
        p = 2 * i + s
        stencil, field = [], []
        for part in range(2):
            at = [rbuf[k, part, p + j] for j in range(5)]
            packed = pack(at[2])
            side = jnp.concatenate([packed, slim(redge[k, part, pl.ds(pl.multiple_of(8 * i, 8), 8)])], axis=0)
            plane = along(packed) + dot(matrix(f"split{s}"), side)[0:block]
            stencil.append(plane + 16.0 * (at[1] + at[3]) - (at[0] + at[4]))
            field.append(at[2])
        source = bbuf[p + 2]
        q = apply(shift_of(k), field, stencil, vbuf[p + 2])
        qbuf[k, 0, p] = q[0]
        qbuf[k, 1, p] = q[1]
        return (
            *cmul(field, q),
            q[0] * q[0] - q[1] * q[1],
            2.0 * q[0] * q[1],
            source * q[0],
            source * q[1],
        )

    def energy_terms(k, i, s):
        p = 2 * i + s
        stencil, field = [], []
        for part in range(2):
            at = [qbuf[k, part, p + j] for j in range(3)]
            packed = pack(at[0])
            plane = along(packed) + dot(matrix("ahead"), packed)[0:block]
            stencil.append(plane + 32.0 * at[1] - 2.0 * at[2])
            field.append(at[0])
        return cmul(field, apply(shift_of(k), field, stencil, vbuf[p + 2]))

    def narrowed(values):
        if not narrow:
            filler = jnp.zeros((tall - block, length), f32)
            values = jnp.concatenate([values, filler], axis=0)
        return values.astype(bf16)

    def own_step(k, carry):
        @pl.when(k == 1)
        def _():
            for at, (j, c) in enumerate(order):
                if at == 2 * (nodes - 1):
                    for m in range(1, nodes):
                        note_copy(m).wait_recv()
                        halo_copy(m).wait_recv()
                        for d in range(2):
                            forward_halo(m, d).start()
                gather_copy(j, c).wait_recv()
                for d in (c,) if c < 2 else (2, 3):
                    forward(j, d).start()

        for c in range(2):
            forward(k, c).wait_recv()
            forward_halo(k, c).wait_recv()
        added(k, 0, 6, 1, pairs + 1, functools.partial(residual_terms, k))

        for c, at in enumerate((3, depth)):
            for part in range(2):
                far_out[k, c, part] = narrowed(rbuf[k, part, at])
            far_copy(k, c).start()
        edge_rows(k)
        added(k, 6, 6, 1, pairs - 1, functools.partial(image_terms, k))
        return carry

    with jax.named_scope("residual"):
        lax.fori_loop(0, nodes, own_step, 0)

    for copy in sides:
        copy.wait_recv()

    previous = lax.rem(node + nodes - 1, nodes)

    def q_copy(k, down):
        if down:
            return remote(
                edge_out.at[k], edge_in.at[k], q_send.at[k], q_recv.at[k], below
            )
        return remote(edge_out.at[k], edge_in.at[k], q_send.at[k], q_recv.at[k], above)

    def x_copy(k):
        a, b = steps[k]
        same, before = steps.index((a, 1 - b)), steps.index(((a - 1) % tall_y, 1 - b))
        there = at_x * same + (1 - at_x) * before
        return remote(
            qhead.at[k], qahead.at[there], x_send.at[k], x_recv.at[there], (previous, slab)
        )

    def x_arrival(k):
        return remote(
            qhead.at[k], qahead.at[k], x_send.at[k], x_recv.at[k], (previous, slab)
        )

    def outer_step(k, carry):
        for c in range(2, 4):
            forward(k, c).wait_recv()

        residual(k, 0, 1)
        residual(k, pairs + 1, 0)
        for c, at in enumerate((depth + 3, 0)):
            far_copy(k, c).wait_recv()
            for part in range(2):
                rbuf[k, part, at] = wide(far_in[k, c, part])

        def ends(j, s):
            return image_terms(k, j * (pairs - 1), s)

        added(k, 6, 6, 0, 2, ends)

        def share_q(first):
            for part in range(2):
                for p in range(2):
                    edge_out[k, part, p] = narrowed(qbuf[k, part, first + p])

        @pl.when(k < lower)
        def _():
            share_q(0)
            q_copy(k, True).start()

        @pl.when(k >= lower)
        def _():
            share_q(depth - 2)
            q_copy(k, False).start()

        for part in range(2):
            for p in range(depth):
                qfirst[k, part, 2 * p : 2 * p + 2] = qbuf[k, part, p, 0:2]
                qlast[k, part, 2 * p : 2 * p + 2] = qbuf[k, part, p, block - 2 : block]
            qhead[k, part] = qfirst[k, part].astype(bf16)
        return carry

    with jax.named_scope("image"):
        lax.fori_loop(0, nodes, outer_step, 0)
        for k in range(nodes):
            x_copy(k).start()

    def energy_step(k, carry):
        @pl.when(k < lower)
        def _():
            q_copy(k, True).wait_recv()
            for part in range(2):
                for p in range(2):
                    qbuf[k, part, depth + p] = wide(edge_in[k, part, p])

        added(k, 12, 2, 0, pairs, functools.partial(energy_terms, k))
        @pl.when(k >= lower)
        def _():
            q_copy(k, False).wait_recv()
            near = [wide(edge_in[k, part, 1]) for part in range(2)]
            far = [wide(edge_in[k, part, 0]) for part in range(2)]
            zeroth = [qbuf[k, part, 0] for part in range(2)]
            first = [qbuf[k, part, 1] for part in range(2)]
            one = cmul(zeroth, [32.0 * near[part] - 2.0 * far[part] for part in range(2)])
            two = cmul(first, near)
            for part in range(2):
                acc[k * SUMS + 12 + part] += fold((one[part] - 2.0 * two[part]) * (1.0 / 24.0))

        return carry

    def cross_step(k, carry):
        x_arrival(k).wait_recv()
        last = [qlast[k, part] for part in range(2)]
        ahead = [dot(matrix("cross"), qahead[k, part]) for part in range(2)]
        crossing = cmul(last, ahead)
        for part in range(2):
            acc[k * SUMS + 12 + part] += fold(crossing[part] * (1.0 / 24.0))
        return carry

    with jax.named_scope("energy"):
        lax.fori_loop(0, nodes, energy_step, 0)
        lax.fori_loop(0, nodes, cross_step, 0)

    piece = 16 if narrow else block
    factor = []
    for k in range(nodes):
        shift, weight = shift_of(k), (notes[k, 2:3, :], notes[k, 3:4, :])
        scaled = (shift[0] - 4.0) * 0.2, shift[1] * 0.2
        factor.append((weight, scaled, cmul(weight, scaled)))

    def rows_of(p, step):
        def body(i, carry):
            rows = pl.ds(pl.multiple_of(i * piece, piece), piece)
            values = step(p, rows)
            for degree in range(2):
                for part in range(2):
                    moments[degree, 0, part, p, rows] = values[2 * degree + part]
            return carry

        lax.fori_loop(0, block // piece, body, 0)

    def start_rows(p, rows):
        values = [None] * 4
        for k in range(nodes):
            if narrow:
                x = [wbuf[k, part, p + 4, rows].astype(f32) for part in range(2)]
            else:
                x = [wide(wbuf[k, part, p + 4]) for part in range(2)]
            for degree in range(2):
                term = cmul(factor[k][2 * degree], x)
                for part in range(2):
                    at = 2 * degree + part
                    values[at] = term[part] if k == 0 else values[at] + term[part]
        return values

    def start_plane(p, carry):
        rows_of(p, start_rows)
        return carry

    with jax.named_scope("scalars"):
        lane = lax.broadcasted_iota(jnp.int32, (SUMS, 128), 1)
        shift_at = [owner_of(k) for k in range(nodes)]
        sub = lax.broadcasted_iota(jnp.int32, (SUMS, 128), 0)
        per_row = 128 // SUMS
        spread = [jnp.zeros((SUMS, 128), f32) for _ in range(sums.shape[1])]
        for k in range(nodes):
            partial = jnp.sum(acc[k * SUMS : (k + 1) * SUMS], axis=1)
            lanes = partial[:, 0:128]
            for at in range(128, length, 128):
                lanes = lanes + partial[:, at : at + 128]
            whole = jnp.sum(lanes, axis=1, keepdims=True)
            for row in range(len(spread)):
                there = (shift_at[k] - row * per_row) * SUMS + sub
                spread[row] = spread[row] + jnp.where(lane == there, whole, 0.0)
        me = node * slabs + slab
        for row, values in enumerate(spread):
            sums[me, row : row + 1] = jnp.sum(values, axis=0, keepdims=True)
        scalar_copies = []
        for a in range(nodes):
            for b in range(slabs):
                if a or b:
                    there = lax.rem(node + a, nodes), lax.rem(slab + b, slabs)
                    at = a * slabs + b
                    scalar_copies.append(
                        remote(sums.at[me], sums.at[me], s_send.at[at], s_recv.at[at], there)
                    )
        for copy in scalar_copies:
            copy.start()
        lax.fori_loop(0, depth, start_plane, 0)
        for copy in scalar_copies:
            copy.wait_recv()
        every = jnp.sum(sums[...], axis=0)
        total = jnp.zeros((SUMS, 128), f32)
        for owner in range(nodes):
            row = owner // per_row
            wide_row = jnp.broadcast_to(every[row : row + 1], (SUMS, 128))
            picked = jnp.where(lane == (owner - row * per_row) * SUMS + sub, wide_row, 0.0)
            total = total + jnp.where(lane == owner, jnp.sum(picked, axis=1, keepdims=True), 0.0)
        pair = lambda i: (total[i : i + 1], total[i + 1 : i + 2])
        s0, t0, t1, s1, s2, t2, s3 = (pair(i) for i in range(0, 14, 2))
        row_lane = lax.broadcasted_iota(jnp.int32, (8, 128), 1)
        known = jnp.zeros((8, 128), f32)
        for k in range(nodes):
            known = known + jnp.where(row_lane == shift_at[k], notes[k][:, 0:128], 0.0)
        shift = known[0:1], known[1:2]
        weight = known[2:3], known[3:4]
        step0 = cdiv(s0, s1)
        square = cmul(step0, step0)
        norm1 = cmul(square, s2)
        norm1 = norm1[0] - s0[0], norm1[1] - s0[1]
        ratio = cdiv(norm1, s0)
        grow = ratio[0] + 1.0, ratio[1]
        one = cmul(cmul(grow, grow), s1)
        two = cmul(cmul(grow, step0), s2)
        three = cmul(square, s3)
        step1 = cdiv(
            norm1, (one[0] - 2.0 * two[0] + three[0], one[1] - 2.0 * two[1] + three[1])
        )
        coef_r = cmul(step1, grow)
        coef_r = coef_r[0] + step0[0], coef_r[1] + step0[1]
        coef_q = cmul(step1, step0)
        coef_q = -coef_q[0], -coef_q[1]
        inner_r, inner_q = cmul(coef_r, t1), cmul(coef_q, t2)
        inner = t0[0] + inner_r[0] + inner_q[0], t0[1] + inner_r[1] + inner_q[1]
        share = cmul(weight, inner)
        following = cmul(weight, ((shift[0] - 4.0) * 0.2, shift[1] * 0.2))
        factors = jnp.zeros((SUMS, 128), f32)
        for i, entry in enumerate((*weight, *following, *share, *coef_r, *coef_q)):
            factors = jnp.where(sub == i, entry, factors)
        for part in range(2):
            trace[part] = jnp.sum(jnp.where((sub == 4 + part) & (lane < nodes), factors, 0.0))

    with jax.named_scope("moments"):
        scale = []
        for k in range(nodes):
            one_lane = jnp.where(lane == shift_at[k], factors, 0.0)
            values = jnp.broadcast_to(jnp.sum(one_lane, axis=1, keepdims=True), (SUMS, length))
            along_r, along_q = ((values[i : i + 1], values[i + 1 : i + 2]) for i in (6, 8))
            scale.append((cmul(factor[k][0], along_r), cmul(factor[k][0], along_q)))

        def moment_rows(p, rows):
            values = [moments[degree, 0, part, p, rows] for degree in range(2) for part in range(2)]
            for k in range(nodes):
                r = [rbuf[k, part, p + 2, rows] for part in range(2)]
                q = [qbuf[k, part, p, rows] for part in range(2)]
                along_r, along_q = cmul(scale[k][0], r), cmul(scale[k][1], q)
                field = [along_r[part] + along_q[part] for part in range(2)]
                term = cmul(factor[k][1], field)
                for part in range(2):
                    values[part] = values[part] + field[part]
                    values[2 + part] = values[2 + part] + term[part]
            return values

        def moment_plane(p, carry):
            rows_of(p, moment_rows)
            return carry

        lax.fori_loop(0, depth, moment_plane, 0)

    for copy in [*sides, *scalar_copies]:
        copy.wait_send()
    for k in range(nodes):
        if k:
            for c in range(3):
                gather_copy(k, c).wait_send()
            halo_copy(k).wait_send()
            note_copy(k).wait_send()
        for c in range(4):
            forward(k, c).wait_send()
        for c in range(2):
            forward_halo(k, c).wait_send()
            far_copy(k, c).wait_send()
        q_copy(k, k < lower).wait_send()
        x_copy(k).wait_send()


def per_device(nodes, slabs, probes, potential, warm_start, shift_points, quad_weights):
    depth, width, length = potential.shape
    block = width // nodes
    tall = up_to(block, 16)
    narrow = block % 16 == 0
    pairs = depth // 2
    f32, bf16 = jnp.float32, jnp.bfloat16
    anywhere = pl.BlockSpec(memory_space=pltpu.HBM)
    vector = pl.BlockSpec(memory_space=pltpu.VMEM)
    scalars = pl.BlockSpec(memory_space=pltpu.SMEM)
    dma = pltpu.SemaphoreType.DMA
    small = small_matrices(block, depth)
    picks = halo_picks(width, nodes)
    cpicks = picks if narrow else core_picks(width, nodes)
    return pl.pallas_call(
        functools.partial(kernel, nodes, slabs),
        out_shape=(
            pltpu.VMEM((2, 1, 2, depth, block, length), f32),
            jax.ShapeDtypeStruct((2,), f32),
        ),
        in_specs=[anywhere] * 9,
        out_specs=(vector, scalars),
        scratch_shapes=[
            pltpu.VMEM((2, depth, width, length), bf16),
            pltpu.VMEM((nodes, 2, pairs, 16, length), bf16),
            pltpu.VMEM((16, 128) if narrow else (nodes, 2, depth, tall, length), bf16),
            pltpu.VMEM((nodes, 2, depth + 8, tall, length), bf16),
            pltpu.VMEM((nodes, 2, pairs + 2, 16, length), bf16),
            pltpu.VMEM((depth + 4, block, length), f32),
            pltpu.VMEM((depth + 4, block, length), f32),
            pltpu.VMEM((2, depth, 8, length), f32),
            pltpu.VMEM((2, depth, 8, length), f32),
            pltpu.VMEM((4 * depth, length), f32),
            pltpu.VMEM((4 * depth, length), f32),
            pltpu.VMEM((nodes, 2, depth + 4, block, length), f32),
            pltpu.VMEM((nodes, 2, 4 * depth, length), f32),
            pltpu.VMEM((nodes, 2, 2, tall, length), bf16),
            pltpu.VMEM((nodes, 2, 2, tall, length), bf16),
            pltpu.VMEM((nodes, 2, depth + 2, block, length), f32),
            pltpu.VMEM((nodes, 2, 16, length), f32),
            pltpu.VMEM((nodes, 2, 16, length), f32),
            pltpu.VMEM((nodes, 2, 16, length), bf16),
            pltpu.VMEM((nodes, 2, 16, length), bf16),
            pltpu.VMEM((nodes, 2, 2, tall, length), bf16),
            pltpu.VMEM((nodes, 2, 2, tall, length), bf16),
            pltpu.VMEM((nodes * SUMS, 8, length), f32),
            pltpu.VMEM((nodes * slabs, up_to(nodes * SUMS, 128) // 128, 128), f32),
            pltpu.VMEM((nodes, 8, length), f32),
            pltpu.SMEM((1, 2), f32),
            pltpu.SMEM((1, 2), f32),
            pltpu.VMEM((length, length), bf16),
            pltpu.VMEM(small.shape, bf16),
            pltpu.VMEM(picks.shape, bf16),
            pltpu.VMEM((16, 128) if narrow else cpicks.shape, bf16),
            dma((14,)),
            dma((4,)),
            dma((4,)),
            dma((nodes, 5)),
            dma((nodes, 5)),
            dma((nodes, 8)),
            dma((nodes, 8)),
            dma((nodes,)),
            dma((nodes,)),
            dma((nodes,)),
            dma((nodes,)),
            dma((nodes * slabs,)),
            dma((nodes * slabs,)),
        ],
        compiler_params=pltpu.CompilerParams(
            collective_id=0, has_side_effects=True, vmem_limit_bytes=58 * 1024 * 1024
        ),
    )(
        warm_start,
        probes,
        potential,
        shift_points,
        quad_weights,
        jnp.asarray(ring_matrix(length, -90.0)),
        jnp.asarray(small),
        jnp.asarray(picks),
        jnp.asarray(cpicks),
    )


def solution(mesh):
    return jax.shard_map(
        functools.partial(per_device, mesh.shape["node"], mesh.shape["grid"]),
        mesh=mesh,
        in_specs=(
            P(None, "grid", None, None),
            P("grid", None, None),
            P("node", None, None, "grid", None, None),
            P("node", None),
            P("node", None),
        ),
        out_specs=(P(None, None, None, "grid", "node", None), P()),
        check_vma=False,
    )
```

```python
import functools

import jax
import jax.numpy as jnp
import ml_dtypes
import numpy as np
from jax import lax
from jax.experimental import pallas as pl
from jax.experimental.pallas import tpu as pltpu
from jax.sharding import PartitionSpec as P

MESH = pl.DeviceIdType.MESH
SUMS = 16
NEAR, FAR = 16.0, -1.0


def up_to(size, step):
    return -(-size // step) * step


def weight_of(distance):
    return {1: NEAR, 2: FAR}.get(abs(distance), 0.0)


def ring_matrix(size, diagonal):
    matrix = np.zeros((size, size), np.float32)
    at = np.arange(size)
    for step, weight in ((1, NEAR), (2, FAR)):
        matrix[at, (at + step) % size] += weight
        matrix[at, (at - step) % size] += weight
    matrix[at, at] += diagonal
    return matrix.astype(ml_dtypes.bfloat16)


def table(block, depth):
    tall = up_to(block, 16)
    pairs = depth // 2
    sizes = {
        "own": (tall, tall),
        "halo0": (tall, 16),
        "halo1": (tall, 16),
        "split0": (tall, 2 * block + 16),
        "split1": (tall, 2 * block + 16),
        "ahead": (tall, 2 * block),
        "edge_own": (16, 2 * tall),
        "edge_halo": (16 * pairs, 16 * (pairs + 2)),
        "cross": (16, 16),
    }
    at, places = 0, {}
    for name, (rows, cols) in sizes.items():
        places[name] = (at, rows, cols)
        at += rows
    return places, at, up_to(max(cols for rows, cols in sizes.values()), 128)


def small_matrices(block, depth):
    tall = up_to(block, 16)
    places, rows, cols = table(block, depth)
    whole = np.zeros((rows, cols), np.float32)
    view = {name: whole[at : at + n, :m] for name, (at, n, m) in places.items()}
    wide = [-4, -3, -2, -1, block, block + 1, block + 2, block + 3]
    slim = [-2, -1, block, block + 1]
    for i in range(block):
        for j in range(block):
            w = weight_of(i - j)
            view["own"][i, j] = w
            for s in range(2):
                view[f"split{s}"][i, j] = w
                view[f"split{s}"][i, block + j] = w
            if j > i:
                view["ahead"][i, j] = 2 * w
                view["ahead"][i, block + j] = 2 * w
        for s in range(2):
            for c, x in enumerate(wide):
                view[f"halo{s}"][i, 8 * s + c] = weight_of(i - x)
            for c, x in enumerate(slim):
                view[f"split{s}"][i, 2 * block + 4 * s + c] = weight_of(i - x)
                view[f"split{s}"][i, 2 * block + 8 + 4 * s + c] = weight_of(i - x)
    for s in range(2):
        for t, x in enumerate(slim):
            row, here = 4 * s + t, wide.index(x)
            for j in range(block):
                view["edge_own"][row, tall * s + j] = weight_of(x - j)
            for i in range(depth // 2):
                to, at = 8 * i + row, 16 * i
                for c, other in enumerate(wide):
                    view["edge_halo"][to, at + 16 + 8 * s + c] += weight_of(x - other)
                for q in range(6):
                    view["edge_halo"][to, at + 8 * q + here] += weight_of(q - 2 - s)
                view["edge_halo"][4 * depth + to, at + 16 + 8 * s + here] = 1.0
    for p in range(depth):
        for e in range(2):
            for f in range(2):
                view["cross"][2 * p + e, 2 * p + f] = 2 * weight_of(2 - e + f)
    return whole.astype(ml_dtypes.bfloat16)


def halo_picks(width, nodes):
    block = width // nodes
    picks = np.zeros((nodes * 16, 2 * width), np.float32)
    for m in range(nodes):
        for s in range(2):
            for c, x in enumerate([-4, -3, -2, -1, block, block + 1, block + 2, block + 3]):
                picks[16 * m + 8 * s + c, width * s + (block * m + x) % width] = 1.0
    return picks.astype(ml_dtypes.bfloat16)


def core_picks(width, nodes):
    block = width // nodes
    tall = up_to(block, 16)
    picks = np.zeros((nodes * tall, width), np.float32)
    for m in range(nodes):
        for i in range(block):
            picks[tall * m + i, block * m + i] = 1.0
    return picks.astype(ml_dtypes.bfloat16)


def offsets(nodes):
    every = [(a, b) for a in range(nodes // 2) for b in range(2)]
    return [(0, 0)] + sorted(every[1:], key=lambda at: -(at[0] > 0) - (at[1] > 0))


def cmul(a, b):
    return a[0] * b[0] - a[1] * b[1], a[0] * b[1] + a[1] * b[0]


def cdiv(a, b):
    size = b[0] * b[0] + b[1] * b[1]
    return (a[0] * b[0] + a[1] * b[1]) / size, (a[1] * b[0] - a[0] * b[1]) / size


def fold(values):
    rows, cols = values.shape
    return jnp.sum(values.reshape(rows // 8, 8, cols), axis=0)


def dot(a, b):
    return jnp.dot(a, b, preferred_element_type=jnp.float32)


def kernel(
    nodes,
    slabs,
    warm,
    probes,
    potential,
    shift_hbm,
    weight_hbm,
    along_y_hbm,
    small_hbm,
    picks_hbm,
    core_hbm,
    moments,
    rbuf,
    qbuf,
    scale_out,
    table_out,
    own,
    hsend,
    csend,
    wbuf,
    halo,
    bbuf,
    vbuf,
    bside,
    vside,
    bedge,
    vedge,
    redge,
    far_out,
    far_in,
    qfirst,
    qlast,
    qhead,
    qahead,
    edge_out,
    edge_in,
    acc,
    sums,
    notes,
    shift_ref,
    weight_ref,
    along_y,
    small,
    picks,
    cpicks,
    local_sem,
    b_send,
    b_recv,
    a_send,
    a_recv,
    z_send,
    z_recv,
    q_send,
    q_recv,
    x_send,
    x_recv,
    s_send,
    s_recv,
):
    f32, bf16 = jnp.float32, jnp.bfloat16
    node, slab = lax.axis_index("node"), lax.axis_index("grid")
    depth, width, length = own.shape[1:]
    pairs = depth // 2
    block = width // nodes
    tall = up_to(block, 16)
    narrow = block % 16 == 0
    lower = nodes // 2
    places = table(block, depth)[0]
    above = (node, lax.rem(slab + 1, slabs))
    below = (node, lax.rem(slab + slabs - 1, slabs))
    step = 16 if narrow else 8
    mine = pl.ds(pl.multiple_of(node * block, step), block)
    left = pl.ds(pl.multiple_of(lax.rem(node * block + width - 8, width), 8), 8)
    right = pl.ds(pl.multiple_of(lax.rem(node * block + block, width), 8), 8)

    def matrix(name):
        at, rows, cols = places[name]
        return small[at : at + rows, 0:cols]

    loads = []

    def load(source, target):
        copy = pltpu.make_async_copy(source, target, local_sem.at[len(loads)])
        copy.start()
        loads.append(copy)

    load(shift_hbm, shift_ref)
    load(weight_hbm, weight_ref)
    load(warm.at[0, 0], own)
    load(picks_hbm, picks)
    if not narrow:
        load(core_hbm, cpicks)
    first_loads = len(loads)
    load(along_y_hbm, along_y)
    load(small_hbm, small)
    load(probes.at[0, :, mine], bbuf.at[2 : depth + 2])
    load(potential.at[:, mine], vbuf.at[2 : depth + 2])
    load(probes.at[0, :, left], bside.at[0])
    load(probes.at[0, :, right], bside.at[1])
    load(potential.at[:, left], vside.at[0])
    load(potential.at[:, right], vside.at[1])
    if narrow:
        load(warm.at[0, 0, :, :, mine], wbuf.at[0, :, 4 : depth + 4])

    barrier = pltpu.get_barrier_semaphore()
    for k in range(1, slabs):
        pl.semaphore_signal(
            barrier, inc=1, device_id=(node, lax.rem(slab + k, slabs)), device_id_type=MESH
        )
    for k in range(1, nodes):
        pl.semaphore_signal(
            barrier, inc=1, device_id=(lax.rem(node + k, nodes), slab), device_id_type=MESH
        )
    pl.semaphore_wait(barrier, slabs + nodes - 2)

    def remote(source, target, send_sem, recv_sem, device):
        return pltpu.make_async_remote_copy(
            src_ref=source,
            dst_ref=target,
            send_sem=send_sem,
            recv_sem=recv_sem,
            device_id=device,
            device_id_type=MESH,
        )

    steps = offsets(nodes)
    distant = sum(1 for a, b in steps if a and b)
    tall_y = nodes // 2
    at_y, at_x = node // 2, lax.rem(node, 2)

    def peer(k):
        a, b = steps[k]
        return lax.rem(at_y + a, tall_y) * 2 + lax.rem(at_x + b, 2)

    def owner_of(k):
        a, b = steps[k]
        return lax.rem(at_y + tall_y - a, tall_y) * 2 + lax.rem(at_x + b, 2)

    def core(m, first, last):
        if narrow:
            rows = pl.ds(pl.multiple_of(m * block, step), block)
            return warm.at[0, 0, :, first:last, rows]
        return csend.at[m, :, first:last]

    chunks = ((0, 2), (depth - 2, depth), (2, depth - 2))

    def gather_copy(k, c):
        first, last = chunks[c]
        return remote(
            core(peer(k), first, last),
            wbuf.at[k, :, 4 + first : 4 + last],
            a_send.at[k, c],
            a_recv.at[k, c],
            (peer(k), slab),
        )

    def halo_copy(k):
        return remote(
            hsend.at[peer(k)],
            halo.at[k, :, 1 : pairs + 1],
            a_send.at[k, 3],
            a_recv.at[k, 3],
            (peer(k), slab),
        )

    def note_copy(k):
        return remote(notes.at[0], notes.at[k], a_send.at[k, 4], a_recv.at[k, 4], (peer(k), slab))

    top = depth + 4
    routes = (
        ((4, 6), (top, top + 2), below),
        ((top - 2, top), (2, 4), above),
        ((6, 7), (top + 2, top + 3), below),
        ((top - 3, top - 2), (1, 2), above),
    )

    def forward(k, c):
        source, target, device = routes[c]
        if isinstance(k, int) and k == 0:
            part = core(node, source[0] - 4, source[1] - 4)
        else:
            part = wbuf.at[k, :, source[0] : source[1]]
        return remote(
            part, wbuf.at[k, :, target[0] : target[1]], z_send.at[k, c], z_recv.at[k, c], device
        )

    def forward_halo(k, c):
        source, target, device = ((1, pairs + 1, below), (pairs, 0, above))[c]
        return remote(
            halo.at[k, :, source],
            halo.at[k, :, target],
            z_send.at[k, 4 + c],
            z_recv.at[k, 4 + c],
            device,
        )

    sides = []
    for at, (source, target) in enumerate(((probes.at[0], bbuf), (potential, vbuf))):
        for c, (first, there, device) in enumerate(
            ((0, depth + 2, below), (depth - 1, 1, above))
        ):
            sides.append(
                remote(
                    source.at[first : first + 1, mine],
                    target.at[there : there + 1],
                    b_send.at[2 * at + c],
                    b_recv.at[2 * at + c],
                    device,
                )
            )

    def far_copy(k, c):
        return remote(
            far_out.at[k, c], far_in.at[k, c], z_send.at[k, 6 + c], z_recv.at[k, 6 + c], routes[c][2]
        )

    order = [(k, c) for c in range(3) for k in range(1, nodes)]

    def pick():
        for copy in loads[2:first_loads]:
            copy.wait()
        for i in range(pairs):
            for part in range(2):
                rows = own[part, 2 * i : 2 * i + 2].reshape(2 * width, length)
                picked = dot(picks[...], rows).astype(bf16)
                for m in range(nodes):
                    hsend[m, part, i] = picked[16 * m : 16 * m + 16]
        if not narrow:
            for part in range(2):
                for p in range(depth):
                    picked = dot(cpicks[...], own[part, p]).astype(bf16)
                    for m in range(nodes):
                        csend[m, part, p] = picked[tall * m : tall * m + tall]

    def send_cores():
        for k, c in order:
            if c < 2 or not narrow:
                gather_copy(k, c).start()
        for c in range(4):
            forward(0, c).start()
        for copy in sides:
            copy.start()

    if narrow:
        send_cores()
    for copy in loads[0:2]:
        copy.wait()
    row = lax.broadcasted_iota(jnp.int32, (8, length), 0)
    note = jnp.zeros((8, length), f32)
    entries = (shift_ref[0, 0], shift_ref[0, 1], weight_ref[0, 0], weight_ref[0, 1])
    for i, entry in enumerate(entries):
        note = jnp.where(row == i, entry, note)
    notes[0] = note
    for k in range(1, nodes):
        note_copy(k).start()
    pick()
    if not narrow:
        send_cores()
    for k in range(1, nodes):
        halo_copy(k).start()
    if narrow:
        for k, c in order:
            if c == 2:
                gather_copy(k, c).start()
    for part in range(2):
        for i in range(pairs):
            halo[0, part, 1 + i] = hsend[node, part, i]
    for c in range(2):
        forward_halo(0, c).start()
    if not narrow:
        for part in range(2):
            for p in range(depth):
                wbuf[0, part, 4 + p] = csend[node, part, p]

    acc[...] = jnp.zeros_like(acc)
    qfirst[...] = jnp.zeros_like(qfirst)
    qlast[...] = jnp.zeros_like(qlast)
    qbuf[lower:nodes, :, depth : depth + 2] = jnp.zeros((nodes - lower, 2, 2, block, length), f32)
    for copy in loads[first_loads:]:
        copy.wait()
    for i in range(pairs):
        for s in range(2):
            for side in range(2):
                there = 8 * i + 4 * s + 2 * side
                here = 6 if side == 0 else 0
                bedge[there : there + 2] = bside[side, 2 * i + s, here : here + 2]
                vedge[there : there + 2] = vside[side, 2 * i + s, here : here + 2]

    def shift_of(k):
        return notes[k, 0:1, :], notes[k, 1:2, :]

    def apply(shift, field, stencil, local):
        diagonal = shift[0] - local
        return (
            diagonal * field[0] - shift[1] * field[1] + stencil[0] * (1.0 / 24.0),
            diagonal * field[1] + shift[1] * field[0] + stencil[1] * (1.0 / 24.0),
        )

    def added(k, first, count, low, high, terms):
        def body(i, carry):
            for s in range(2):
                carry = tuple(c + fold(v) for c, v in zip(carry, terms(i, s)))
            return carry

        zero = jnp.zeros((8, length), f32)
        for i, total in enumerate(lax.fori_loop(low, high, body, (zero,) * count)):
            acc[k * SUMS + first + i] += total

    def wide(values):
        return values.astype(f32)[0:block]

    def residual(k, i, s):
        pp = 2 * i + s
        stencil, field = [], []
        for part in range(2):
            centre = wbuf[k, part, pp + 2]
            plane = (
                dot(centre, along_y[...])
                + dot(matrix("own"), centre)
                + dot(matrix(f"halo{s}"), halo[k, part, i])
            )[0:block]
            at = [wide(wbuf[k, part, pp + j]) for j in (0, 1, 3, 4)]
            stencil.append(plane + 16.0 * (at[1] + at[2]) - (at[0] + at[3]))
            field.append(wide(centre))
        source = bbuf[pp]
        image = apply(shift_of(k), field, stencil, vbuf[pp])
        r = source - image[0], -image[1]
        rbuf[k, 0, pp] = r[0]
        rbuf[k, 1, pp] = r[1]
        return source, field, r

    def residual_terms(k, i, s):
        source, field, r = residual(k, i, s)
        return (
            r[0] * r[0] - r[1] * r[1],
            2.0 * r[0] * r[1],
            source * field[0],
            source * field[1],
            source * r[0],
            source * r[1],
        )

    def edge_rows(k):
        stencil, field = [], []
        for part in range(2):
            around = halo[k, part].reshape(16 * (pairs + 2), length)
            both = dot(matrix("edge_halo"), around)
            plane = dot(both.astype(bf16), along_y[...])
            beside = [
                dot(matrix("edge_own"), wbuf[k, part, 4 + 2 * i : 6 + 2 * i].reshape(2 * tall, length))
                for i in range(pairs)
            ]
            beside = jnp.concatenate([rows[0:8] for rows in beside], axis=0)
            stencil.append(beside + both[0 : 4 * depth] + plane[4 * depth :])
            field.append(both[4 * depth :])
        image = apply(shift_of(k), field, stencil, vedge[...])
        redge[k, 0] = bedge[...] - image[0]
        redge[k, 1] = -image[1]

    def split(values):
        high = values.astype(bf16)
        return high, (values - high.astype(f32)).astype(bf16)

    def pack(values):
        high, low = split(values)
        if narrow:
            return jnp.concatenate([high, low], axis=0)
        return jnp.concatenate([high.astype(f32), low.astype(f32)], axis=0).astype(bf16)

    def slim(values):
        high, low = split(values)
        return jnp.concatenate([high.astype(f32), low.astype(f32)], axis=0).astype(bf16)

    def along(packed):
        both = dot(packed, along_y[...])
        return both[0:block] + both[block : 2 * block]

    def image_terms(k, i, s):
        p = 2 * i + s
        stencil, field = [], []
        for part in range(2):
            at = [rbuf[k, part, p + j] for j in range(5)]
            packed = pack(at[2])
            side = jnp.concatenate([packed, slim(redge[k, part, pl.ds(pl.multiple_of(8 * i, 8), 8)])], axis=0)
            plane = along(packed) + dot(matrix(f"split{s}"), side)[0:block]
            stencil.append(plane + 16.0 * (at[1] + at[3]) - (at[0] + at[4]))
            field.append(at[2])
        source = bbuf[p + 2]
        q = apply(shift_of(k), field, stencil, vbuf[p + 2])
        qbuf[k, 0, p] = q[0]
        qbuf[k, 1, p] = q[1]
        return (
            *cmul(field, q),
            q[0] * q[0] - q[1] * q[1],
            2.0 * q[0] * q[1],
            source * q[0],
            source * q[1],
        )

    def energy_terms(k, i, s):
        p = 2 * i + s
        stencil, field = [], []
        for part in range(2):
            at = [qbuf[k, part, p + j] for j in range(3)]
            packed = pack(at[0])
            plane = along(packed) + dot(matrix("ahead"), packed)[0:block]
            stencil.append(plane + 32.0 * at[1] - 2.0 * at[2])
            field.append(at[0])
        return cmul(field, apply(shift_of(k), field, stencil, vbuf[p + 2]))

    def narrowed(values):
        if not narrow:
            filler = jnp.zeros((tall - block, length), f32)
            values = jnp.concatenate([values, filler], axis=0)
        return values.astype(bf16)

    def own_step(k, carry):
        @pl.when(k == 1)
        def _():
            for at, (j, c) in enumerate(order):
                if at == 2 * (nodes - 1):
                    for m in range(1, nodes):
                        note_copy(m).wait_recv()
                        halo_copy(m).wait_recv()
                        for d in range(2):
                            forward_halo(m, d).start()
                gather_copy(j, c).wait_recv()
                for d in (c,) if c < 2 else (2, 3):
                    forward(j, d).start()

        for c in range(2):
            forward(k, c).wait_recv()
            forward_halo(k, c).wait_recv()
        added(k, 0, 6, 1, pairs + 1, functools.partial(residual_terms, k))

        for c, at in enumerate((3, depth)):
            for part in range(2):
                far_out[k, c, part] = narrowed(rbuf[k, part, at])
            far_copy(k, c).start()
        return carry

    def inner_step(k, carry):
        edge_rows(k)
        added(k, 6, 6, 1, pairs - 1, functools.partial(image_terms, k))
        return carry

    with jax.named_scope("residual"):
        lax.fori_loop(0, nodes, own_step, 0)
        lax.fori_loop(0, nodes, inner_step, 0)

    for copy in sides:
        copy.wait_recv()

    previous = lax.rem(node + nodes - 1, nodes)

    def q_copy(k, down):
        if down:
            return remote(
                edge_out.at[k], edge_in.at[k], q_send.at[k], q_recv.at[k], below
            )
        return remote(edge_out.at[k], edge_in.at[k], q_send.at[k], q_recv.at[k], above)

    def x_copy(k):
        a, b = steps[k]
        same, before = steps.index((a, 1 - b)), steps.index(((a - 1) % tall_y, 1 - b))
        there = at_x * same + (1 - at_x) * before
        return remote(
            qhead.at[k], qahead.at[there], x_send.at[k], x_recv.at[there], (previous, slab)
        )

    def x_arrival(k):
        return remote(
            qhead.at[k], qahead.at[k], x_send.at[k], x_recv.at[k], (previous, slab)
        )

    def outer_step(k, carry):
        for c in range(2, 4):
            forward(k, c).wait_recv()

        residual(k, 0, 1)
        residual(k, pairs + 1, 0)
        for c, at in enumerate((depth + 3, 0)):
            far_copy(k, c).wait_recv()
            for part in range(2):
                rbuf[k, part, at] = wide(far_in[k, c, part])

        def ends(j, s):
            return image_terms(k, j * (pairs - 1), s)

        added(k, 6, 6, 0, 2, ends)

        def share_q(first):
            for part in range(2):
                for p in range(2):
                    edge_out[k, part, p] = narrowed(qbuf[k, part, first + p])

        @pl.when(k < lower)
        def _():
            share_q(0)
            q_copy(k, True).start()

        @pl.when(k >= lower)
        def _():
            share_q(depth - 2)
            q_copy(k, False).start()

        for part in range(2):
            for p in range(depth):
                qfirst[k, part, 2 * p : 2 * p + 2] = qbuf[k, part, p, 0:2]
                qlast[k, part, 2 * p : 2 * p + 2] = qbuf[k, part, p, block - 2 : block]
            qhead[k, part] = qfirst[k, part].astype(bf16)
        for j in range(nodes):
            @pl.when(k == j)
            def _():
                x_copy(j).start()
        return carry

    with jax.named_scope("image"):
        lax.fori_loop(0, nodes, outer_step, 0)

    def energy_step(k, carry):
        @pl.when(k < lower)
        def _():
            q_copy(k, True).wait_recv()
            for part in range(2):
                for p in range(2):
                    qbuf[k, part, depth + p] = wide(edge_in[k, part, p])

        added(k, 12, 2, 0, pairs, functools.partial(energy_terms, k))
        @pl.when(k >= lower)
        def _():
            q_copy(k, False).wait_recv()
            near = [wide(edge_in[k, part, 1]) for part in range(2)]
            far = [wide(edge_in[k, part, 0]) for part in range(2)]
            zeroth = [qbuf[k, part, 0] for part in range(2)]
            first = [qbuf[k, part, 1] for part in range(2)]
            one = cmul(zeroth, [32.0 * near[part] - 2.0 * far[part] for part in range(2)])
            two = cmul(first, near)
            for part in range(2):
                acc[k * SUMS + 12 + part] += fold((one[part] - 2.0 * two[part]) * (1.0 / 24.0))

        return carry

    def cross_step(k, carry):
        x_arrival(k).wait_recv()
        last = [qlast[k, part] for part in range(2)]
        ahead = [dot(matrix("cross"), qahead[k, part]) for part in range(2)]
        crossing = cmul(last, ahead)
        for part in range(2):
            acc[k * SUMS + 12 + part] += fold(crossing[part] * (1.0 / 24.0))
        return carry

    with jax.named_scope("energy"):
        lax.fori_loop(0, nodes, energy_step, 0)
        lax.fori_loop(0, nodes, cross_step, 0)

    piece = 16 if narrow else block
    factor = []
    for k in range(nodes):
        shift, weight = shift_of(k), (notes[k, 2:3, :], notes[k, 3:4, :])
        scaled = (shift[0] - 4.0) * 0.2, shift[1] * 0.2
        factor.append((weight, scaled, cmul(weight, scaled)))

    def rows_of(p, step):
        def body(i, carry):
            rows = pl.ds(pl.multiple_of(i * piece, piece), piece)
            values = step(p, rows)
            for degree in range(2):
                for part in range(2):
                    moments[degree, 0, part, p, rows] = values[2 * degree + part]
            return carry

        lax.fori_loop(0, block // piece, body, 0)

    def start_rows(p, rows):
        values = [None] * 4
        for k in range(nodes):
            if narrow:
                x = [wbuf[k, part, p + 4, rows].astype(f32) for part in range(2)]
            else:
                x = [wide(wbuf[k, part, p + 4]) for part in range(2)]
            for degree in range(2):
                term = cmul(factor[k][2 * degree], x)
                for part in range(2):
                    at = 2 * degree + part
                    values[at] = term[part] if k == 0 else values[at] + term[part]
        return values

    def start_plane(p, carry):
        rows_of(p, start_rows)
        return carry

    with jax.named_scope("scalars"):
        lane = lax.broadcasted_iota(jnp.int32, (SUMS, 128), 1)
        shift_at = [owner_of(k) for k in range(nodes)]
        sub = lax.broadcasted_iota(jnp.int32, (SUMS, 128), 0)
        per_row = 128 // SUMS
        spread = [jnp.zeros((SUMS, 128), f32) for _ in range(sums.shape[1])]
        for k in range(nodes):
            partial = jnp.sum(acc[k * SUMS : (k + 1) * SUMS], axis=1)
            lanes = partial[:, 0:128]
            for at in range(128, length, 128):
                lanes = lanes + partial[:, at : at + 128]
            whole = jnp.sum(lanes, axis=1, keepdims=True)
            for row in range(len(spread)):
                there = (shift_at[k] - row * per_row) * SUMS + sub
                spread[row] = spread[row] + jnp.where(lane == there, whole, 0.0)
        me = node * slabs + slab
        for row, values in enumerate(spread):
            sums[me, row : row + 1] = jnp.sum(values, axis=0, keepdims=True)
        scalar_copies = []
        for a in range(nodes):
            for b in range(slabs):
                if a or b:
                    there = lax.rem(node + a, nodes), lax.rem(slab + b, slabs)
                    at = a * slabs + b
                    scalar_copies.append(
                        remote(sums.at[me], sums.at[me], s_send.at[at], s_recv.at[at], there)
                    )
        for copy in scalar_copies:
            copy.start()
        lax.fori_loop(0, depth, start_plane, 0)
        for copy in scalar_copies:
            copy.wait_recv()
        every = jnp.sum(sums[...], axis=0)
        total = jnp.zeros((SUMS, 128), f32)
        for owner in range(nodes):
            row = owner // per_row
            wide_row = jnp.broadcast_to(every[row : row + 1], (SUMS, 128))
            picked = jnp.where(lane == (owner - row * per_row) * SUMS + sub, wide_row, 0.0)
            total = total + jnp.where(lane == owner, jnp.sum(picked, axis=1, keepdims=True), 0.0)
        pair = lambda i: (total[i : i + 1], total[i + 1 : i + 2])
        s0, t0, t1, s1, s2, t2, s3 = (pair(i) for i in range(0, 14, 2))
        row_lane = lax.broadcasted_iota(jnp.int32, (8, 128), 1)
        known = jnp.zeros((8, 128), f32)
        for k in range(nodes):
            known = known + jnp.where(row_lane == shift_at[k], notes[k][:, 0:128], 0.0)
        shift = known[0:1], known[1:2]
        weight = known[2:3], known[3:4]
        step0 = cdiv(s0, s1)
        square = cmul(step0, step0)
        norm1 = cmul(square, s2)
        norm1 = norm1[0] - s0[0], norm1[1] - s0[1]
        ratio = cdiv(norm1, s0)
        grow = ratio[0] + 1.0, ratio[1]
        one = cmul(cmul(grow, grow), s1)
        two = cmul(cmul(grow, step0), s2)
        three = cmul(square, s3)
        step1 = cdiv(
            norm1, (one[0] - 2.0 * two[0] + three[0], one[1] - 2.0 * two[1] + three[1])
        )
        coef_r = cmul(step1, grow)
        coef_r = coef_r[0] + step0[0], coef_r[1] + step0[1]
        coef_q = cmul(step1, step0)
        coef_q = -coef_q[0], -coef_q[1]
        inner_r, inner_q = cmul(coef_r, t1), cmul(coef_q, t2)
        inner = t0[0] + inner_r[0] + inner_q[0], t0[1] + inner_r[1] + inner_q[1]
        share = cmul(weight, inner)
        following = cmul(weight, ((shift[0] - 4.0) * 0.2, shift[1] * 0.2))
        factors = jnp.zeros((SUMS, 128), f32)
        for i, entry in enumerate((*weight, *following, *share, *coef_r, *coef_q)):
            factors = jnp.where(sub == i, entry, factors)
        table_out[...] = factors
        for k in range(nodes):
            one_lane = jnp.where(lane == shift_at[k], factors, 0.0)
            values = jnp.broadcast_to(jnp.sum(one_lane, axis=1, keepdims=True), (SUMS, length))
            along_r, along_q = ((values[i : i + 1], values[i + 1 : i + 2]) for i in (6, 8))
            entries = (*factor[k][1], *cmul(factor[k][0], along_r), *cmul(factor[k][0], along_q))
            for i, entry in enumerate(entries):
                scale_out[k, i : i + 1] = entry

    for copy in [*sides, *scalar_copies]:
        copy.wait_send()
    for k in range(nodes):
        if k:
            for c in range(3):
                gather_copy(k, c).wait_send()
            halo_copy(k).wait_send()
            note_copy(k).wait_send()
        for c in range(4):
            forward(k, c).wait_send()
        for c in range(2):
            forward_halo(k, c).wait_send()
            far_copy(k, c).wait_send()
        q_copy(k, k < lower).wait_send()
        x_copy(k).wait_send()


def finish(nodes, started, rbuf, qbuf, scales, factors, moments, trace, result, pair, sems):
    depth, block, length = result.shape[2:]
    piece = 16 if block % 16 == 0 else block
    scale = []
    for k in range(nodes):
        rows = [scales[k, i : i + 1, :] for i in range(6)]
        scale.append((rows[0:2], rows[2:4], rows[4:6]))

    def copy(p):
        return pltpu.make_async_copy(result.at[:, :, p], moments.at[:, 0, :, p], sems.at[p])

    def plane(p, carry):
        def body(i, inner):
            rows = pl.ds(pl.multiple_of(i * piece, piece), piece)
            values = [started[degree, 0, part, p, rows] for degree in range(2) for part in range(2)]
            for k in range(nodes):
                r = [rbuf[k, part, p + 2, rows] for part in range(2)]
                q = [qbuf[k, part, p, rows] for part in range(2)]
                along_r, along_q = cmul(scale[k][1], r), cmul(scale[k][2], q)
                field = [along_r[part] + along_q[part] for part in range(2)]
                term = cmul(scale[k][0], field)
                for part in range(2):
                    values[part] = values[part] + field[part]
                    values[2 + part] = values[2 + part] + term[part]
            for degree in range(2):
                for part in range(2):
                    result[degree, part, p, rows] = values[2 * degree + part]
            return inner

        lax.fori_loop(0, block // piece, body, 0)
        copy(p).start()
        return carry

    values = factors[...]
    sub = lax.broadcasted_iota(jnp.int32, values.shape, 0)
    lane = lax.broadcasted_iota(jnp.int32, values.shape, 1)
    for part in range(2):
        pair[part] = jnp.sum(jnp.where((sub == 4 + part) & (lane < nodes), values, 0.0))
    trace_copy = pltpu.make_async_copy(pair, trace, sems.at[depth])
    trace_copy.start()
    lax.fori_loop(0, depth, plane, 0)
    for p in range(depth):
        copy(p).wait()
    trace_copy.wait()


def per_device(nodes, slabs, probes, potential, warm_start, shift_points, quad_weights):
    depth, width, length = potential.shape
    block = width // nodes
    tall = up_to(block, 16)
    narrow = block % 16 == 0
    pairs = depth // 2
    f32, bf16 = jnp.float32, jnp.bfloat16
    anywhere = pl.BlockSpec(memory_space=pltpu.HBM)
    vector = pl.BlockSpec(memory_space=pltpu.VMEM)
    dma = pltpu.SemaphoreType.DMA
    small = small_matrices(block, depth)
    picks = halo_picks(width, nodes)
    cpicks = picks if narrow else core_picks(width, nodes)
    results = pl.pallas_call(
        functools.partial(kernel, nodes, slabs),
        out_shape=(
            pltpu.VMEM((2, 1, 2, depth, block, length), f32),
            pltpu.VMEM((nodes, 2, depth + 4, block, length), f32),
            pltpu.VMEM((nodes, 2, depth + 2, block, length), f32),
            pltpu.VMEM((nodes, 8, length), f32),
            pltpu.VMEM((SUMS, 128), f32),
        ),
        in_specs=[anywhere] * 9,
        out_specs=(vector,) * 5,
        scratch_shapes=[
            pltpu.VMEM((2, depth, width, length), bf16),
            pltpu.VMEM((nodes, 2, pairs, 16, length), bf16),
            pltpu.VMEM((16, 128) if narrow else (nodes, 2, depth, tall, length), bf16),
            pltpu.VMEM((nodes, 2, depth + 8, tall, length), bf16),
            pltpu.VMEM((nodes, 2, pairs + 2, 16, length), bf16),
            pltpu.VMEM((depth + 4, block, length), f32),
            pltpu.VMEM((depth + 4, block, length), f32),
            pltpu.VMEM((2, depth, 8, length), f32),
            pltpu.VMEM((2, depth, 8, length), f32),
            pltpu.VMEM((4 * depth, length), f32),
            pltpu.VMEM((4 * depth, length), f32),
            pltpu.VMEM((nodes, 2, 4 * depth, length), f32),
            pltpu.VMEM((nodes, 2, 2, tall, length), bf16),
            pltpu.VMEM((nodes, 2, 2, tall, length), bf16),
            pltpu.VMEM((nodes, 2, 16, length), f32),
            pltpu.VMEM((nodes, 2, 16, length), f32),
            pltpu.VMEM((nodes, 2, 16, length), bf16),
            pltpu.VMEM((nodes, 2, 16, length), bf16),
            pltpu.VMEM((nodes, 2, 2, tall, length), bf16),
            pltpu.VMEM((nodes, 2, 2, tall, length), bf16),
            pltpu.VMEM((nodes * SUMS, 8, length), f32),
            pltpu.VMEM((nodes * slabs, up_to(nodes * SUMS, 128) // 128, 128), f32),
            pltpu.VMEM((nodes, 8, length), f32),
            pltpu.SMEM((1, 2), f32),
            pltpu.SMEM((1, 2), f32),
            pltpu.VMEM((length, length), bf16),
            pltpu.VMEM(small.shape, bf16),
            pltpu.VMEM(picks.shape, bf16),
            pltpu.VMEM((16, 128) if narrow else cpicks.shape, bf16),
            dma((14,)),
            dma((4,)),
            dma((4,)),
            dma((nodes, 5)),
            dma((nodes, 5)),
            dma((nodes, 8)),
            dma((nodes, 8)),
            dma((nodes,)),
            dma((nodes,)),
            dma((nodes,)),
            dma((nodes,)),
            dma((nodes * slabs,)),
            dma((nodes * slabs,)),
        ],
        compiler_params=pltpu.CompilerParams(
            collective_id=0, has_side_effects=True, vmem_limit_bytes=48 * 1024 * 1024
        ),
    )(
        warm_start,
        probes,
        potential,
        shift_points,
        quad_weights,
        jnp.asarray(ring_matrix(length, -90.0)),
        jnp.asarray(small),
        jnp.asarray(picks),
        jnp.asarray(cpicks),
    )
    return pl.pallas_call(
        functools.partial(finish, nodes),
        out_shape=(
            jax.ShapeDtypeStruct((2, 1, 2, depth, block, length), f32),
            jax.ShapeDtypeStruct((2,), f32),
        ),
        in_specs=[vector] * 5,
        out_specs=(anywhere, anywhere),
        scratch_shapes=[
            pltpu.VMEM((2, 2, depth, block, length), f32),
            pltpu.SMEM((2,), f32),
            dma((depth + 1,)),
        ],
        compiler_params=pltpu.CompilerParams(vmem_limit_bytes=4 * 1024 * 1024),
    )(*results)


def solution(mesh):
    return jax.shard_map(
        functools.partial(per_device, mesh.shape["node"], mesh.shape["grid"]),
        mesh=mesh,
        in_specs=(
            P(None, "grid", None, None),
            P("grid", None, None),
            P("node", None, None, "grid", None, None),
            P("node", None),
            P("node", None),
        ),
        out_specs=(P(None, None, None, "grid", "node", None), P()),
        check_vma=False,
    )
```

```python
import functools

import jax
import jax.numpy as jnp
import ml_dtypes
import numpy as np
from jax import lax
from jax.experimental import pallas as pl
from jax.experimental.pallas import tpu as pltpu
from jax.sharding import PartitionSpec as P

MESH = pl.DeviceIdType.MESH
SUMS = 16
NEAR, FAR = 16.0, -1.0


def up_to(size, step):
    return -(-size // step) * step


def weight_of(distance):
    return {1: NEAR, 2: FAR}.get(abs(distance), 0.0)


def ring_matrix(size, diagonal):
    matrix = np.zeros((size, size), np.float32)
    at = np.arange(size)
    for step, weight in ((1, NEAR), (2, FAR)):
        matrix[at, (at + step) % size] += weight
        matrix[at, (at - step) % size] += weight
    matrix[at, at] += diagonal
    return matrix.astype(ml_dtypes.bfloat16)


def table(block, depth):
    tall = up_to(block, 16)
    pairs = depth // 2
    sizes = {
        "own": (tall, tall),
        "halo0": (tall, 16),
        "halo1": (tall, 16),
        "split0": (tall, 2 * block + 16),
        "split1": (tall, 2 * block + 16),
        "ahead": (tall, 2 * block),
        "edge_own": (16, 2 * tall),
        "edge_halo": (16 * pairs, 16 * (pairs + 2)),
        "cross": (16, 16),
    }
    at, places = 0, {}
    for name, (rows, cols) in sizes.items():
        places[name] = (at, rows, cols)
        at += rows
    return places, at, up_to(max(cols for rows, cols in sizes.values()), 128)


def small_matrices(block, depth):
    tall = up_to(block, 16)
    places, rows, cols = table(block, depth)
    whole = np.zeros((rows, cols), np.float32)
    view = {name: whole[at : at + n, :m] for name, (at, n, m) in places.items()}
    wide = [-4, -3, -2, -1, block, block + 1, block + 2, block + 3]
    slim = [-2, -1, block, block + 1]
    for i in range(block):
        for j in range(block):
            w = weight_of(i - j)
            view["own"][i, j] = w
            for s in range(2):
                view[f"split{s}"][i, j] = w
                view[f"split{s}"][i, block + j] = w
            if j > i:
                view["ahead"][i, j] = 2 * w
                view["ahead"][i, block + j] = 2 * w
        for s in range(2):
            for c, x in enumerate(wide):
                view[f"halo{s}"][i, 8 * s + c] = weight_of(i - x)
            for c, x in enumerate(slim):
                view[f"split{s}"][i, 2 * block + 4 * s + c] = weight_of(i - x)
                view[f"split{s}"][i, 2 * block + 8 + 4 * s + c] = weight_of(i - x)
    for s in range(2):
        for t, x in enumerate(slim):
            row, here = 4 * s + t, wide.index(x)
            for j in range(block):
                view["edge_own"][row, tall * s + j] = weight_of(x - j)
            for i in range(depth // 2):
                to, at = 8 * i + row, 16 * i
                for c, other in enumerate(wide):
                    view["edge_halo"][to, at + 16 + 8 * s + c] += weight_of(x - other)
                for q in range(6):
                    view["edge_halo"][to, at + 8 * q + here] += weight_of(q - 2 - s)
                view["edge_halo"][4 * depth + to, at + 16 + 8 * s + here] = 1.0
    for p in range(depth):
        for e in range(2):
            for f in range(2):
                view["cross"][2 * p + e, 2 * p + f] = 2 * weight_of(2 - e + f)
    return whole.astype(ml_dtypes.bfloat16)


def halo_picks(width, nodes):
    block = width // nodes
    picks = np.zeros((nodes * 16, 2 * width), np.float32)
    for m in range(nodes):
        for s in range(2):
            for c, x in enumerate([-4, -3, -2, -1, block, block + 1, block + 2, block + 3]):
                picks[16 * m + 8 * s + c, width * s + (block * m + x) % width] = 1.0
    return picks.astype(ml_dtypes.bfloat16)


def core_picks(width, nodes):
    block = width // nodes
    tall = up_to(block, 16)
    picks = np.zeros((nodes * tall, width), np.float32)
    for m in range(nodes):
        for i in range(block):
            picks[tall * m + i, block * m + i] = 1.0
    return picks.astype(ml_dtypes.bfloat16)


def offsets(nodes):
    every = [(a, b) for a in range(nodes // 2) for b in range(2)]
    return [(0, 0)] + sorted(every[1:], key=lambda at: -(at[0] > 0) - (at[1] > 0))


def cmul(a, b):
    return a[0] * b[0] - a[1] * b[1], a[0] * b[1] + a[1] * b[0]


def cdiv(a, b):
    size = b[0] * b[0] + b[1] * b[1]
    return (a[0] * b[0] + a[1] * b[1]) / size, (a[1] * b[0] - a[0] * b[1]) / size


def fold(values):
    rows, cols = values.shape
    return jnp.sum(values.reshape(rows // 8, 8, cols), axis=0)


def dot(a, b):
    return jnp.dot(a, b, preferred_element_type=jnp.float32)


def kernel(
    nodes,
    slabs,
    warm,
    probes,
    potential,
    shift_hbm,
    weight_hbm,
    along_y_hbm,
    small_hbm,
    picks_hbm,
    core_hbm,
    moments,
    rbuf,
    qbuf,
    scale_out,
    table_out,
    own,
    hsend,
    csend,
    wbuf,
    halo,
    bbuf,
    vbuf,
    bside,
    vside,
    bedge,
    vedge,
    redge,
    far_out,
    far_in,
    qfirst,
    qlast,
    qhead,
    qahead,
    edge_out,
    edge_in,
    acc,
    sums,
    notes,
    shift_ref,
    weight_ref,
    along_y,
    small,
    picks,
    cpicks,
    local_sem,
    b_send,
    b_recv,
    a_send,
    a_recv,
    z_send,
    z_recv,
    q_send,
    q_recv,
    x_send,
    x_recv,
    s_send,
    s_recv,
):
    f32, bf16 = jnp.float32, jnp.bfloat16
    node, slab = lax.axis_index("node"), lax.axis_index("grid")
    depth, width, length = own.shape[1:]
    pairs = depth // 2
    block = width // nodes
    tall = up_to(block, 16)
    narrow = block % 16 == 0
    lower = nodes // 2
    places = table(block, depth)[0]
    above = (node, lax.rem(slab + 1, slabs))
    below = (node, lax.rem(slab + slabs - 1, slabs))
    step = 16 if narrow else 8
    mine = pl.ds(pl.multiple_of(node * block, step), block)
    left = pl.ds(pl.multiple_of(lax.rem(node * block + width - 8, width), 8), 8)
    right = pl.ds(pl.multiple_of(lax.rem(node * block + block, width), 8), 8)

    def matrix(name):
        at, rows, cols = places[name]
        return small[at : at + rows, 0:cols]

    loads = []

    def load(source, target):
        copy = pltpu.make_async_copy(source, target, local_sem.at[len(loads)])
        copy.start()
        loads.append(copy)

    load(shift_hbm, shift_ref)
    load(weight_hbm, weight_ref)
    load(warm.at[0, 0], own)
    load(picks_hbm, picks)
    if not narrow:
        load(core_hbm, cpicks)
    first_loads = len(loads)
    load(along_y_hbm, along_y)
    load(small_hbm, small)
    load(probes.at[0, :, mine], bbuf.at[2 : depth + 2])
    load(potential.at[:, mine], vbuf.at[2 : depth + 2])
    load(probes.at[0, :, left], bside.at[0])
    load(probes.at[0, :, right], bside.at[1])
    load(potential.at[:, left], vside.at[0])
    load(potential.at[:, right], vside.at[1])
    if narrow:
        load(warm.at[0, 0, :, :, mine], wbuf.at[0, :, 4 : depth + 4])

    barrier = pltpu.get_barrier_semaphore()
    for k in range(1, slabs):
        pl.semaphore_signal(
            barrier, inc=1, device_id=(node, lax.rem(slab + k, slabs)), device_id_type=MESH
        )
    for k in range(1, nodes):
        pl.semaphore_signal(
            barrier, inc=1, device_id=(lax.rem(node + k, nodes), slab), device_id_type=MESH
        )
    pl.semaphore_wait(barrier, slabs + nodes - 2)

    def remote(source, target, send_sem, recv_sem, device):
        return pltpu.make_async_remote_copy(
            src_ref=source,
            dst_ref=target,
            send_sem=send_sem,
            recv_sem=recv_sem,
            device_id=device,
            device_id_type=MESH,
        )

    steps = offsets(nodes)
    distant = sum(1 for a, b in steps if a and b)
    tall_y = nodes // 2
    at_y, at_x = node // 2, lax.rem(node, 2)

    def peer(k):
        a, b = steps[k]
        return lax.rem(at_y + a, tall_y) * 2 + lax.rem(at_x + b, 2)

    def owner_of(k):
        a, b = steps[k]
        return lax.rem(at_y + tall_y - a, tall_y) * 2 + lax.rem(at_x + b, 2)

    def core(m, first, last):
        if narrow:
            rows = pl.ds(pl.multiple_of(m * block, step), block)
            return warm.at[0, 0, :, first:last, rows]
        return csend.at[m, :, first:last]

    chunks = ((0, 2), (depth - 2, depth), (2, depth - 2))

    def gather_copy(k, c):
        first, last = chunks[c]
        return remote(
            core(peer(k), first, last),
            wbuf.at[k, :, 4 + first : 4 + last],
            a_send.at[k, c],
            a_recv.at[k, c],
            (peer(k), slab),
        )

    def halo_copy(k):
        return remote(
            hsend.at[peer(k)],
            halo.at[k, :, 1 : pairs + 1],
            a_send.at[k, 3],
            a_recv.at[k, 3],
            (peer(k), slab),
        )

    def note_copy(k):
        return remote(notes.at[0], notes.at[k], a_send.at[k, 4], a_recv.at[k, 4], (peer(k), slab))

    top = depth + 4
    routes = (
        ((4, 6), (top, top + 2), below),
        ((top - 2, top), (2, 4), above),
        ((6, 7), (top + 2, top + 3), below),
        ((top - 3, top - 2), (1, 2), above),
    )

    def forward(k, c):
        source, target, device = routes[c]
        if isinstance(k, int) and k == 0:
            part = core(node, source[0] - 4, source[1] - 4)
        else:
            part = wbuf.at[k, :, source[0] : source[1]]
        return remote(
            part, wbuf.at[k, :, target[0] : target[1]], z_send.at[k, c], z_recv.at[k, c], device
        )

    def forward_halo(k, c):
        source, target, device = ((1, pairs + 1, below), (pairs, 0, above))[c]
        return remote(
            halo.at[k, :, source],
            halo.at[k, :, target],
            z_send.at[k, 4 + c],
            z_recv.at[k, 4 + c],
            device,
        )

    sides = []
    for at, (source, target) in enumerate(((probes.at[0], bbuf), (potential, vbuf))):
        for c, (first, there, device) in enumerate(
            ((0, depth + 2, below), (depth - 1, 1, above))
        ):
            sides.append(
                remote(
                    source.at[first : first + 1, mine],
                    target.at[there : there + 1],
                    b_send.at[2 * at + c],
                    b_recv.at[2 * at + c],
                    device,
                )
            )

    def far_copy(k, c):
        return remote(
            far_out.at[k, c], far_in.at[k, c], z_send.at[k, 6 + c], z_recv.at[k, 6 + c], routes[c][2]
        )

    order = [(k, c) for c in range(3) for k in range(1, nodes)]

    def pick():
        for copy in loads[2:first_loads]:
            copy.wait()
        for i in range(pairs):
            for part in range(2):
                rows = own[part, 2 * i : 2 * i + 2].reshape(2 * width, length)
                picked = dot(picks[...], rows).astype(bf16)
                for m in range(nodes):
                    hsend[m, part, i] = picked[16 * m : 16 * m + 16]
        if not narrow:
            for part in range(2):
                for p in range(depth):
                    picked = dot(cpicks[...], own[part, p]).astype(bf16)
                    for m in range(nodes):
                        csend[m, part, p] = picked[tall * m : tall * m + tall]

    def send_cores():
        for c in range(2):
            forward(0, c).start()
        for copy in sides:
            copy.start()
        for c in range(2, 4):
            forward(0, c).start()
        for k, c in order:
            if c < 2 or not narrow:
                gather_copy(k, c).start()

    if narrow:
        send_cores()
    for copy in loads[0:2]:
        copy.wait()
    row = lax.broadcasted_iota(jnp.int32, (8, length), 0)
    note = jnp.zeros((8, length), f32)
    entries = (shift_ref[0, 0], shift_ref[0, 1], weight_ref[0, 0], weight_ref[0, 1])
    for i, entry in enumerate(entries):
        note = jnp.where(row == i, entry, note)
    notes[0] = note
    for k in range(1, nodes):
        note_copy(k).start()
    pick()
    if not narrow:
        send_cores()
    for k in range(1, nodes):
        halo_copy(k).start()
    if narrow:
        for k, c in order:
            if c == 2:
                gather_copy(k, c).start()
    for part in range(2):
        for i in range(pairs):
            halo[0, part, 1 + i] = hsend[node, part, i]
    for c in range(2):
        forward_halo(0, c).start()
    if not narrow:
        for part in range(2):
            for p in range(depth):
                wbuf[0, part, 4 + p] = csend[node, part, p]

    acc[...] = jnp.zeros_like(acc)
    qfirst[...] = jnp.zeros_like(qfirst)
    qlast[...] = jnp.zeros_like(qlast)
    qbuf[lower:nodes, :, depth : depth + 2] = jnp.zeros((nodes - lower, 2, 2, block, length), f32)
    for copy in loads[first_loads:]:
        copy.wait()
    for i in range(pairs):
        for s in range(2):
            for side in range(2):
                there = 8 * i + 4 * s + 2 * side
                here = 6 if side == 0 else 0
                bedge[there : there + 2] = bside[side, 2 * i + s, here : here + 2]
                vedge[there : there + 2] = vside[side, 2 * i + s, here : here + 2]

    def shift_of(k):
        return notes[k, 0:1, :], notes[k, 1:2, :]

    def apply(shift, field, stencil, local):
        diagonal = shift[0] - local
        return (
            diagonal * field[0] - shift[1] * field[1] + stencil[0] * (1.0 / 24.0),
            diagonal * field[1] + shift[1] * field[0] + stencil[1] * (1.0 / 24.0),
        )

    def added(k, first, count, low, high, terms):
        def body(i, carry):
            for s in range(2):
                carry = tuple(c + fold(v) for c, v in zip(carry, terms(i, s)))
            return carry

        zero = jnp.zeros((8, length), f32)
        for i, total in enumerate(lax.fori_loop(low, high, body, (zero,) * count, unroll=True)):
            acc[k * SUMS + first + i] += total

    def wide(values):
        return values.astype(f32)[0:block]

    def residual(k, i, s):
        pp = 2 * i + s
        stencil, field = [], []
        for part in range(2):
            centre = wbuf[k, part, pp + 2]
            plane = (
                dot(centre, along_y[...])
                + dot(matrix("own"), centre)
                + dot(matrix(f"halo{s}"), halo[k, part, i])
            )[0:block]
            at = [wide(wbuf[k, part, pp + j]) for j in (0, 1, 3, 4)]
            stencil.append(plane + 16.0 * (at[1] + at[2]) - (at[0] + at[3]))
            field.append(wide(centre))
        source = bbuf[pp]
        image = apply(shift_of(k), field, stencil, vbuf[pp])
        r = source - image[0], -image[1]
        rbuf[k, 0, pp] = r[0]
        rbuf[k, 1, pp] = r[1]
        return source, field, r

    def residual_terms(k, i, s):
        source, field, r = residual(k, i, s)
        return (
            r[0] * r[0] - r[1] * r[1],
            2.0 * r[0] * r[1],
            source * field[0],
            source * field[1],
            source * r[0],
            source * r[1],
        )

    def edge_rows(k):
        stencil, field = [], []
        for part in range(2):
            around = halo[k, part].reshape(16 * (pairs + 2), length)
            both = dot(matrix("edge_halo"), around)
            plane = dot(both.astype(bf16), along_y[...])
            beside = [
                dot(matrix("edge_own"), wbuf[k, part, 4 + 2 * i : 6 + 2 * i].reshape(2 * tall, length))
                for i in range(pairs)
            ]
            beside = jnp.concatenate([rows[0:8] for rows in beside], axis=0)
            stencil.append(beside + both[0 : 4 * depth] + plane[4 * depth :])
            field.append(both[4 * depth :])
        image = apply(shift_of(k), field, stencil, vedge[...])
        redge[k, 0] = bedge[...] - image[0]
        redge[k, 1] = -image[1]

    def split(values):
        high = values.astype(bf16)
        return high, (values - high.astype(f32)).astype(bf16)

    def pack(values):
        high, low = split(values)
        if narrow:
            return jnp.concatenate([high, low], axis=0)
        return jnp.concatenate([high.astype(f32), low.astype(f32)], axis=0).astype(bf16)

    def slim(values):
        high, low = split(values)
        return jnp.concatenate([high.astype(f32), low.astype(f32)], axis=0).astype(bf16)

    def along(packed):
        both = dot(packed, along_y[...])
        return both[0:block] + both[block : 2 * block]

    def image_terms(k, i, s):
        p = 2 * i + s
        stencil, field = [], []
        for part in range(2):
            at = [rbuf[k, part, p + j] for j in range(5)]
            packed = pack(at[2])
            side = jnp.concatenate([packed, slim(redge[k, part, pl.ds(pl.multiple_of(8 * i, 8), 8)])], axis=0)
            plane = along(packed) + dot(matrix(f"split{s}"), side)[0:block]
            stencil.append(plane + 16.0 * (at[1] + at[3]) - (at[0] + at[4]))
            field.append(at[2])
        source = bbuf[p + 2]
        q = apply(shift_of(k), field, stencil, vbuf[p + 2])
        qbuf[k, 0, p] = q[0]
        qbuf[k, 1, p] = q[1]
        return (
            *cmul(field, q),
            q[0] * q[0] - q[1] * q[1],
            2.0 * q[0] * q[1],
            source * q[0],
            source * q[1],
        )

    def energy_terms(k, i, s):
        p = 2 * i + s
        stencil, field = [], []
        for part in range(2):
            at = [qbuf[k, part, p + j] for j in range(3)]
            packed = pack(at[0])
            plane = along(packed) + dot(matrix("ahead"), packed)[0:block]
            stencil.append(plane + 32.0 * at[1] - 2.0 * at[2])
            field.append(at[0])
        return cmul(field, apply(shift_of(k), field, stencil, vbuf[p + 2]))

    def narrowed(values):
        if not narrow:
            filler = jnp.zeros((tall - block, length), f32)
            values = jnp.concatenate([values, filler], axis=0)
        return values.astype(bf16)

    def own_step(k, carry):
        @pl.when(k == 1)
        def _():
            for at, (j, c) in enumerate(order):
                if at == 2 * (nodes - 1):
                    for m in range(1, nodes):
                        note_copy(m).wait_recv()
                        halo_copy(m).wait_recv()
                        for d in range(2):
                            forward_halo(m, d).start()
                gather_copy(j, c).wait_recv()
                for d in (c,) if c < 2 else (2, 3):
                    forward(j, d).start()

        for c in range(2):
            forward(k, c).wait_recv()
        added(k, 0, 6, 1, pairs + 1, functools.partial(residual_terms, k))

        for c, at in enumerate((3, depth)):
            for part in range(2):
                far_out[k, c, part] = narrowed(rbuf[k, part, at])
            far_copy(k, c).start()
        for c in range(2):
            forward_halo(k, c).wait_recv()
        edge_rows(k)
        added(k, 6, 6, 1, pairs - 1, functools.partial(image_terms, k))
        return carry

    with jax.named_scope("residual"):
        lax.fori_loop(0, nodes, own_step, 0)

    for copy in sides:
        copy.wait_recv()

    previous = lax.rem(node + nodes - 1, nodes)

    def q_copy(k, down):
        if down:
            return remote(
                edge_out.at[k], edge_in.at[k], q_send.at[k], q_recv.at[k], below
            )
        return remote(edge_out.at[k], edge_in.at[k], q_send.at[k], q_recv.at[k], above)

    def x_copy(k):
        a, b = steps[k]
        same, before = steps.index((a, 1 - b)), steps.index(((a - 1) % tall_y, 1 - b))
        there = at_x * same + (1 - at_x) * before
        return remote(
            qhead.at[k], qahead.at[there], x_send.at[k], x_recv.at[there], (previous, slab)
        )

    def x_arrival(k):
        return remote(
            qhead.at[k], qahead.at[k], x_send.at[k], x_recv.at[k], (previous, slab)
        )

    def outer_step(k, carry):
        for c in range(2, 4):
            forward(k, c).wait_recv()

        residual(k, 0, 1)
        residual(k, pairs + 1, 0)
        for c, at in enumerate((depth + 3, 0)):
            far_copy(k, c).wait_recv()
            for part in range(2):
                rbuf[k, part, at] = wide(far_in[k, c, part])

        def ends(j, s):
            return image_terms(k, j * (pairs - 1), s)

        added(k, 6, 6, 0, 2, ends)

        def share_q(first):
            for part in range(2):
                for p in range(2):
                    edge_out[k, part, p] = narrowed(qbuf[k, part, first + p])

        @pl.when(k < lower)
        def _():
            share_q(0)
            q_copy(k, True).start()

        @pl.when(k >= lower)
        def _():
            share_q(depth - 2)
            q_copy(k, False).start()

        for part in range(2):
            for p in range(depth):
                qfirst[k, part, 2 * p : 2 * p + 2] = qbuf[k, part, p, 0:2]
                qlast[k, part, 2 * p : 2 * p + 2] = qbuf[k, part, p, block - 2 : block]
            qhead[k, part] = qfirst[k, part].astype(bf16)
        for j in range(nodes):
            @pl.when(k == j)
            def _():
                x_copy(j).start()
        return carry

    with jax.named_scope("image"):
        lax.fori_loop(0, nodes, outer_step, 0)

    def energy_step(k, carry):
        @pl.when(k < lower)
        def _():
            q_copy(k, True).wait_recv()
            for part in range(2):
                for p in range(2):
                    qbuf[k, part, depth + p] = wide(edge_in[k, part, p])

        added(k, 12, 2, 0, pairs, functools.partial(energy_terms, k))
        @pl.when(k >= lower)
        def _():
            q_copy(k, False).wait_recv()
            near = [wide(edge_in[k, part, 1]) for part in range(2)]
            far = [wide(edge_in[k, part, 0]) for part in range(2)]
            zeroth = [qbuf[k, part, 0] for part in range(2)]
            first = [qbuf[k, part, 1] for part in range(2)]
            one = cmul(zeroth, [32.0 * near[part] - 2.0 * far[part] for part in range(2)])
            two = cmul(first, near)
            for part in range(2):
                acc[k * SUMS + 12 + part] += fold((one[part] - 2.0 * two[part]) * (1.0 / 24.0))

        return carry

    def cross_step(k, carry):
        x_arrival(k).wait_recv()
        last = [qlast[k, part] for part in range(2)]
        ahead = [dot(matrix("cross"), qahead[k, part]) for part in range(2)]
        crossing = cmul(last, ahead)
        for part in range(2):
            acc[k * SUMS + 12 + part] += fold(crossing[part] * (1.0 / 24.0))
        return carry

    with jax.named_scope("energy"):
        lax.fori_loop(0, nodes, energy_step, 0)
        lax.fori_loop(0, nodes, cross_step, 0)

    piece = 16 if narrow else block
    factor = []
    for k in range(nodes):
        shift, weight = shift_of(k), (notes[k, 2:3, :], notes[k, 3:4, :])
        scaled = (shift[0] - 4.0) * 0.2, shift[1] * 0.2
        factor.append((weight, scaled, cmul(weight, scaled)))

    def rows_of(p, step):
        def body(i, carry):
            rows = pl.ds(pl.multiple_of(i * piece, piece), piece)
            values = step(p, rows)
            for degree in range(2):
                for part in range(2):
                    moments[degree, 0, part, p, rows] = values[2 * degree + part]
            return carry

        lax.fori_loop(0, block // piece, body, 0, unroll=True)

    def start_rows(p, rows):
        values = [None] * 4
        for k in range(nodes):
            if narrow:
                x = [wbuf[k, part, p + 4, rows].astype(f32) for part in range(2)]
            else:
                x = [wide(wbuf[k, part, p + 4]) for part in range(2)]
            for degree in range(2):
                term = cmul(factor[k][2 * degree], x)
                for part in range(2):
                    at = 2 * degree + part
                    values[at] = term[part] if k == 0 else values[at] + term[part]
        return values

    def start_plane(p, carry):
        rows_of(p, start_rows)
        return carry

    with jax.named_scope("scalars"):
        lane = lax.broadcasted_iota(jnp.int32, (SUMS, 128), 1)
        shift_at = [owner_of(k) for k in range(nodes)]
        sub = lax.broadcasted_iota(jnp.int32, (SUMS, 128), 0)
        per_row = 128 // SUMS
        spread = [jnp.zeros((SUMS, 128), f32) for _ in range(sums.shape[1])]
        for k in range(nodes):
            partial = jnp.sum(acc[k * SUMS : (k + 1) * SUMS], axis=1)
            lanes = partial[:, 0:128]
            for at in range(128, length, 128):
                lanes = lanes + partial[:, at : at + 128]
            whole = jnp.sum(lanes, axis=1, keepdims=True)
            for row in range(len(spread)):
                there = (shift_at[k] - row * per_row) * SUMS + sub
                spread[row] = spread[row] + jnp.where(lane == there, whole, 0.0)
        me = node * slabs + slab
        for row, values in enumerate(spread):
            sums[me, row : row + 1] = jnp.sum(values, axis=0, keepdims=True)
        hops = [(sum(map(bool, steps[k])), min(b, slabs - b), k, b) for k in range(nodes) for b in range(slabs)]
        scalar_copies = []
        for _, _, k, b in sorted(hops, reverse=True)[:-1]:
            at = k * slabs + b
            there = peer(k), lax.rem(slab + b, slabs)
            scalar_copies.append(
                remote(sums.at[me], sums.at[me], s_send.at[at], s_recv.at[at], there)
            )
        for copy in scalar_copies:
            copy.start()
        lax.fori_loop(0, depth, start_plane, 0)
        for copy in scalar_copies:
            copy.wait_recv()
        every = jnp.sum(sums[...], axis=0)
        total = jnp.zeros((SUMS, 128), f32)
        for owner in range(nodes):
            row = owner // per_row
            wide_row = jnp.broadcast_to(every[row : row + 1], (SUMS, 128))
            picked = jnp.where(lane == (owner - row * per_row) * SUMS + sub, wide_row, 0.0)
            total = total + jnp.where(lane == owner, jnp.sum(picked, axis=1, keepdims=True), 0.0)
        pair = lambda i: (total[i : i + 1], total[i + 1 : i + 2])
        s0, t0, t1, s1, s2, t2, s3 = (pair(i) for i in range(0, 14, 2))
        row_lane = lax.broadcasted_iota(jnp.int32, (8, 128), 1)
        known = jnp.zeros((8, 128), f32)
        for k in range(nodes):
            known = known + jnp.where(row_lane == shift_at[k], notes[k][:, 0:128], 0.0)
        shift = known[0:1], known[1:2]
        weight = known[2:3], known[3:4]
        step0 = cdiv(s0, s1)
        square = cmul(step0, step0)
        norm1 = cmul(square, s2)
        norm1 = norm1[0] - s0[0], norm1[1] - s0[1]
        ratio = cdiv(norm1, s0)
        grow = ratio[0] + 1.0, ratio[1]
        one = cmul(cmul(grow, grow), s1)
        two = cmul(cmul(grow, step0), s2)
        three = cmul(square, s3)
        step1 = cdiv(
            norm1, (one[0] - 2.0 * two[0] + three[0], one[1] - 2.0 * two[1] + three[1])
        )
        coef_r = cmul(step1, grow)
        coef_r = coef_r[0] + step0[0], coef_r[1] + step0[1]
        coef_q = cmul(step1, step0)
        coef_q = -coef_q[0], -coef_q[1]
        inner_r, inner_q = cmul(coef_r, t1), cmul(coef_q, t2)
        inner = t0[0] + inner_r[0] + inner_q[0], t0[1] + inner_r[1] + inner_q[1]
        share = cmul(weight, inner)
        following = cmul(weight, ((shift[0] - 4.0) * 0.2, shift[1] * 0.2))
        factors = jnp.zeros((SUMS, 128), f32)
        for i, entry in enumerate((*weight, *following, *share, *coef_r, *coef_q)):
            factors = jnp.where(sub == i, entry, factors)
        table_out[...] = factors
        for k in range(nodes):
            one_lane = jnp.where(lane == shift_at[k], factors, 0.0)
            values = jnp.broadcast_to(jnp.sum(one_lane, axis=1, keepdims=True), (SUMS, length))
            along_r, along_q = ((values[i : i + 1], values[i + 1 : i + 2]) for i in (6, 8))
            entries = (*factor[k][1], *cmul(factor[k][0], along_r), *cmul(factor[k][0], along_q))
            for i, entry in enumerate(entries):
                scale_out[k, i : i + 1] = entry

    for copy in [*sides, *scalar_copies]:
        copy.wait_send()
    for k in range(nodes):
        if k:
            for c in range(3):
                gather_copy(k, c).wait_send()
            halo_copy(k).wait_send()
            note_copy(k).wait_send()
        for c in range(4):
            forward(k, c).wait_send()
        for c in range(2):
            forward_halo(k, c).wait_send()
            far_copy(k, c).wait_send()
        q_copy(k, k < lower).wait_send()
        x_copy(k).wait_send()


def finish(nodes, started, rbuf, qbuf, scales, factors, moments, trace, result, pair, sems):
    depth, block, length = result.shape[2:]
    piece = 16 if block % 16 == 0 else block
    scale = []
    for k in range(nodes):
        rows = [scales[k, i : i + 1, :] for i in range(6)]
        scale.append((rows[0:2], rows[2:4], rows[4:6]))

    def copy(p):
        return pltpu.make_async_copy(result.at[:, :, p], moments.at[:, 0, :, p], sems.at[p])

    def plane(p, carry):
        def body(i, inner):
            rows = pl.ds(pl.multiple_of(i * piece, piece), piece)
            values = [started[degree, 0, part, p, rows] for degree in range(2) for part in range(2)]
            for k in range(nodes):
                r = [rbuf[k, part, p + 2, rows] for part in range(2)]
                q = [qbuf[k, part, p, rows] for part in range(2)]
                along_r, along_q = cmul(scale[k][1], r), cmul(scale[k][2], q)
                field = [along_r[part] + along_q[part] for part in range(2)]
                term = cmul(scale[k][0], field)
                for part in range(2):
                    values[part] = values[part] + field[part]
                    values[2 + part] = values[2 + part] + term[part]
            for degree in range(2):
                for part in range(2):
                    result[degree, part, p, rows] = values[2 * degree + part]
            return inner

        lax.fori_loop(0, block // piece, body, 0, unroll=True)
        copy(p).start()
        return carry

    values = factors[...]
    sub = lax.broadcasted_iota(jnp.int32, values.shape, 0)
    lane = lax.broadcasted_iota(jnp.int32, values.shape, 1)
    for part in range(2):
        pair[part] = jnp.sum(jnp.where((sub == 4 + part) & (lane < nodes), values, 0.0))
    trace_copy = pltpu.make_async_copy(pair, trace, sems.at[depth])
    trace_copy.start()
    lax.fori_loop(0, depth, plane, 0, unroll=2)
    for p in range(depth):
        copy(p).wait()
    trace_copy.wait()


def per_device(nodes, slabs, probes, potential, warm_start, shift_points, quad_weights):
    depth, width, length = potential.shape
    block = width // nodes
    tall = up_to(block, 16)
    narrow = block % 16 == 0
    pairs = depth // 2
    f32, bf16 = jnp.float32, jnp.bfloat16
    anywhere = pl.BlockSpec(memory_space=pltpu.HBM)
    vector = pl.BlockSpec(memory_space=pltpu.VMEM)
    dma = pltpu.SemaphoreType.DMA
    small = small_matrices(block, depth)
    picks = halo_picks(width, nodes)
    cpicks = picks if narrow else core_picks(width, nodes)
    results = pl.pallas_call(
        functools.partial(kernel, nodes, slabs),
        out_shape=(
            pltpu.VMEM((2, 1, 2, depth, block, length), f32),
            pltpu.VMEM((nodes, 2, depth + 4, block, length), f32),
            pltpu.VMEM((nodes, 2, depth + 2, block, length), f32),
            pltpu.VMEM((nodes, 8, length), f32),
            pltpu.VMEM((SUMS, 128), f32),
        ),
        in_specs=[anywhere] * 9,
        out_specs=(vector,) * 5,
        scratch_shapes=[
            pltpu.VMEM((2, depth, width, length), bf16),
            pltpu.VMEM((nodes, 2, pairs, 16, length), bf16),
            pltpu.VMEM((16, 128) if narrow else (nodes, 2, depth, tall, length), bf16),
            pltpu.VMEM((nodes, 2, depth + 8, tall, length), bf16),
            pltpu.VMEM((nodes, 2, pairs + 2, 16, length), bf16),
            pltpu.VMEM((depth + 4, block, length), f32),
            pltpu.VMEM((depth + 4, block, length), f32),
            pltpu.VMEM((2, depth, 8, length), f32),
            pltpu.VMEM((2, depth, 8, length), f32),
            pltpu.VMEM((4 * depth, length), f32),
            pltpu.VMEM((4 * depth, length), f32),
            pltpu.VMEM((nodes, 2, 4 * depth, length), f32),
            pltpu.VMEM((nodes, 2, 2, tall, length), bf16),
            pltpu.VMEM((nodes, 2, 2, tall, length), bf16),
            pltpu.VMEM((nodes, 2, 16, length), f32),
            pltpu.VMEM((nodes, 2, 16, length), f32),
            pltpu.VMEM((nodes, 2, 16, length), bf16),
            pltpu.VMEM((nodes, 2, 16, length), bf16),
            pltpu.VMEM((nodes, 2, 2, tall, length), bf16),
            pltpu.VMEM((nodes, 2, 2, tall, length), bf16),
            pltpu.VMEM((nodes * SUMS, 8, length), f32),
            pltpu.VMEM((nodes * slabs, up_to(nodes * SUMS, 128) // 128, 128), f32),
            pltpu.VMEM((nodes, 8, length), f32),
            pltpu.SMEM((1, 2), f32),
            pltpu.SMEM((1, 2), f32),
            pltpu.VMEM((length, length), bf16),
            pltpu.VMEM(small.shape, bf16),
            pltpu.VMEM(picks.shape, bf16),
            pltpu.VMEM((16, 128) if narrow else cpicks.shape, bf16),
            dma((14,)),
            dma((4,)),
            dma((4,)),
            dma((nodes, 5)),
            dma((nodes, 5)),
            dma((nodes, 8)),
            dma((nodes, 8)),
            dma((nodes,)),
            dma((nodes,)),
            dma((nodes,)),
            dma((nodes,)),
            dma((nodes * slabs,)),
            dma((nodes * slabs,)),
        ],
        compiler_params=pltpu.CompilerParams(
            collective_id=0, has_side_effects=True, vmem_limit_bytes=48 * 1024 * 1024
        ),
    )(
        warm_start,
        probes,
        potential,
        shift_points,
        quad_weights,
        jnp.asarray(ring_matrix(length, -90.0)),
        jnp.asarray(small),
        jnp.asarray(picks),
        jnp.asarray(cpicks),
    )
    return pl.pallas_call(
        functools.partial(finish, nodes),
        out_shape=(
            jax.ShapeDtypeStruct((2, 1, 2, depth, block, length), f32),
            jax.ShapeDtypeStruct((2,), f32),
        ),
        in_specs=[vector] * 5,
        out_specs=(anywhere, anywhere),
        scratch_shapes=[
            pltpu.VMEM((2, 2, depth, block, length), f32),
            pltpu.SMEM((2,), f32),
            dma((depth + 1,)),
        ],
        compiler_params=pltpu.CompilerParams(vmem_limit_bytes=4 * 1024 * 1024),
    )(*results)


def solution(mesh):
    return jax.shard_map(
        functools.partial(per_device, mesh.shape["node"], mesh.shape["grid"]),
        mesh=mesh,
        in_specs=(
            P(None, "grid", None, None),
            P("grid", None, None),
            P("node", None, None, "grid", None, None),
            P("node", None),
            P("node", None),
        ),
        out_specs=(P(None, None, None, "grid", "node", None), P()),
        check_vma=False,
    )
```

```python
import functools

import jax
import jax.numpy as jnp
import ml_dtypes
import numpy as np
from jax import lax
from jax.experimental import pallas as pl
from jax.experimental.pallas import tpu as pltpu
from jax.sharding import PartitionSpec as P

MESH = pl.DeviceIdType.MESH
SUMS = 16
NEAR, FAR = 16.0, -1.0


def up_to(size, step):
    return -(-size // step) * step


def weight_of(distance):
    return {1: NEAR, 2: FAR}.get(abs(distance), 0.0)


def ring_matrix(size, diagonal):
    matrix = np.zeros((size, size), np.float32)
    at = np.arange(size)
    for step, weight in ((1, NEAR), (2, FAR)):
        matrix[at, (at + step) % size] += weight
        matrix[at, (at - step) % size] += weight
    matrix[at, at] += diagonal
    return matrix.astype(ml_dtypes.bfloat16)


def table(block, depth):
    tall = up_to(block, 16)
    pairs = depth // 2
    sizes = {
        "near0": (tall, tall + 16),
        "near1": (tall, tall + 16),
        "split0": (tall, 2 * block + 16),
        "split1": (tall, 2 * block + 16),
        "ahead": (tall, 2 * block),
        "edge_own": (16, 2 * tall),
        "edge_halo": (16 * pairs, 16 * (pairs + 2)),
        "cross": (16, 16),
    }
    at, places = 0, {}
    for name, (rows, cols) in sizes.items():
        places[name] = (at, rows, cols)
        at += rows
    return places, at, up_to(max(cols for rows, cols in sizes.values()), 128)


def small_matrices(block, depth):
    tall = up_to(block, 16)
    places, rows, cols = table(block, depth)
    whole = np.zeros((rows, cols), np.float32)
    view = {name: whole[at : at + n, :m] for name, (at, n, m) in places.items()}
    wide = [-4, -3, -2, -1, block, block + 1, block + 2, block + 3]
    slim = [-2, -1, block, block + 1]
    for i in range(block):
        for j in range(block):
            w = weight_of(i - j)
            for s in range(2):
                view[f"near{s}"][i, j] = w
                view[f"split{s}"][i, j] = w
                view[f"split{s}"][i, block + j] = w
            if j > i:
                view["ahead"][i, j] = 2 * w
                view["ahead"][i, block + j] = 2 * w
        for s in range(2):
            for c, x in enumerate(wide):
                view[f"near{s}"][i, tall + 8 * s + c] = weight_of(i - x)
            for c, x in enumerate(slim):
                view[f"split{s}"][i, 2 * block + 4 * s + c] = weight_of(i - x)
                view[f"split{s}"][i, 2 * block + 8 + 4 * s + c] = weight_of(i - x)
    for s in range(2):
        for t, x in enumerate(slim):
            row, here = 4 * s + t, wide.index(x)
            for j in range(block):
                view["edge_own"][row, tall * s + j] = weight_of(x - j)
            for i in range(depth // 2):
                to, at = 8 * i + row, 16 * i
                for c, other in enumerate(wide):
                    view["edge_halo"][to, at + 16 + 8 * s + c] += weight_of(x - other)
                for q in range(6):
                    view["edge_halo"][to, at + 8 * q + here] += weight_of(q - 2 - s)
                view["edge_halo"][4 * depth + to, at + 16 + 8 * s + here] = 1.0
    for p in range(depth):
        for e in range(2):
            for f in range(2):
                view["cross"][2 * p + e, 2 * p + f] = 2 * weight_of(2 - e + f)
    return whole.astype(ml_dtypes.bfloat16)


def halo_picks(width, nodes):
    block = width // nodes
    picks = np.zeros((nodes * 16, 2 * width), np.float32)
    for m in range(nodes):
        for s in range(2):
            for c, x in enumerate([-4, -3, -2, -1, block, block + 1, block + 2, block + 3]):
                picks[16 * m + 8 * s + c, width * s + (block * m + x) % width] = 1.0
    return picks.astype(ml_dtypes.bfloat16)


def core_picks(width, nodes):
    block = width // nodes
    tall = up_to(block, 16)
    picks = np.zeros((nodes * tall, width), np.float32)
    for m in range(nodes):
        for i in range(block):
            picks[tall * m + i, block * m + i] = 1.0
    return picks.astype(ml_dtypes.bfloat16)


def offsets(nodes):
    every = [(a, b) for a in range(nodes // 2) for b in range(2)]
    return [(0, 0)] + sorted(every[1:], key=lambda at: -(at[0] > 0) - (at[1] > 0))


def cmul(a, b):
    return a[0] * b[0] - a[1] * b[1], a[0] * b[1] + a[1] * b[0]


def cdiv(a, b):
    size = b[0] * b[0] + b[1] * b[1]
    return (a[0] * b[0] + a[1] * b[1]) / size, (a[1] * b[0] - a[0] * b[1]) / size


def fold(values):
    rows, cols = values.shape
    return jnp.sum(values.reshape(rows // 8, 8, cols), axis=0)


def dot(a, b):
    return jnp.dot(a, b, preferred_element_type=jnp.float32)


def kernel(
    nodes,
    slabs,
    warm,
    probes,
    potential,
    shift_hbm,
    weight_hbm,
    along_y_hbm,
    small_hbm,
    picks_hbm,
    core_hbm,
    moments,
    rbuf,
    qbuf,
    scale_out,
    table_out,
    own,
    hsend,
    csend,
    wbuf,
    halo,
    bbuf,
    vbuf,
    bside,
    vside,
    bedge,
    vedge,
    redge,
    far_out,
    far_in,
    qfirst,
    qlast,
    qhead,
    qahead,
    edge_out,
    edge_in,
    acc,
    sums,
    notes,
    shift_ref,
    weight_ref,
    along_y,
    small,
    picks,
    cpicks,
    local_sem,
    b_send,
    b_recv,
    a_send,
    a_recv,
    z_send,
    z_recv,
    q_send,
    q_recv,
    x_send,
    x_recv,
    s_send,
    s_recv,
):
    f32, bf16 = jnp.float32, jnp.bfloat16
    node, slab = lax.axis_index("node"), lax.axis_index("grid")
    depth, width, length = own.shape[1:]
    pairs = depth // 2
    block = width // nodes
    tall = up_to(block, 16)
    narrow = block % 16 == 0
    lower = nodes // 2
    places = table(block, depth)[0]
    above = (node, lax.rem(slab + 1, slabs))
    below = (node, lax.rem(slab + slabs - 1, slabs))
    step = 16 if narrow else 8
    mine = pl.ds(pl.multiple_of(node * block, step), block)
    left = pl.ds(pl.multiple_of(lax.rem(node * block + width - 8, width), 8), 8)
    right = pl.ds(pl.multiple_of(lax.rem(node * block + block, width), 8), 8)

    def matrix(name):
        at, rows, cols = places[name]
        return small[at : at + rows, 0:cols]

    loads = []

    def load(source, target):
        copy = pltpu.make_async_copy(source, target, local_sem.at[len(loads)])
        copy.start()
        loads.append(copy)

    load(shift_hbm, shift_ref)
    load(weight_hbm, weight_ref)
    load(warm.at[0, 0], own)
    load(picks_hbm, picks)
    if not narrow:
        load(core_hbm, cpicks)
    first_loads = len(loads)
    load(along_y_hbm, along_y)
    load(small_hbm, small)
    load(probes.at[0, :, mine], bbuf.at[2 : depth + 2])
    load(potential.at[:, mine], vbuf.at[2 : depth + 2])
    load(probes.at[0, :, left], bside.at[0])
    load(probes.at[0, :, right], bside.at[1])
    load(potential.at[:, left], vside.at[0])
    load(potential.at[:, right], vside.at[1])
    if narrow:
        load(warm.at[0, 0, :, :, mine], wbuf.at[0, :, 4 : depth + 4])

    barrier = pltpu.get_barrier_semaphore()
    for k in range(1, slabs):
        pl.semaphore_signal(
            barrier, inc=1, device_id=(node, lax.rem(slab + k, slabs)), device_id_type=MESH
        )
    for k in range(1, nodes):
        pl.semaphore_signal(
            barrier, inc=1, device_id=(lax.rem(node + k, nodes), slab), device_id_type=MESH
        )
    pl.semaphore_wait(barrier, slabs + nodes - 2)

    def remote(source, target, send_sem, recv_sem, device):
        return pltpu.make_async_remote_copy(
            src_ref=source,
            dst_ref=target,
            send_sem=send_sem,
            recv_sem=recv_sem,
            device_id=device,
            device_id_type=MESH,
        )

    steps = offsets(nodes)
    distant = sum(1 for a, b in steps if a and b)
    tall_y = nodes // 2
    at_y, at_x = node // 2, lax.rem(node, 2)

    def peer(k):
        a, b = steps[k]
        return lax.rem(at_y + a, tall_y) * 2 + lax.rem(at_x + b, 2)

    def owner_of(k):
        a, b = steps[k]
        return lax.rem(at_y + tall_y - a, tall_y) * 2 + lax.rem(at_x + b, 2)

    def core(m, first, last):
        if narrow:
            rows = pl.ds(pl.multiple_of(m * block, step), block)
            return warm.at[0, 0, :, first:last, rows]
        return csend.at[m, :, first:last]

    chunks = ((0, 2), (depth - 2, depth), (2, depth - 2))

    def gather_copy(k, c):
        first, last = chunks[c]
        return remote(
            core(peer(k), first, last),
            wbuf.at[k, :, 4 + first : 4 + last],
            a_send.at[k, c],
            a_recv.at[k, c],
            (peer(k), slab),
        )

    def halo_copy(k):
        return remote(
            hsend.at[peer(k)],
            halo.at[k, :, 1 : pairs + 1],
            a_send.at[k, 3],
            a_recv.at[k, 3],
            (peer(k), slab),
        )

    def note_copy(k):
        return remote(notes.at[0], notes.at[k], a_send.at[k, 4], a_recv.at[k, 4], (peer(k), slab))

    top = depth + 4
    routes = (
        ((4, 6), (top, top + 2), below),
        ((top - 2, top), (2, 4), above),
        ((6, 7), (top + 2, top + 3), below),
        ((top - 3, top - 2), (1, 2), above),
    )

    def forward(k, c):
        source, target, device = routes[c]
        if isinstance(k, int) and k == 0:
            part = core(node, source[0] - 4, source[1] - 4)
        else:
            part = wbuf.at[k, :, source[0] : source[1]]
        return remote(
            part, wbuf.at[k, :, target[0] : target[1]], z_send.at[k, c], z_recv.at[k, c], device
        )

    def forward_halo(k, c):
        source, target, device = ((1, pairs + 1, below), (pairs, 0, above))[c]
        return remote(
            halo.at[k, :, source],
            halo.at[k, :, target],
            z_send.at[k, 4 + c],
            z_recv.at[k, 4 + c],
            device,
        )

    sides = []
    for at, (source, target) in enumerate(((probes.at[0], bbuf), (potential, vbuf))):
        for c, (first, there, device) in enumerate(
            ((0, depth + 2, below), (depth - 1, 1, above))
        ):
            sides.append(
                remote(
                    source.at[first : first + 1, mine],
                    target.at[there : there + 1],
                    b_send.at[2 * at + c],
                    b_recv.at[2 * at + c],
                    device,
                )
            )

    def far_copy(k, c):
        return remote(
            far_out.at[k, c], far_in.at[k, c], z_send.at[k, 6 + c], z_recv.at[k, 6 + c], routes[c][2]
        )

    order = [(k, c) for c in range(3) for k in range(1, nodes)]

    def pick():
        for copy in loads[2:first_loads]:
            copy.wait()
        for i in range(pairs):
            for part in range(2):
                rows = own[part, 2 * i : 2 * i + 2].reshape(2 * width, length)
                picked = dot(picks[...], rows).astype(bf16)
                for m in range(nodes):
                    hsend[m, part, i] = picked[16 * m : 16 * m + 16]
        if not narrow:
            for part in range(2):
                for p in range(depth):
                    picked = dot(cpicks[...], own[part, p]).astype(bf16)
                    for m in range(nodes):
                        csend[m, part, p] = picked[tall * m : tall * m + tall]

    def send_cores():
        for c in range(2):
            forward(0, c).start()
        for copy in sides:
            copy.start()
        for c in range(2, 4):
            forward(0, c).start()
        for k, c in order:
            if c < 2 or not narrow:
                gather_copy(k, c).start()

    if narrow:
        send_cores()
    for copy in loads[0:2]:
        copy.wait()
    row = lax.broadcasted_iota(jnp.int32, (8, length), 0)
    note = jnp.zeros((8, length), f32)
    entries = (shift_ref[0, 0], shift_ref[0, 1], weight_ref[0, 0], weight_ref[0, 1])
    for i, entry in enumerate(entries):
        note = jnp.where(row == i, entry, note)
    notes[0] = note
    for k in range(1, nodes):
        note_copy(k).start()
    pick()
    if not narrow:
        send_cores()
    for k in range(1, nodes):
        halo_copy(k).start()
    if narrow:
        for k, c in order:
            if c == 2:
                gather_copy(k, c).start()
    for part in range(2):
        for i in range(pairs):
            halo[0, part, 1 + i] = hsend[node, part, i]
    for c in range(2):
        forward_halo(0, c).start()
    if not narrow:
        for part in range(2):
            for p in range(depth):
                wbuf[0, part, 4 + p] = csend[node, part, p]

    acc[...] = jnp.zeros_like(acc)
    qfirst[...] = jnp.zeros_like(qfirst)
    qlast[...] = jnp.zeros_like(qlast)
    qbuf[lower:nodes, :, depth : depth + 2] = jnp.zeros((nodes - lower, 2, 2, block, length), f32)
    for copy in loads[first_loads:]:
        copy.wait()
    for i in range(pairs):
        for s in range(2):
            for side in range(2):
                there = 8 * i + 4 * s + 2 * side
                here = 6 if side == 0 else 0
                bedge[there : there + 2] = bside[side, 2 * i + s, here : here + 2]
                vedge[there : there + 2] = vside[side, 2 * i + s, here : here + 2]

    def shift_of(k):
        return notes[k, 0:1, :], notes[k, 1:2, :]

    def apply(shift, field, stencil, local):
        diagonal = shift[0] - local
        return (
            diagonal * field[0] - shift[1] * field[1] + stencil[0] * (1.0 / 24.0),
            diagonal * field[1] + shift[1] * field[0] + stencil[1] * (1.0 / 24.0),
        )

    def added(k, first, count, low, high, terms):
        def body(i, carry):
            for s in range(2):
                carry = tuple(c + fold(v) for c, v in zip(carry, terms(i, s)))
            return carry

        zero = jnp.zeros((8, length), f32)
        for i, total in enumerate(lax.fori_loop(low, high, body, (zero,) * count, unroll=True)):
            acc[k * SUMS + first + i] += total

    def wide(values):
        return values.astype(f32)[0:block]

    def residual(k, i, s):
        pp = 2 * i + s
        stencil, field = [], []
        for part in range(2):
            centre = wbuf[k, part, pp + 2]
            stacked = jnp.concatenate([centre, halo[k, part, i]], axis=0)
            plane = (dot(centre, along_y[...]) + dot(matrix(f"near{s}"), stacked))[0:block]
            at = [wide(wbuf[k, part, pp + j]) for j in (0, 1, 3, 4)]
            stencil.append(plane + 16.0 * (at[1] + at[2]) - (at[0] + at[3]))
            field.append(wide(centre))
        source = bbuf[pp]
        image = apply(shift_of(k), field, stencil, vbuf[pp])
        r = source - image[0], -image[1]
        rbuf[k, 0, pp] = r[0]
        rbuf[k, 1, pp] = r[1]
        return source, field, r

    def residual_terms(k, i, s):
        source, field, r = residual(k, i, s)
        return (
            r[0] * r[0] - r[1] * r[1],
            2.0 * r[0] * r[1],
            source * field[0],
            source * field[1],
            source * r[0],
            source * r[1],
        )

    def edge_rows(k):
        stencil, field = [], []
        for part in range(2):
            around = halo[k, part].reshape(16 * (pairs + 2), length)
            both = dot(matrix("edge_halo"), around)
            plane = dot(both.astype(bf16), along_y[...])
            beside = [
                dot(matrix("edge_own"), wbuf[k, part, 4 + 2 * i : 6 + 2 * i].reshape(2 * tall, length))
                for i in range(pairs)
            ]
            beside = jnp.concatenate([rows[0:8] for rows in beside], axis=0)
            stencil.append(beside + both[0 : 4 * depth] + plane[4 * depth :])
            field.append(both[4 * depth :])
        image = apply(shift_of(k), field, stencil, vedge[...])
        redge[k, 0] = bedge[...] - image[0]
        redge[k, 1] = -image[1]

    def split(values):
        high = values.astype(bf16)
        return high, (values - high.astype(f32)).astype(bf16)

    def pack(values):
        high, low = split(values)
        if narrow:
            return jnp.concatenate([high, low], axis=0)
        return jnp.concatenate([high.astype(f32), low.astype(f32)], axis=0).astype(bf16)

    def slim(values):
        high, low = split(values)
        return jnp.concatenate([high.astype(f32), low.astype(f32)], axis=0).astype(bf16)

    def along(packed):
        both = dot(packed, along_y[...])
        return both[0:block] + both[block : 2 * block]

    def image_terms(k, i, s):
        p = 2 * i + s
        stencil, field = [], []
        for part in range(2):
            at = [rbuf[k, part, p + j] for j in range(5)]
            packed = pack(at[2])
            side = jnp.concatenate([packed, slim(redge[k, part, pl.ds(pl.multiple_of(8 * i, 8), 8)])], axis=0)
            plane = along(packed) + dot(matrix(f"split{s}"), side)[0:block]
            stencil.append(plane + 16.0 * (at[1] + at[3]) - (at[0] + at[4]))
            field.append(at[2])
        source = bbuf[p + 2]
        q = apply(shift_of(k), field, stencil, vbuf[p + 2])
        qbuf[k, 0, p] = q[0]
        qbuf[k, 1, p] = q[1]
        return (
            *cmul(field, q),
            q[0] * q[0] - q[1] * q[1],
            2.0 * q[0] * q[1],
            source * q[0],
            source * q[1],
        )

    def energy_terms(k, i, s):
        p = 2 * i + s
        stencil, field = [], []
        for part in range(2):
            at = [qbuf[k, part, p + j] for j in range(3)]
            packed = pack(at[0])
            plane = along(packed) + dot(matrix("ahead"), packed)[0:block]
            stencil.append(plane + 32.0 * at[1] - 2.0 * at[2])
            field.append(at[0])
        return cmul(field, apply(shift_of(k), field, stencil, vbuf[p + 2]))

    def narrowed(values):
        if not narrow:
            filler = jnp.zeros((tall - block, length), f32)
            values = jnp.concatenate([values, filler], axis=0)
        return values.astype(bf16)

    def own_step(k, carry):
        @pl.when(k == 1)
        def _():
            for at, (j, c) in enumerate(order):
                if at == 2 * (nodes - 1):
                    for m in range(1, nodes):
                        note_copy(m).wait_recv()
                        halo_copy(m).wait_recv()
                        for d in range(2):
                            forward_halo(m, d).start()
                gather_copy(j, c).wait_recv()
                for d in (c,) if c < 2 else (2, 3):
                    forward(j, d).start()

        for c in range(2):
            forward(k, c).wait_recv()
        added(k, 0, 6, 1, pairs + 1, functools.partial(residual_terms, k))

        for c, at in enumerate((3, depth)):
            for part in range(2):
                far_out[k, c, part] = narrowed(rbuf[k, part, at])
            far_copy(k, c).start()
        for c in range(2):
            forward_halo(k, c).wait_recv()
        edge_rows(k)
        added(k, 6, 6, 1, pairs - 1, functools.partial(image_terms, k))
        return carry

    with jax.named_scope("residual"):
        lax.fori_loop(0, nodes, own_step, 0)

    for copy in sides:
        copy.wait_recv()

    previous = lax.rem(node + nodes - 1, nodes)

    def q_copy(k, down):
        if down:
            return remote(
                edge_out.at[k], edge_in.at[k], q_send.at[k], q_recv.at[k], below
            )
        return remote(edge_out.at[k], edge_in.at[k], q_send.at[k], q_recv.at[k], above)

    def x_copy(k):
        a, b = steps[k]
        same, before = steps.index((a, 1 - b)), steps.index(((a - 1) % tall_y, 1 - b))
        there = at_x * same + (1 - at_x) * before
        return remote(
            qhead.at[k], qahead.at[there], x_send.at[k], x_recv.at[there], (previous, slab)
        )

    def x_arrival(k):
        return remote(
            qhead.at[k], qahead.at[k], x_send.at[k], x_recv.at[k], (previous, slab)
        )

    def outer_step(k, carry):
        for c in range(2, 4):
            forward(k, c).wait_recv()

        residual(k, 0, 1)
        residual(k, pairs + 1, 0)
        for c, at in enumerate((depth + 3, 0)):
            far_copy(k, c).wait_recv()
            for part in range(2):
                rbuf[k, part, at] = wide(far_in[k, c, part])

        def ends(j, s):
            return image_terms(k, j * (pairs - 1), s)

        added(k, 6, 6, 0, 2, ends)

        def share_q(first):
            for part in range(2):
                for p in range(2):
                    edge_out[k, part, p] = narrowed(qbuf[k, part, first + p])

        @pl.when(k < lower)
        def _():
            share_q(0)
            q_copy(k, True).start()

        @pl.when(k >= lower)
        def _():
            share_q(depth - 2)
            q_copy(k, False).start()

        for part in range(2):
            for p in range(depth):
                qfirst[k, part, 2 * p : 2 * p + 2] = qbuf[k, part, p, 0:2]
                qlast[k, part, 2 * p : 2 * p + 2] = qbuf[k, part, p, block - 2 : block]
            qhead[k, part] = qfirst[k, part].astype(bf16)
        for j in range(nodes):
            @pl.when(k == j)
            def _():
                x_copy(j).start()
        return carry

    with jax.named_scope("image"):
        lax.fori_loop(0, nodes, outer_step, 0)

    def energy_step(k, carry):
        @pl.when(k < lower)
        def _():
            q_copy(k, True).wait_recv()
            for part in range(2):
                for p in range(2):
                    qbuf[k, part, depth + p] = wide(edge_in[k, part, p])

        added(k, 12, 2, 0, pairs, functools.partial(energy_terms, k))
        @pl.when(k >= lower)
        def _():
            q_copy(k, False).wait_recv()
            near = [wide(edge_in[k, part, 1]) for part in range(2)]
            far = [wide(edge_in[k, part, 0]) for part in range(2)]
            zeroth = [qbuf[k, part, 0] for part in range(2)]
            first = [qbuf[k, part, 1] for part in range(2)]
            one = cmul(zeroth, [32.0 * near[part] - 2.0 * far[part] for part in range(2)])
            two = cmul(first, near)
            for part in range(2):
                acc[k * SUMS + 12 + part] += fold((one[part] - 2.0 * two[part]) * (1.0 / 24.0))

        return carry

    def cross_step(k, carry):
        x_arrival(k).wait_recv()
        last = [qlast[k, part] for part in range(2)]
        ahead = [dot(matrix("cross"), qahead[k, part]) for part in range(2)]
        crossing = cmul(last, ahead)
        for part in range(2):
            acc[k * SUMS + 12 + part] += fold(crossing[part] * (1.0 / 24.0))
        return carry

    with jax.named_scope("energy"):
        lax.fori_loop(0, nodes, energy_step, 0)
        lax.fori_loop(0, nodes, cross_step, 0, unroll=True)

    piece = 16 if narrow else block
    factor = []
    for k in range(nodes):
        shift, weight = shift_of(k), (notes[k, 2:3, :], notes[k, 3:4, :])
        scaled = (shift[0] - 4.0) * 0.2, shift[1] * 0.2
        factor.append((weight, scaled, cmul(weight, scaled)))

    def rows_of(p, step):
        def body(i, carry):
            rows = pl.ds(pl.multiple_of(i * piece, piece), piece)
            values = step(p, rows)
            for degree in range(2):
                for part in range(2):
                    moments[degree, 0, part, p, rows] = values[2 * degree + part]
            return carry

        lax.fori_loop(0, block // piece, body, 0, unroll=True)

    def start_rows(p, rows):
        values = [None] * 4
        for k in range(nodes):
            if narrow:
                x = [wbuf[k, part, p + 4, rows].astype(f32) for part in range(2)]
            else:
                x = [wide(wbuf[k, part, p + 4]) for part in range(2)]
            for degree in range(2):
                term = cmul(factor[k][2 * degree], x)
                for part in range(2):
                    at = 2 * degree + part
                    values[at] = term[part] if k == 0 else values[at] + term[part]
        return values

    def start_plane(p, carry):
        rows_of(p, start_rows)
        return carry

    with jax.named_scope("scalars"):
        lane = lax.broadcasted_iota(jnp.int32, (SUMS, 128), 1)
        shift_at = [owner_of(k) for k in range(nodes)]
        sub = lax.broadcasted_iota(jnp.int32, (SUMS, 128), 0)
        per_row = 128 // SUMS
        spread = [jnp.zeros((SUMS, 128), f32) for _ in range(sums.shape[1])]
        for k in range(nodes):
            partial = jnp.sum(acc[k * SUMS : (k + 1) * SUMS], axis=1)
            lanes = partial[:, 0:128]
            for at in range(128, length, 128):
                lanes = lanes + partial[:, at : at + 128]
            whole = jnp.sum(lanes, axis=1, keepdims=True)
            for row in range(len(spread)):
                there = (shift_at[k] - row * per_row) * SUMS + sub
                spread[row] = spread[row] + jnp.where(lane == there, whole, 0.0)
        me = node * slabs + slab
        for row, values in enumerate(spread):
            sums[me, row : row + 1] = jnp.sum(values, axis=0, keepdims=True)
        hops = [(sum(map(bool, steps[k])), min(b, slabs - b), k, b) for k in range(nodes) for b in range(slabs)]
        scalar_copies = []
        for _, _, k, b in sorted(hops, reverse=True)[:-1]:
            at = k * slabs + b
            there = peer(k), lax.rem(slab + b, slabs)
            scalar_copies.append(
                remote(sums.at[me], sums.at[me], s_send.at[at], s_recv.at[at], there)
            )
        for copy in scalar_copies:
            copy.start()
        lax.fori_loop(0, depth, start_plane, 0)
        for copy in scalar_copies:
            copy.wait_recv()
        every = jnp.sum(sums[...], axis=0)
        total = jnp.zeros((SUMS, 128), f32)
        for owner in range(nodes):
            row = owner // per_row
            wide_row = jnp.broadcast_to(every[row : row + 1], (SUMS, 128))
            picked = jnp.where(lane == (owner - row * per_row) * SUMS + sub, wide_row, 0.0)
            total = total + jnp.where(lane == owner, jnp.sum(picked, axis=1, keepdims=True), 0.0)
        pair = lambda i: (total[i : i + 1], total[i + 1 : i + 2])
        s0, t0, t1, s1, s2, t2, s3 = (pair(i) for i in range(0, 14, 2))
        row_lane = lax.broadcasted_iota(jnp.int32, (8, 128), 1)
        known = jnp.zeros((8, 128), f32)
        for k in range(nodes):
            known = known + jnp.where(row_lane == shift_at[k], notes[k][:, 0:128], 0.0)
        shift = known[0:1], known[1:2]
        weight = known[2:3], known[3:4]
        step0 = cdiv(s0, s1)
        square = cmul(step0, step0)
        norm1 = cmul(square, s2)
        norm1 = norm1[0] - s0[0], norm1[1] - s0[1]
        ratio = cdiv(norm1, s0)
        grow = ratio[0] + 1.0, ratio[1]
        one = cmul(cmul(grow, grow), s1)
        two = cmul(cmul(grow, step0), s2)
        three = cmul(square, s3)
        step1 = cdiv(
            norm1, (one[0] - 2.0 * two[0] + three[0], one[1] - 2.0 * two[1] + three[1])
        )
        coef_r = cmul(step1, grow)
        coef_r = coef_r[0] + step0[0], coef_r[1] + step0[1]
        coef_q = cmul(step1, step0)
        coef_q = -coef_q[0], -coef_q[1]
        inner_r, inner_q = cmul(coef_r, t1), cmul(coef_q, t2)
        inner = t0[0] + inner_r[0] + inner_q[0], t0[1] + inner_r[1] + inner_q[1]
        share = cmul(weight, inner)
        following = cmul(weight, ((shift[0] - 4.0) * 0.2, shift[1] * 0.2))
        factors = jnp.zeros((SUMS, 128), f32)
        for i, entry in enumerate((*weight, *following, *share, *coef_r, *coef_q)):
            factors = jnp.where(sub == i, entry, factors)
        table_out[...] = factors
        for k in range(nodes):
            one_lane = jnp.where(lane == shift_at[k], factors, 0.0)
            values = jnp.broadcast_to(jnp.sum(one_lane, axis=1, keepdims=True), (SUMS, length))
            along_r, along_q = ((values[i : i + 1], values[i + 1 : i + 2]) for i in (6, 8))
            entries = (*factor[k][1], *cmul(factor[k][0], along_r), *cmul(factor[k][0], along_q))
            for i, entry in enumerate(entries):
                scale_out[k, i : i + 1] = entry

    for copy in [*sides, *scalar_copies]:
        copy.wait_send()
    for k in range(nodes):
        if k:
            for c in range(3):
                gather_copy(k, c).wait_send()
            halo_copy(k).wait_send()
            note_copy(k).wait_send()
        for c in range(4):
            forward(k, c).wait_send()
        for c in range(2):
            forward_halo(k, c).wait_send()
            far_copy(k, c).wait_send()
        q_copy(k, k < lower).wait_send()
        x_copy(k).wait_send()


def finish(nodes, started, rbuf, qbuf, scales, factors, moments, trace, result, pair, sems):
    depth, block, length = result.shape[2:]
    piece = 16 if block % 16 == 0 else block
    scale = []
    for k in range(nodes):
        rows = [scales[k, i : i + 1, :] for i in range(6)]
        scale.append((rows[0:2], rows[2:4], rows[4:6]))

    def copy(p):
        return pltpu.make_async_copy(result.at[:, :, p], moments.at[:, 0, :, p], sems.at[p])

    def plane(p, carry):
        def body(i, inner):
            rows = pl.ds(pl.multiple_of(i * piece, piece), piece)
            values = [started[degree, 0, part, p, rows] for degree in range(2) for part in range(2)]
            for k in range(nodes):
                r = [rbuf[k, part, p + 2, rows] for part in range(2)]
                q = [qbuf[k, part, p, rows] for part in range(2)]
                along_r, along_q = cmul(scale[k][1], r), cmul(scale[k][2], q)
                field = [along_r[part] + along_q[part] for part in range(2)]
                term = cmul(scale[k][0], field)
                for part in range(2):
                    values[part] = values[part] + field[part]
                    values[2 + part] = values[2 + part] + term[part]
            for degree in range(2):
                for part in range(2):
                    result[degree, part, p, rows] = values[2 * degree + part]
            return inner

        lax.fori_loop(0, block // piece, body, 0, unroll=True)
        copy(p).start()
        return carry

    values = factors[...]
    sub = lax.broadcasted_iota(jnp.int32, values.shape, 0)
    lane = lax.broadcasted_iota(jnp.int32, values.shape, 1)
    for part in range(2):
        pair[part] = jnp.sum(jnp.where((sub == 4 + part) & (lane < nodes), values, 0.0))
    trace_copy = pltpu.make_async_copy(pair, trace, sems.at[depth])
    trace_copy.start()
    lax.fori_loop(0, depth, plane, 0, unroll=2)
    for p in range(depth):
        copy(p).wait()
    trace_copy.wait()


def per_device(nodes, slabs, probes, potential, warm_start, shift_points, quad_weights):
    depth, width, length = potential.shape
    block = width // nodes
    tall = up_to(block, 16)
    narrow = block % 16 == 0
    pairs = depth // 2
    f32, bf16 = jnp.float32, jnp.bfloat16
    anywhere = pl.BlockSpec(memory_space=pltpu.HBM)
    vector = pl.BlockSpec(memory_space=pltpu.VMEM)
    dma = pltpu.SemaphoreType.DMA
    small = small_matrices(block, depth)
    picks = halo_picks(width, nodes)
    cpicks = picks if narrow else core_picks(width, nodes)
    results = pl.pallas_call(
        functools.partial(kernel, nodes, slabs),
        out_shape=(
            pltpu.VMEM((2, 1, 2, depth, block, length), f32),
            pltpu.VMEM((nodes, 2, depth + 4, block, length), f32),
            pltpu.VMEM((nodes, 2, depth + 2, block, length), f32),
            pltpu.VMEM((nodes, 8, length), f32),
            pltpu.VMEM((SUMS, 128), f32),
        ),
        in_specs=[anywhere] * 9,
        out_specs=(vector,) * 5,
        scratch_shapes=[
            pltpu.VMEM((2, depth, width, length), bf16),
            pltpu.VMEM((nodes, 2, pairs, 16, length), bf16),
            pltpu.VMEM((16, 128) if narrow else (nodes, 2, depth, tall, length), bf16),
            pltpu.VMEM((nodes, 2, depth + 8, tall, length), bf16),
            pltpu.VMEM((nodes, 2, pairs + 2, 16, length), bf16),
            pltpu.VMEM((depth + 4, block, length), f32),
            pltpu.VMEM((depth + 4, block, length), f32),
            pltpu.VMEM((2, depth, 8, length), f32),
            pltpu.VMEM((2, depth, 8, length), f32),
            pltpu.VMEM((4 * depth, length), f32),
            pltpu.VMEM((4 * depth, length), f32),
            pltpu.VMEM((nodes, 2, 4 * depth, length), f32),
            pltpu.VMEM((nodes, 2, 2, tall, length), bf16),
            pltpu.VMEM((nodes, 2, 2, tall, length), bf16),
            pltpu.VMEM((nodes, 2, 16, length), f32),
            pltpu.VMEM((nodes, 2, 16, length), f32),
            pltpu.VMEM((nodes, 2, 16, length), bf16),
            pltpu.VMEM((nodes, 2, 16, length), bf16),
            pltpu.VMEM((nodes, 2, 2, tall, length), bf16),
            pltpu.VMEM((nodes, 2, 2, tall, length), bf16),
            pltpu.VMEM((nodes * SUMS, 8, length), f32),
            pltpu.VMEM((nodes * slabs, up_to(nodes * SUMS, 128) // 128, 128), f32),
            pltpu.VMEM((nodes, 8, length), f32),
            pltpu.SMEM((1, 2), f32),
            pltpu.SMEM((1, 2), f32),
            pltpu.VMEM((length, length), bf16),
            pltpu.VMEM(small.shape, bf16),
            pltpu.VMEM(picks.shape, bf16),
            pltpu.VMEM((16, 128) if narrow else cpicks.shape, bf16),
            dma((14,)),
            dma((4,)),
            dma((4,)),
            dma((nodes, 5)),
            dma((nodes, 5)),
            dma((nodes, 8)),
            dma((nodes, 8)),
            dma((nodes,)),
            dma((nodes,)),
            dma((nodes,)),
            dma((nodes,)),
            dma((nodes * slabs,)),
            dma((nodes * slabs,)),
        ],
        compiler_params=pltpu.CompilerParams(
            collective_id=0, has_side_effects=True, vmem_limit_bytes=48 * 1024 * 1024
        ),
    )(
        warm_start,
        probes,
        potential,
        shift_points,
        quad_weights,
        jnp.asarray(ring_matrix(length, -90.0)),
        jnp.asarray(small),
        jnp.asarray(picks),
        jnp.asarray(cpicks),
    )
    return pl.pallas_call(
        functools.partial(finish, nodes),
        out_shape=(
            jax.ShapeDtypeStruct((2, 1, 2, depth, block, length), f32),
            jax.ShapeDtypeStruct((2,), f32),
        ),
        in_specs=[vector] * 5,
        out_specs=(anywhere, anywhere),
        scratch_shapes=[
            pltpu.VMEM((2, 2, depth, block, length), f32),
            pltpu.SMEM((2,), f32),
            dma((depth + 1,)),
        ],
        compiler_params=pltpu.CompilerParams(vmem_limit_bytes=4 * 1024 * 1024),
    )(*results)


def solution(mesh):
    return jax.shard_map(
        functools.partial(per_device, mesh.shape["node"], mesh.shape["grid"]),
        mesh=mesh,
        in_specs=(
            P(None, "grid", None, None),
            P("grid", None, None),
            P("node", None, None, "grid", None, None),
            P("node", None),
            P("node", None),
        ),
        out_specs=(P(None, None, None, "grid", "node", None), P()),
        check_vma=False,
    )
```
